32 devices in a mesh: dev: 32 (over z, y, x, core).
Axes of the slice: x: 2, y: 2, z: 4, core: 2. Of those that a mesh axis runs over, the one named last changes fastest.
Arguments:
- images: bfloat16 [160, 197, 512], P('dev'), may hold values from -6 to 6
- cotangent: bfloat16 [160, 197, 512], P('dev'), may hold values from -6 to 6
- routes: int32 [31520, 2], P('dev'), may hold values from 0 to 3, as said below
- priority: int32 [32, 985], P('dev'), may hold values from 0 to 984, each once within a row
- image_count: int32 [32], P('dev'), may hold values from 1 to 5, 112 in all
- ln1_gain: bfloat16 [512], P('dev'), may hold values from 0.5 to 1.5
- ln1_bias: bfloat16 [512], P('dev'), may hold values from -4 to 4
- w_qkv: bfloat16 [786432], P('dev'), may hold values from -0.375 to 0.375
- b_qv: bfloat16 [1024], P('dev'), may hold values from -4 to 4
- w_out: bfloat16 [262144], P('dev'), may hold values from -0.75 to 0.75
- b_out: bfloat16 [512], P('dev'), may hold values from -4 to 4
- ln2_gain: bfloat16 [512], P('dev'), may hold values from 0.5 to 1.5
- ln2_bias: bfloat16 [512], P('dev'), may hold values from -1.5 to 1.5
- w_router: bfloat16 [2048], P('dev'), may hold values from -0.1875 to 0.1875
- w_in: bfloat16 [4194304], P('dev'), may hold values from -0.25 to 0.25
- b_in: bfloat16 [8192], P('dev'), may hold values from -4 to 4
- w_back: bfloat16 [4194304], P('dev'), may hold values from -0.375 to 0.375
- b_back: bfloat16 [2048], P('dev'), may hold values from -4 to 4
Outputs:
- blocks: bfloat16 [160, 197, 512], P('dev')
- grad_images: bfloat16 [160, 197, 512], P('dev')
- grad_ln1_gain: float32 [512], P('dev')
- grad_ln1_bias: float32 [512], P('dev')
- grad_w_qkv: float32 [786432], P('dev')
- grad_b_qv: float32 [1024], P('dev')
- grad_w_out: float32 [262144], P('dev')
- grad_b_out: float32 [512], P('dev')
- grad_ln2_gain: float32 [512], P('dev')
- grad_ln2_bias: float32 [512], P('dev')
- grad_w_router: float32 [2048], P('dev')
- grad_w_in: float32 [4194304], P('dev')
- grad_b_in: float32 [8192], P('dev')
- grad_w_back: float32 [4194304], P('dev')
- grad_b_back: float32 [2048], P('dev')
The draws below stay inside these ranges and needn't reach their ends.
Inputs may be any that keep to these rules, and one draw needn't show every extreme that they name: `routes`: each token slot names two different experts, its first choice in column 0. `priority`: each row lists every token slot of a device once, index in image-major order; earlier entries claim expert slots first. `image_count`: a device's image slots from this count on hold padding, whose output and gradient rows are zero.
All inputs are finite; a program needn't handle non-finite values.
Results may differ from the reference program's by a relative error of at most 0.013.
The reference program's roundings to bfloat16 on the way count: a program that leaves them out, or rounds other values in their place, can miss the bound.
Values may be sent and summed in bfloat16 or wider, within the bound.
A program may use at most 192 MiB of HBM per device.

```python
import math
import jax
import jax.numpy as jnp
import numpy as np
from jax import lax

D = 512
HEADS = 8
HID = 2048
EXPERTS = 4
SEQ = 197
SLOTS = 5
HEAD_DIM = 64
TOK_DEV = 985
CAP = 555
IMAGES = 160
TOKENS = 31520
N_DEV = 32


def draw_routes(key, part):
    key = jax.random.fold_in(key, 11)
    keys = jax.random.split(key, 5)
    device_count = TOKENS // TOK_DEV
    favored = jax.random.randint(keys[0], (device_count,), 0, EXPERTS)
    favored_row = jnp.repeat(favored, TOK_DEV, total_repeat_length=TOKENS)
    takes = jax.random.randint(keys[1], (TOKENS,), 0, 10) < 9
    order_bit = jax.random.randint(keys[2], (TOKENS,), 0, 2)
    first_off = 1 + jax.random.randint(keys[3], (TOKENS,), 0, EXPERTS - 1)
    second_off = 1 + (first_off + jax.random.randint(keys[4], (TOKENS,), 0, EXPERTS - 2)) % (EXPERTS - 1)
    other = (favored_row + first_off) % EXPERTS
    second = (favored_row + second_off) % EXPERTS
    column_one = jnp.where(takes, jnp.where(order_bit == 0, favored_row, other), other)
    column_two = jnp.where(takes, jnp.where(order_bit == 0, other, favored_row), second)
    return jnp.stack([column_one, column_two], axis=1).astype(jnp.int32)


def block_levels(own_key, extent, cuts, low, high):
    level = 1.0
    for dim, shards_of in cuts:
        steps = jax.random.uniform(jax.random.fold_in(jax.random.fold_in(own_key, 6), dim), (shards_of,), jnp.float32, low / len(cuts), high / len(cuts))
        level = level * jnp.repeat(jnp.exp(steps), extent[dim] // shards_of).reshape((-1,) + (1,) * (len(extent) - 1 - dim))
    return level


def split_up(amount, total, reach, slope):
    weights = [(1 << 20) // math.isqrt(standing ** slope) + 1 for standing in range(2, amount + 1)]
    surplus, given = total - reach - (amount - 1), [1] * (amount - 1)
    while surplus > 0:
        free = [i for i in range(amount - 1) if given[i] < reach]
        whole, left = sum([weights[i] for i in free]), surplus
        for i in free:
            more = min(reach - given[i], max(1, left * weights[i] // whole), surplus)
            given[i] = given[i] + more
            surplus = surplus - more
    return np.array([reach] + given)


def ragged_sizes(own_key, amount, total, most, lean):
    if amount == 2:
        one = jax.random.randint(own_key, (), max(1, total - most), min(most, total - 1) + 1)
        return jnp.stack([one, total - one])
    lengths = jnp.asarray(split_up(amount, total, most, lean), jnp.int32)
    pairs = (amount - 1) // 2
    source_of, taker = lengths[1:1 + 2 * pairs:2], lengths[2:2 + 2 * pairs:2]
    margin = jnp.minimum(source_of - 1, most - taker)
    shifted = jax.random.randint(jax.random.fold_in(own_key, 1), (pairs,), 0, 1 << 20) % (margin + 1)
    lengths = lengths.at[1:1 + 2 * pairs:2].set(source_of - shifted).at[2:2 + 2 * pairs:2].set(taker + shifted)
    return lengths[jax.random.permutation(jax.random.fold_in(own_key, 2), amount)]


def noise(rng, shape, deviation, bound, cuts=(), held_as=jnp.bfloat16):
    entries = deviation * jax.random.normal(rng, shape, jnp.float32)
    if cuts:
        entries = entries * block_levels(rng, shape, cuts, -0.22, 0.18)
    return jnp.clip(entries, -bound, bound).astype(held_as)


def setup_inputs(seed: int = 0) -> dict:
    arg_keys = jax.random.split(jax.random.key(seed), 19)
    images = noise(arg_keys[0], (IMAGES, SEQ, D), 1.0, 6.0, ((0, 32),))
    cotangent = noise(arg_keys[1], (IMAGES, SEQ, D), 1.0, 6.0, ((0, 32),))
    routes = draw_routes(jax.random.fold_in(arg_keys[18], 71), 0)
    priority = jax.vmap(lambda own: jax.random.permutation(own, TOK_DEV))(jax.random.split(arg_keys[3], N_DEV)).reshape((N_DEV, TOK_DEV)).astype(jnp.int32)
    image_count = ragged_sizes(arg_keys[4], N_DEV, max(N_DEV, 7 * SLOTS * N_DEV // 10), SLOTS, 1).astype(jnp.int32)
    ln1_gain = jnp.clip(1.0 + 0.1 * jax.random.normal(arg_keys[5], (D,), jnp.float32), 0.5, 1.5).astype(jnp.bfloat16)
    ln1_bias = noise(arg_keys[6], (D,), 0.3, 4.0, ((0, 32),))
    w_qkv = noise(arg_keys[7], (3 * D * D,), (D // 2) ** -0.5, 0.375, ((0, 32),))
    b_qv = noise(arg_keys[8], (2 * D,), 0.3, 4.0, ((0, 32),))
    w_out = noise(arg_keys[9], (D * D,), (D // 8) ** -0.5, 0.75, ((0, 32),))
    b_out = noise(arg_keys[10], (D,), 0.3, 4.0, ((0, 32),))
    ln2_gain = jnp.clip(1.0 + 0.1 * jax.random.normal(arg_keys[11], (D,), jnp.float32), 0.5, 1.5).astype(jnp.bfloat16)
    ln2_bias = noise(arg_keys[12], (D,), 0.1, 1.5, ((0, 32),))
    w_router = noise(arg_keys[13], (D * EXPERTS,), (2 * D) ** -0.5, 0.1875, ((0, 32),))
    w_in = noise(arg_keys[14], (EXPERTS * D * HID,), D ** -0.5, 0.25, ((0, 32),))
    b_in = noise(arg_keys[15], (EXPERTS * HID,), 0.3, 4.0, ((0, 32),))
    w_back = noise(arg_keys[16], (EXPERTS * HID * D,), (HID // 8) ** -0.5, 0.375, ((0, 32),))
    b_back = noise(arg_keys[17], (EXPERTS * D,), 0.3, 4.0, ((0, 32),))
    return dict(images=images, cotangent=cotangent, routes=routes, priority=priority, image_count=image_count, ln1_gain=ln1_gain, ln1_bias=ln1_bias, w_qkv=w_qkv, b_qv=b_qv, w_out=w_out, b_out=b_out, ln2_gain=ln2_gain, ln2_bias=ln2_bias, w_router=w_router, w_in=w_in, b_in=b_in, w_back=w_back, b_back=b_back)


EPSILON = 1e-06
PRECISE = lax.Precision.HIGHEST

@jax.custom_vjp
def low(v):
    return lax.optimization_barrier(v.astype(jnp.bfloat16)).astype(jnp.float32)

@jax.custom_vjp
def low_back(v):
    return v

def low_keep(v):
    return (low(v), None)

def low_pass(kept, grad):
    return (grad,)

def back_keep(v):
    return (v, None)

def back_low(kept, grad):
    return (low(grad),)
low.defvjp(low_keep, low_pass)
low_back.defvjp(back_keep, back_low)

def layer_norm(inputs, scaling, offset):
    centre = inputs - lax.optimization_barrier(jnp.mean(inputs, axis=-1, keepdims=True))
    spread = lax.optimization_barrier(jnp.mean(centre * centre, axis=-1, keepdims=True))
    return centre * lax.rsqrt(spread + EPSILON) * scaling + offset

def assign_slots(route_dev, order_dev, live_tok):
    row_count = route_dev.shape[0]
    expert_ids = jnp.arange(EXPERTS, dtype=jnp.int32)
    ordered = jnp.concatenate([route_dev[order_dev, 0], route_dev[order_dev, 1]])
    owners = jnp.concatenate([order_dev, order_dev])
    alive_pair = jnp.concatenate([live_tok[order_dev], live_tok[order_dev]])
    rank_pair = jnp.concatenate([jnp.zeros((row_count,), jnp.int32), jnp.ones((row_count,), jnp.int32)])
    onehot = (ordered[:, None] == expert_ids[None, :]).astype(jnp.int32) * alive_pair[:, None]
    before = jnp.cumsum(onehot, axis=0, dtype=jnp.int32) - onehot
    position = lax.optimization_barrier(jnp.sum(before * onehot, axis=1, dtype=jnp.int32))
    kept_pair = alive_pair * (position < CAP).astype(jnp.int32)
    slot_pair = jnp.where(kept_pair > 0, ordered * CAP + position, EXPERTS * CAP).astype(jnp.int32)
    slot_tok = jnp.zeros((row_count, 2), jnp.int32).at[owners, rank_pair].set(slot_pair)
    kept_tok = jnp.zeros((row_count, 2), jnp.int32).at[owners, rank_pair].set(kept_pair)
    slot_owner = jnp.zeros((EXPERTS * CAP + 1,), jnp.int32).at[slot_pair].set(owners)[:EXPERTS * CAP]
    slot_rank = jnp.zeros((EXPERTS * CAP + 1,), jnp.int32).at[slot_pair].set(rank_pair)[:EXPERTS * CAP]
    slot_used = jnp.zeros((EXPERTS * CAP + 1,), jnp.int32).at[slot_pair].set(kept_pair)[:EXPERTS * CAP]
    return (slot_tok, kept_tok, slot_owner, slot_rank, slot_used)

def device_forward(params, image_dev, live_count, route_dev, order_dev):
    ln1_gain, ln1_bias, w_qkv, b_qv, w_out, b_out, ln2_gain, ln2_bias, w_router, w_in, b_in, w_back, b_back = params
    row_count = SLOTS * SEQ
    hidden_in = image_dev.reshape(row_count, D)
    live_tok = (jnp.arange(row_count, dtype=jnp.int32) // SEQ < live_count).astype(jnp.int32)
    normed1 = low(layer_norm(hidden_in, ln1_gain, ln1_bias))
    projected = jnp.dot(normed1, w_qkv.reshape(D, 3 * D), precision=PRECISE)
    queries = low(low_back(projected[:, :D] + b_qv[:D])).reshape(SLOTS, SEQ, HEADS, HEAD_DIM)
    keys_all = low(low_back(projected[:, D:2 * D])).reshape(SLOTS, SEQ, HEADS, HEAD_DIM)
    values_all = low(low_back(projected[:, 2 * D:] + b_qv[D:])).reshape(SLOTS, SEQ, HEADS, HEAD_DIM)
    scores = low_back(jnp.einsum('bqhd,bkhd->bhqk', queries, keys_all, precision=PRECISE) * HEAD_DIM ** (-0.5))
    weights_att = low(jax.nn.softmax(scores, axis=-1))
    attn_mix = low(low_back(jnp.einsum('bhqk,bkhd->bqhd', weights_att, values_all, precision=PRECISE).reshape(row_count, D)))
    attended = low_back(jnp.dot(attn_mix, w_out.reshape(D, D), precision=PRECISE) + b_out)
    residual = hidden_in + attended
    normed2 = low(layer_norm(residual, ln2_gain, ln2_bias))
    logits = low_back(jnp.dot(normed2, w_router.reshape(D, EXPERTS), precision=PRECISE))
    gate_probs = jax.nn.softmax(logits, axis=-1)
    slot_tok, kept_tok, slot_owner, slot_rank, slot_used = assign_slots(route_dev, order_dev, live_tok)
    dispatched = (normed2[slot_owner] * slot_used[:, None].astype(jnp.float32)).reshape(EXPERTS, CAP, D)
    inner_pre = low_back(jnp.einsum('ecd,edf->ecf', dispatched, w_in.reshape(EXPERTS, D, HID), precision=PRECISE) + b_in.reshape(EXPERTS, 1, HID))
    active = low(jax.nn.gelu(inner_pre, approximate=False))
    expert_out = low_back(jnp.einsum('ecf,efd->ecd', active, w_back.reshape(EXPERTS, HID, D), precision=PRECISE) + b_back.reshape(EXPERTS, 1, D))
    padded_out = jnp.concatenate([expert_out.reshape(EXPERTS * CAP, D), jnp.zeros((1, D), jnp.float32)])
    pair_weight = jnp.take_along_axis(gate_probs, route_dev, axis=1) * kept_tok.astype(jnp.float32)
    mixture = pair_weight[:, 0:1] * padded_out[slot_tok[:, 0]] + pair_weight[:, 1:2] * padded_out[slot_tok[:, 1]]
    return ((residual + mixture) * live_tok[:, None].astype(jnp.float32)).reshape(SLOTS, SEQ, D)

def reference(images, cotangent, routes, priority, image_count, ln1_gain, ln1_bias, w_qkv, b_qv, w_out, b_out, ln2_gain, ln2_bias, w_router, w_in, b_in, w_back, b_back):
    params = tuple((weight.astype(jnp.float32) for weight in (ln1_gain, ln1_bias, w_qkv, b_qv, w_out, b_out, ln2_gain, ln2_bias, w_router, w_in, b_in, w_back, b_back)))
    image_all = images.astype(jnp.float32).reshape(N_DEV, SLOTS, SEQ, D)
    route_all = routes.reshape(N_DEV, SLOTS * SEQ, 2)

    def whole_layer(image_in, weight_set):

        def per_device(device_item):
            return device_forward(weight_set, device_item[0], device_item[1], device_item[2], device_item[3])
        return lax.map(jax.checkpoint(per_device), (image_in, image_count, route_all, priority))
    result, pullback = jax.vjp(whole_layer, image_all, params)
    grad_image, grad_set = pullback(cotangent.astype(jnp.float32).reshape(N_DEV, SLOTS, SEQ, D))
    return (result.reshape(IMAGES, SEQ, D).astype(jnp.bfloat16), grad_image.reshape(IMAGES, SEQ, D).astype(jnp.bfloat16), grad_set[0], grad_set[1], grad_set[2], grad_set[3], grad_set[4], grad_set[5], grad_set[6], grad_set[7], grad_set[8], grad_set[9], grad_set[10], grad_set[11], grad_set[12])
```

```python
import functools

import jax
import jax.numpy as jnp
from jax import lax
from jax.experimental import pallas as pl
from jax.experimental.pallas import tpu as pltpu
from jax.sharding import PartitionSpec as P

D = 512
HEADS = 8
HID = 2048
EXPERTS = 4
SEQ = 197
SLOTS = 5
HEAD_DIM = 64
CAP = 555
EPSILON = 1e-06

ROWS = -(-SEQ // 16) * 16
TOK = SLOTS * ROWS
CAPP = -(-CAP // 16) * 16
LANES = 128
WIDE = 2 * D + LANES
GROUP = EXPERTS * 2 * 2 * 2
BLOCK_IN = EXPERTS * D // GROUP
BLOCK_BACK = EXPERTS * HID // GROUP
SLOT_TILE = CAPP // 5
FT = 256
VMEM_LIMIT = 63 * 1024 * 1024
F32 = jnp.float32
BF16 = jnp.bfloat16


def mm(a, b):
    return lax.dot_general(a, b, (((1,), (0,)), ((), ())), preferred_element_type=F32)


def mm_nt(a, b):
    return lax.dot_general(a, b, (((1,), (1,)), ((), ())), preferred_element_type=F32)


def mm_tn(a, b):
    return lax.dot_general(a, b, (((0,), (0,)), ((), ())), preferred_element_type=F32)


def iota(shape, dim):
    return lax.broadcasted_iota(jnp.int32, shape, dim)


def normalize(inputs):
    centre = inputs - jnp.mean(inputs, axis=-1, keepdims=True)
    inverse = lax.rsqrt(jnp.mean(centre * centre, axis=-1, keepdims=True) + EPSILON)
    return centre * inverse, inverse


def norm_back(grad_normed, scaled, inverse, gain):
    grad_scaled = grad_normed * gain
    return inverse * (
        grad_scaled
        - jnp.mean(grad_scaled, axis=-1, keepdims=True)
        - scaled * jnp.mean(grad_scaled * scaled, axis=-1, keepdims=True)
    )


def gelu_parts(pre):
    size = jnp.abs(pre)
    t = 1.0 / (1.0 + (0.3275911 * 0.7071067811865476) * size)
    bell = jnp.exp(-0.5 * (pre * pre))
    poly = t * (
        0.127414796
        + t * (-0.142248368 + t * (0.7107068705 + t * (-0.7265760135 + t * 0.5307027145)))
    )
    tail = poly * bell
    phi = jnp.where(pre >= 0, 1.0 - tail, tail)
    return pre * phi, phi + pre * (bell * 0.3989422804014327)


def split3(value):
    high = value.astype(BF16).astype(F32)
    rest = value - high
    mid = rest.astype(BF16).astype(F32)
    return high, mid, rest - mid


def image_rows(i):
    return pl.ds(i * ROWS if isinstance(i, int) else pl.multiple_of(i * ROWS, 16), ROWS)


def attention_forward(i, r):
    rows = image_rows(i)
    r.xs[0:SEQ, :] = r.image_at[i % 2].astype(F32)
    hidden = r.xs[...]
    scaled, _ = normalize(hidden)
    normed = (scaled * r.vec[0:1, :] + r.vec[1:2, :]).astype(BF16)
    projected = mm(normed, r.wqkv[...].reshape(D, 3 * D))
    r.qkv[rows, 0:D] = (projected[:, :D] + r.vec[2:3, :]).astype(BF16)
    r.qkv[rows, D : 2 * D] = projected[:, D : 2 * D].astype(BF16)
    r.qkv[rows, 2 * D :] = (projected[:, 2 * D :] + r.vec[3:4, :]).astype(BF16)
    lane = iota((ROWS, LANES), 1)
    column = iota((ROWS, ROWS), 1)
    for pair in range(HEADS // 2):
        at = pair * LANES
        queries = r.qkv[rows, at : at + LANES]
        keys = r.qkv[rows, D + at : D + at + LANES]
        values = r.qkv[rows, 2 * D + at : 2 * D + at + LANES]
        mixes = []
        for half in range(2):
            mine = (lane >= half * HEAD_DIM) & (lane < (half + 1) * HEAD_DIM)
            own = jnp.where(mine, queries, jnp.zeros_like(queries))
            scores = mm_nt(own, keys) * HEAD_DIM**-0.5
            scores = jnp.where(column < SEQ, scores, -1e30)
            expo = jnp.exp(scores - jnp.max(scores, axis=-1, keepdims=True))
            probs = (expo / jnp.sum(expo, axis=-1, keepdims=True)).astype(BF16)
            r.probs[i * HEADS + 2 * pair + half] = probs
            mixes.append(mm(probs, values))
        r.mix[rows, at : at + LANES] = jnp.where(lane < HEAD_DIM, mixes[0], mixes[1]).astype(BF16)
    residual = hidden + mm(r.mix[rows, :], r.wout[...].reshape(D, D)) + r.vec[4:5, :]
    r.residual[rows, :] = residual
    scaled2, _ = normalize(residual)
    normed2 = (scaled2 * r.vec[5:6, :] + r.vec[6:7, :]).astype(BF16)
    r.wide[rows, 0:D] = normed2
    logits = jnp.where(lane < EXPERTS, mm_nt(normed2, r.router[...]), -1e30)
    expo = jnp.exp(logits - jnp.max(logits, axis=-1, keepdims=True))
    gates = expo / jnp.sum(expo, axis=-1, keepdims=True)
    r.gates[rows, :] = gates
    high, mid, low = split3(gates)
    packed = high + pltpu.roll(mid, EXPERTS, 1) + pltpu.roll(low, 2 * EXPERTS, 1)
    r.wide[rows, 2 * D :] = packed.astype(BF16)
    live = jnp.where(i < r.count[0], 1.0, 0.0)
    r.xs[0:SEQ, :] = r.other_at[i % 2].astype(F32) * live
    r.wide[rows, D : 2 * D] = r.xs[...].astype(BF16)


def routing(r):
    limit = r.count[0] * ROWS
    places = r.prow.shape[1]
    lane = iota((ROWS, LANES), 1)

    def find(i, carry):
        rows = image_rows(i)
        place_row, wanted = carry
        seen = r.prow[...] == iota((ROWS, places), 0) + i * ROWS
        place = jnp.sum(
            jnp.where(seen, iota((ROWS, places), 1).astype(F32), 0.0), axis=1, keepdims=True
        )
        r.gates[rows, :] = jnp.broadcast_to(place, (ROWS, LANES))
        same = iota((ROWS, TOK), 0) + i * ROWS == iota((ROWS, TOK), 1)
        place_row = place_row + jnp.sum(jnp.where(same, place, 0.0), axis=0, keepdims=True)
        live = iota((ROWS, LANES), 0) + i * ROWS < limit
        hit0 = jnp.where((r.rcol[rows, 0:1] == lane) & live, 1.0, 0.0)
        hit1 = jnp.where((r.rcol[rows, 1:2] == lane) & live, 1.0, 0.0)
        r.wide[rows, 0:LANES] = hit0.astype(BF16)
        r.wide[rows, LANES : 2 * LANES] = hit1.astype(BF16)
        return place_row, wanted + jnp.sum(hit0, axis=0, keepdims=True)

    place_row, wanted = lax.fori_loop(
        0, SLOTS, find, (jnp.zeros((1, TOK), F32), jnp.zeros((1, LANES), F32))
    )
    r.total[0:LANES, 0:TOK] = jnp.zeros((LANES, TOK), F32)

    def count(i, carry):
        rows = image_rows(i)
        earlier = jnp.where(place_row < r.gates[rows, 0:1], 1.0, 0.0).astype(BF16)
        before = mm(earlier, r.wide[:, 0 : 2 * LANES])
        hit0, hit1 = r.wide[rows, 0:LANES] > 0, r.wide[rows, LANES : 2 * LANES] > 0
        position = jnp.where(
            hit0, before[:, 0:LANES], jnp.where(hit1, before[:, LANES:] + wanted, 1e6)
        )
        position = jnp.where(position < CAP, position, -1.0)
        r.pos_col[rows, :] = position
        same = iota((ROWS, TOK), 0) + i * ROWS == iota((ROWS, TOK), 1)
        same = jnp.where(same, 1.0, 0.0).astype(BF16)
        high = position.astype(BF16)
        low = (position - high.astype(F32)).astype(BF16)
        r.total[0:LANES, 0:TOK] += mm_tn(high, same) + mm_tn(low, same)
        return carry

    lax.fori_loop(0, SLOTS, count, 0)
    r.pos_row[...] = r.total[0:8, 0:TOK]
    r.total[0:LANES, 0:TOK] = jnp.zeros((LANES, TOK), F32)


def dispatch(e, r):
    wanted = r.pos_row[pl.ds(e, 1), :]
    lane = iota((SLOT_TILE, LANES), 1)

    def tile(m, carry):
        rows = pl.ds(pl.multiple_of(m * SLOT_TILE, 16), SLOT_TILE)
        slot = (iota((SLOT_TILE, TOK), 0) + m * SLOT_TILE).astype(F32)
        chosen = jnp.where(slot == wanted, 1.0, 0.0).astype(BF16)
        got = mm(chosen, r.wide[...])
        r.disp[rows, :] = got[:, 0:D].astype(BF16)
        r.up[rows, :] = got[:, D : 2 * D].astype(BF16)
        mine = (lane == e) | (lane == e + EXPERTS) | (lane == e + 2 * EXPERTS)
        gate = jnp.sum(jnp.where(mine, got[:, 2 * D :], 0.0), axis=1, keepdims=True)
        r.gate_slot[rows, :] = jnp.broadcast_to(gate, (SLOT_TILE, LANES))
        r.gexp[rows, :] = (gate * got[:, D : 2 * D]).astype(BF16)
        return carry

    lax.fori_loop(0, CAPP // SLOT_TILE, tile, 0)
    r.eo[...] = jnp.zeros_like(r.eo)
    r.gdisp[...] = jnp.zeros_like(r.gdisp)


def expert_step(e, f, k, r):
    cols = pl.ds(pl.multiple_of(f * FT, FT), FT)
    block = (k, f // 4, f // 2 % 2, f % 2)
    w_in = r.win[k, :, :, :, :, cols].reshape(D, FT)
    w_back = r.wback[block]
    disp = r.disp[...]
    gexp = r.gexp[...]
    bias = r.vec[pl.ds(16 + 4 * e + f // 2, 1), pl.ds(pl.multiple_of(f % 2 * FT, FT), FT)]
    pre = mm(disp, w_in) + bias
    grad_active = mm_nt(gexp, w_back)
    active, slope = gelu_parts(pre)
    active = active.astype(BF16)
    grad_inner = (grad_active * slope).astype(BF16)
    r.eo[...] += mm(active, w_back)
    r.gdisp[...] += mm_nt(grad_inner, w_in)
    r.wback[block] = mm_tn(active, gexp).astype(BF16)
    grad_in = mm_tn(disp, grad_inner).astype(BF16)
    r.win[k, :, :, :, :, cols] = grad_in.reshape(2, 2, 2, BLOCK_IN, FT)
    r.gvec[pl.ds(16 + 4 * e + f // 2, 1), pl.ds(pl.multiple_of(f % 2 * FT, FT), FT)] = jnp.sum(
        grad_inner.astype(F32), axis=0, keepdims=True
    )


def combine(e, r):
    r.gvec[pl.ds(12 + e, 1), :] = jnp.sum(r.gexp[...].astype(F32), axis=0, keepdims=True)
    out = r.eo[...] + r.vec[pl.ds(12 + e, 1), :]
    gate = r.gate_slot[:, 0:1]
    r.disp[...] = (gate * out).astype(BF16)
    r.gexp[...] = r.gdisp[...].astype(BF16)
    high, mid, low = split3(jnp.sum(r.up[...].astype(F32) * out, axis=1, keepdims=True))
    lane = iota((CAPP, LANES), 1)
    parts = jnp.where(
        lane == e,
        high,
        jnp.where(lane == e + EXPERTS, mid, jnp.where(lane == e + 2 * EXPERTS, low, 0.0)),
    )
    r.pairs[...] = parts.astype(BF16)

    def image(i, carry):
        rows = image_rows(i)
        mine = iota((ROWS, LANES), 1) == e
        wanted = jnp.sum(jnp.where(mine, r.pos_col[rows, :], 0.0), axis=1, keepdims=True)
        chosen = jnp.where(wanted == iota((ROWS, CAPP), 1).astype(F32), 1.0, 0.0).astype(BF16)
        r.total[rows, 0:D] += mm(chosen, r.disp[...])
        r.total[rows, D : 2 * D] += mm(chosen, r.gexp[...])
        r.total[rows, 2 * D :] += mm(chosen, r.pairs[...])
        return carry

    lax.fori_loop(0, SLOTS, image, 0)


def attention_backward(i, r):
    rows = image_rows(i)
    lane = iota((ROWS, LANES), 1)
    live = jnp.where(i < r.count[0], 1.0, 0.0)
    residual = r.residual[rows, :]
    r.other_at[i % 2] = ((residual + r.total[rows, 0:D]) * live)[0:SEQ, :].astype(BF16)
    pairs = r.total[rows, 2 * D :]
    gates = r.gates[rows, :]
    grad_gates = (
        pairs + pltpu.roll(pairs, LANES - EXPERTS, 1) + pltpu.roll(pairs, LANES - 2 * EXPERTS, 1)
    )
    grad_gates = jnp.where(lane < EXPERTS, grad_gates, 0.0)
    grad_logits = (
        gates * (grad_gates - jnp.sum(grad_gates * gates, axis=-1, keepdims=True))
    ).astype(BF16)
    r.gvec[8:12, :] += mm_tn(grad_logits, r.wide[rows, 0:D])[0:EXPERTS, :]
    grad_normed2 = r.total[rows, D : 2 * D] + mm(grad_logits, r.router[...])
    scaled2, inverse2 = normalize(residual)
    r.gvec[5:6, :] += jnp.sum(grad_normed2 * scaled2, axis=0, keepdims=True)
    r.gvec[6:7, :] += jnp.sum(grad_normed2, axis=0, keepdims=True)
    grad_residual = r.wide[rows, D : 2 * D].astype(F32) + norm_back(
        grad_normed2, scaled2, inverse2, r.vec[5:6, :]
    )
    grad_attended = grad_residual.astype(BF16)
    r.wide[rows, D : 2 * D] = grad_attended
    r.gvec[4:5, :] += jnp.sum(grad_attended.astype(F32), axis=0, keepdims=True)
    grad_mix = mm_nt(grad_attended, r.wout[...].reshape(D, D)).astype(BF16)
    for pair in range(HEADS // 2):
        at = pair * LANES
        queries = r.qkv[rows, at : at + LANES]
        keys = r.qkv[rows, D + at : D + at + LANES]
        values = r.qkv[rows, 2 * D + at : 2 * D + at + LANES]
        from_mix = grad_mix[:, at : at + LANES]
        grad_q, grad_k, grad_v = [], 0.0, 0.0
        for half in range(2):
            mine = (lane >= half * HEAD_DIM) & (lane < (half + 1) * HEAD_DIM)
            own_q = jnp.where(mine, queries, jnp.zeros_like(queries))
            own_g = jnp.where(mine, from_mix, jnp.zeros_like(from_mix))
            probs_low = r.probs[i * HEADS + 2 * pair + half]
            probs = probs_low.astype(F32)
            grad_probs = mm_nt(own_g, values)
            weighted = grad_probs * probs
            grad_scores = (
                weighted - probs * jnp.sum(weighted, axis=-1, keepdims=True)
            ).astype(BF16)
            grad_v = grad_v + mm_tn(probs_low, own_g)
            grad_k = grad_k + mm_tn(grad_scores, own_q)
            grad_q.append(mm(grad_scores, keys))
        scale = HEAD_DIM**-0.5
        joined = jnp.where(lane < HEAD_DIM, grad_q[0], grad_q[1])
        r.qkv[rows, at : at + LANES] = (joined * scale).astype(BF16)
        r.qkv[rows, D + at : D + at + LANES] = (grad_k * scale).astype(BF16)
        r.qkv[rows, 2 * D + at : 2 * D + at + LANES] = grad_v.astype(BF16)
    grads = r.qkv[rows, :]
    r.gvec[2:3, :] += jnp.sum(grads[:, 0:D].astype(F32), axis=0, keepdims=True)
    r.gvec[3:4, :] += jnp.sum(grads[:, 2 * D :].astype(F32), axis=0, keepdims=True)
    grad_normed1 = mm_nt(grads, r.wqkv[...].reshape(D, 3 * D))
    r.xs[0:SEQ, :] = r.image_at[i % 2].astype(F32)
    scaled1, inverse1 = normalize(r.xs[...])
    r.wide[rows, 0:D] = (scaled1 * r.vec[0:1, :] + r.vec[1:2, :]).astype(BF16)
    r.gvec[0:1, :] += jnp.sum(grad_normed1 * scaled1, axis=0, keepdims=True)
    r.gvec[1:2, :] += jnp.sum(grad_normed1, axis=0, keepdims=True)
    grad_in = grad_residual + norm_back(grad_normed1, scaled1, inverse1, r.vec[0:1, :])
    r.grad_at[i % 2] = grad_in[0:SEQ, :].astype(BF16)


def weight_grads(r):
    def columns(c, carry):
        cols = pl.ds(pl.multiple_of(c * FT, FT), FT)
        grad = mm_tn(r.wide[:, 0:D], r.qkv[:, cols]).astype(BF16)
        r.wqkv[:, :, :, :, :, cols] = grad.reshape(r.wqkv.shape[:5] + (FT,))
        return carry

    lax.fori_loop(0, 3 * D // FT, columns, 0)
    r.wout[...] = mm_tn(r.mix[...], r.wide[:, D : 2 * D]).astype(BF16).reshape(r.wout.shape)


def spread_router(r):
    r.router[...] = jnp.zeros_like(r.router)
    first = r.vec[8:16, :]
    r.router[0:16, :] = jnp.concatenate(
        [jnp.where(iota((8, D), 0) < EXPERTS, first, 0.0), jnp.zeros((8, D), F32)], axis=0
    ).astype(BF16)


def own_vectors(me, r):
    pack = r.pack[...]
    lane, line = iota((8, LANES), 1), iota((8, LANES), 0)
    j, c = iota((LANES, D), 0), iota((LANES, D), 1)
    column, row = iota((8, D), 1), iota((8, D), 0)
    zero = jnp.zeros((8, LANES), F32)

    def spread(values, match):
        return mm(values.astype(BF16), jnp.where(match, 1.0, 0.0).astype(BF16))

    def rows(k):
        return jnp.broadcast_to(pack[k : k + 1, :], (8, LANES))

    start = jnp.where(line < 2, 16 * line, 16 * line)
    sixteen = jnp.where((lane >= start) & (lane < start + 16) & (line != 2) & (line != 3), rows(0), zero)
    both = jnp.where((lane >= 32) & (lane < 64) & ((line == 2) | (line == 3)), rows(0), zero)
    top = spread(sixteen, (j & 15) == (c & 15)) + spread(both, (j & 31) == (c & 31))
    owner = jnp.where(
        row == 2, column >> 5, jnp.where(row == 3, 16 + (column >> 5), column >> 4)
    )
    r.vec[0:8, :] = jnp.where(owner == me, top, 0.0)
    router = jnp.where((lane < 64) & ((lane & 3) == line), rows(1), zero)
    back = jnp.where((lane >= 64) & (line >= 4), rows(1), zero)
    low = spread(router, (j >> 2) == (c & 15)) + spread(back, (j & 63) == (c & 63))
    owner = jnp.where(row < 4, column >> 4, 8 * (row - 4) + (column >> 6))
    r.vec[8:16, :] = jnp.where(owner == me, low, 0.0)
    bias = jnp.concatenate([pack[2:3, :], pack[3:4, :]] * 2, axis=1)
    row, column = iota((16, D), 0), iota((16, D), 1)
    r.vec[16:32, :] = jnp.where(2 * row + (column >> 8) == me, bias, 0.0)


MESH = pl.DeviceIdType.MESH
FULL = slice(None)


class Place:
    def __init__(self):
        me = lax.axis_index("dev")
        self.me, self.c, self.x, self.y, self.z = me, me % 2, me // 2 % 2, me // 4 % 2, me // 8
        self.core = self.device(self.z, self.y, self.x, 1 - self.c)
        self.over_y = self.device(self.z, 1 - self.y, self.x, self.c)
        self.over_x = self.device(self.z, self.y, 1 - self.x, self.c)

    def device(self, z, y, x, c):
        return ((z * 2 + y) * 2 + x) * 2 + c

    def plane(self, k):
        return lax.rem(self.z + k + EXPERTS, EXPERTS)

    def above(self, k):
        return self.device(self.plane(k), self.y, self.x, self.c)

    def greet(self):
        barrier = pltpu.get_barrier_semaphore()
        friends = [self.above(k) for k in range(1, EXPERTS)]
        friends += [self.core, self.over_y, self.over_x]
        for friend in friends:
            pl.semaphore_signal(barrier, inc=1, device_id=(friend,), device_id_type=MESH)
        pl.semaphore_wait(barrier, len(friends))

    def first(self, route):
        return self.over_y if route == 0 else self.over_x

    def second(self, route):
        return self.over_x if route == 0 else self.over_y


class Copies:
    def __init__(self, sems, index):
        self.sems, self.index = sems, index

    def make(self, slot, source, target, device):
        send_sem, recv_sem = self.sems
        return pltpu.make_async_remote_copy(
            src_ref=source, dst_ref=target, send_sem=send_sem.at[self.index, slot],
            recv_sem=recv_sem.at[self.index, slot], device_id=(device,), device_id_type=MESH,
        )


class SumAll(Copies):
    def __init__(self, sems, index, values, landing, place):
        super().__init__(sems, index)
        self.values, self.landing, self.p = values, landing, place

    def stage(self, step):
        p = self.p
        targets = [
            [(k, p.above(k)) for k in range(1, EXPERTS)], [(4, p.over_y)], [(5, p.over_x)],
            [(6, p.core)],
        ][step]
        return [self.make(s, self.values, self.landing.at[s - 1], d) for s, d in targets]

    def begin(self, step):
        for copy in self.stage(step):
            copy.start()

    def end(self, step):
        for copy in self.stage(step):
            copy.wait()
        if step == 0:
            self.values[...] += self.landing[0] + self.landing[1] + self.landing[2]
        else:
            self.values[...] += self.landing[2 + step]


class Gather(Copies):
    def __init__(self, sems, index, shard, full, tail, route, k, place):
        super().__init__(sems, index)
        self.shard, self.full, self.tail, self.route, self.p = shard, full, tail, route, place
        self.k = k

    def at(self, lead, y, x, c):
        return self.full.at[(lead, y, x, c) + self.tail]

    def own(self):
        return self.shard.at[self.tail]

    def local(self, sem):
        p = self.p
        lead = p.z if self.k is None else 0
        return pltpu.make_async_copy(self.own(), self.at(lead, p.y, p.x, p.c), sem)

    def along_z(self, arriving):
        p = self.p
        if self.k is None:
            return [
                self.make(k, self.own(), self.at(p.plane(-k) if arriving else p.z, p.y, p.x, p.c),
                          p.above(k))
                for k in range(1, EXPERTS)
            ]
        if self.k == 0:
            return []
        return [self.make(1, self.own(), self.at(self.k, p.y, p.x, p.c), p.above(-self.k))]

    def lead(self):
        return FULL if self.k is None else self.k

    def across(self, step, arriving):
        p = self.p
        y, x = p.y, p.x
        if step == 0:
            if arriving:
                y, x = (1 - y, x) if self.route == 0 else (y, 1 - x)
            device = p.first(self.route)
        else:
            if arriving:
                y, x = 1 - y, 1 - x
            y, x = (FULL, x) if self.route == 0 else (y, FULL)
            device = p.second(self.route)
        block = self.at(self.lead(), y, x, p.c)
        return self.make(4 + step, block, block, device)

    def to_core(self, step, arriving):
        p = self.p
        y, x = p.y, p.x
        if step == 1:
            y, x = (1 - y, x) if self.route == 0 else (y, 1 - x)
        elif step == 2:
            y, x = (FULL, 1 - x) if self.route == 0 else (1 - y, FULL)
        block = self.at(self.lead(), y, x, 1 - p.c if arriving else p.c)
        return self.make(6 + step, block, block, p.core)

    def start_z(self):
        for copy in self.along_z(False):
            copy.start()

    def stage(self, step):
        if step == 0:
            for copy in self.along_z(True):
                copy.wait_recv()
        else:
            self.across(step - 1, True).wait_recv()
        if step < 2:
            self.across(step, False).start()
        self.to_core(step, False).start()

    def finish(self):
        for step in range(3):
            self.to_core(step, True).wait_recv()
        for copy in self.along_z(False):
            copy.wait_send()
        for step in range(2):
            self.across(step, False).wait_send()
        for step in range(3):
            self.to_core(step, False).wait_send()


class Scatter(Copies):
    def __init__(self, sems, index, full, landing, out, tail, route, k, place):
        super().__init__(sems, index)
        self.full, self.out, self.tail, self.route, self.p, self.k = (
            full, out, tail, route, place, k,
        )
        self.from_core, self.from_first, self.from_second, self.from_z = landing

    def lead(self):
        return FULL if self.k is None else self.k

    def landed(self, ref, spare):
        if self.k is None:
            return (FULL,) * (1 + spare) + self.tail
        return (self.k % ref.shape[0],) + (FULL,) * spare + self.tail

    def to_core(self):
        p = self.p
        return self.make(0, self.full.at[(self.lead(), FULL, FULL, 1 - p.c) + self.tail],
                         self.from_core.at[self.landed(self.from_core, 2)], p.core)

    def to_first(self):
        p = self.p
        y, x = (FULL, 1 - p.x) if self.route == 0 else (1 - p.y, FULL)
        return self.make(1, self.full.at[(self.lead(), y, x, p.c) + self.tail],
                         self.from_first.at[self.landed(self.from_first, 1)],
                         p.second(self.route))

    def to_second(self):
        p = self.p
        y, x = (1 - p.y, p.x) if self.route == 0 else (p.y, 1 - p.x)
        return self.make(2, self.full.at[(self.lead(), y, x, p.c) + self.tail],
                         self.from_second.at[self.landed(self.from_second, 0)],
                         p.first(self.route))

    def along_z(self):
        p = self.p
        steps = range(1, EXPERTS) if self.k is None else ([self.k] if self.k else [])
        return [
            self.make(2 + k, self.full.at[(p.plane(k) if self.k is None else k, p.y, p.x, p.c) + self.tail],
                      self.from_z.at[(k - 1,) + self.tail], p.above(k))
            for k in steps
        ]

    def add(self, mine, landed):
        def layer(k, carry):
            for at, source in zip(mine(k), landed(k)):
                self.full[at + self.tail] = self.full[at + self.tail] + source
            return carry

        if self.k is None:
            lax.fori_loop(0, EXPERTS, layer, 0)
        else:
            layer(self.k, 0)

    def slot(self, ref, k):
        return k if self.k is None else k % ref.shape[0]

    def stage(self, step):
        p, tail = self.p, self.tail
        if step == 0:
            self.to_core().start()
        elif step == 1:
            self.to_core().wait_recv()
            spots = [(y, x) for y in range(2) for x in range(2)]
            ref = self.from_core
            self.add(lambda k: [(k, y, x, p.c) for y, x in spots],
                     lambda k: [ref[(self.slot(ref, k), y, x) + tail] for y, x in spots])
            self.to_first().start()
        elif step == 2:
            self.to_first().wait_recv()
            ref = self.from_first
            self.add(lambda k: [(k, o, p.x, p.c) if self.route == 0 else (k, p.y, o, p.c) for o in range(2)],
                     lambda k: [ref[(self.slot(ref, k), o) + tail] for o in range(2)])
            self.to_second().start()
        else:
            self.to_second().wait_recv()
            ref = self.from_second
            self.add(lambda k: [(k, p.y, p.x, p.c)],
                     lambda k: [ref[(self.slot(ref, k),) + tail]])
            for copy in self.along_z():
                copy.start()

    def collect(self):
        p, tail = self.p, self.tail
        total = self.full[((p.z if self.k is None else 0), p.y, p.x, p.c) + tail].astype(F32)
        for k in range(EXPERTS - 1):
            total = total + self.from_z[(k,) + tail].astype(F32)
        self.out[tail] = total

    def drain(self):
        self.to_core().wait_send()
        self.to_first().wait_send()
        self.to_second().wait_send()
        for copy in self.along_z():
            copy.wait_send()


class Refs:
    def __init__(self, names, refs):
        for name, ref in zip(names, refs, strict=True):
            setattr(self, name, ref)


SCRATCH = dict(
    image_at=((2, SEQ, D), BF16),
    other_at=((2, SEQ, D), BF16),
    grad_at=((2, SEQ, D), BF16),
    xs=((ROWS, D), F32),
    router=((LANES, D), BF16),
    qkv=((TOK, 3 * D), BF16),
    probs=((SLOTS * HEADS, ROWS, ROWS), BF16),
    mix=((TOK, D), BF16),
    residual=((TOK, D), F32),
    wide=((TOK, WIDE), BF16),
    gates=((TOK, LANES), F32),
    pos_col=((TOK, LANES), F32),
    pos_row=((8, TOK), F32),
    disp=((CAPP, D), BF16),
    up=((CAPP, D), BF16),
    gexp=((CAPP, D), BF16),
    gate_slot=((CAPP, LANES), F32),
    pairs=((CAPP, LANES), BF16),
    eo=((CAPP, D), F32),
    gdisp=((CAPP, D), F32),
    total=((TOK, WIDE), F32),
    wqkv=((EXPERTS, 2, 2, 2, 16, 3 * D), BF16),
    wout=((EXPERTS, 2, 2, 2, 16, D), BF16),
    win=((EXPERTS, 2, 2, 2, BLOCK_IN, HID), BF16),
    wback=((EXPERTS, 2, 2, 2, BLOCK_BACK, D), BF16),
)
SHARDS = dict(wqkv=(16, 3 * D), wout=(16, D), win=(BLOCK_IN, HID), wback=(BLOCK_BACK, D))


def columns_of(width, h):
    return (FULL, slice(h * width // 2, (h + 1) * width // 2))


def rows_of(height, h):
    return (slice(h * height // 2, (h + 1) * height // 2), FULL)


FLAT_PIECES = [("wqkv", columns_of(3 * D, h), h) for h in range(2)]
FLAT_PIECES += [("wout", columns_of(D, h), h) for h in range(2)]
EXPERT_PIECES = [("win", rows_of(BLOCK_IN, h), h) for h in range(2)]
EXPERT_PIECES += [("wback", rows_of(BLOCK_BACK, h), h) for h in range(2)]
LANDING = {}
for name in ("wqkv", "wout"):
    for part, lead in dict(core=(4, 2, 2), first=(4, 2), second=(4,), z=(3,)).items():
        LANDING[name, part] = (lead + SHARDS[name], BF16)
for name in ("win", "wback"):
    for part, lead in dict(core=(2, 2, 2), first=(4, 2), second=(4,), z=(3,)).items():
        LANDING[name, part] = (lead + SHARDS[name], BF16)
INPUTS = ["count", "images", "cotangent", "rcol", "prow"]


def whole_kernel(*refs):
    names = INPUTS + ["pack"] + ["shard_" + n for n in SHARDS]
    names += ["blocks", "gimages", "gvec"] + ["out_" + n for n in SHARDS]
    names += list(SCRATCH) + ["vec", "land_vec", "land_gvec"]
    names += ["land_" + "_".join(key) for key in LANDING]
    names += ["local_sem", "vec_send", "vec_recv", "get_send", "get_recv", "put_send", "put_recv"]
    names += ["free_sem", "in_sem", "out_sem"]
    r = Refs(names, refs)
    p = Place()
    p.greet()

    def landing(name):
        return [getattr(r, f"land_{name}_{part}") for part in ("core", "first", "second", "z")]

    get_sems, put_sems = (r.get_send, r.get_recv), (r.put_send, r.put_recv)
    flat_get, flat_put = [], []
    for index, (name, tail, route) in enumerate(FLAT_PIECES):
        flat_get.append(
            Gather(get_sems, index, getattr(r, "shard_" + name), getattr(r, name), tail, route, None, p)
        )
        flat_put.append(
            Scatter(put_sems, index, getattr(r, name), landing(name), getattr(r, "out_" + name),
                    tail, route, None, p)
        )
    get, put = [], []
    for k in range(EXPERTS):
        get.append([])
        put.append([])
        for index, (name, tail, route) in enumerate(EXPERT_PIECES):
            index += len(FLAT_PIECES) + k * len(EXPERT_PIECES)
            get[k].append(
                Gather(get_sems, index, getattr(r, "shard_" + name), getattr(r, name), tail, route, k, p)
            )
            put[k].append(
                Scatter(put_sems, index, getattr(r, name), landing(name), getattr(r, "out_" + name),
                        tail, route, k, p)
            )

    def gather_stage(k, step):
        for piece in get[k]:
            piece.stage(step)

    def scatter_stage(k, step):
        if step == 0 and k >= 2:
            pl.semaphore_wait(r.free_sem, 1)
        for piece in put[k]:
            piece.stage(step)
        if step == 1 and k < 2:
            pl.semaphore_signal(r.free_sem, inc=1, device_id=(p.core,), device_id_type=MESH)

    events = {
        ("image", 0): [("get", 0, 1), ("get", 1, 0)],
        ("image", 2): [("get", 0, 2), ("get", 1, 1), ("get", 2, 0)],
        ("middle", 0): [("get", 1, 2), ("get", 2, 1), ("get", 3, 0)],
        ("loop", 0): [("put", 0, 0)],
        ("dispatch", 1): [("put", 0, 1)],
        ("middle", 1): [("get", 2, 2), ("get", 3, 1)],
        ("loop", 1): [("put", 0, 2), ("put", 1, 0)],
        ("dispatch", 2): [("put", 1, 1)],
        ("middle", 2): [("get", 3, 2), ("put", 0, 3)],
        ("loop", 2): [("put", 1, 2), ("put", 2, 0)],
        ("dispatch", 3): [("put", 2, 1)],
        ("middle", 3): [("put", 1, 3)],
        ("loop", 3): [("put", 2, 2), ("put", 3, 0)],
        ("combine", 3): [("put", 3, 1)],
        ("back", 1): [("put", 2, 3), ("put", 3, 2)],
        ("back", 3): [("put", 3, 3)],
    }

    def fetch(i, both):
        copies = [pltpu.make_async_copy(r.images.at[i], r.image_at.at[i % 2], r.in_sem.at[0, i % 2])]
        if both:
            copies.append(
                pltpu.make_async_copy(r.cotangent.at[i], r.other_at.at[i % 2], r.in_sem.at[1, i % 2])
            )
        return copies

    def emit(i):
        return [
            pltpu.make_async_copy(r.other_at.at[i % 2], r.blocks.at[i], r.out_sem.at[0, i % 2]),
            pltpu.make_async_copy(r.grad_at.at[i % 2], r.gimages.at[i], r.out_sem.at[1, i % 2]),
        ]

    def start(copies):
        for copy in copies:
            copy.start()

    def wait(copies):
        for copy in copies:
            copy.wait()

    def event(*key):
        for kind, k, step in events.get(key, ()):
            (gather_stage if kind == "get" else scatter_stage)(k, step)

    start(fetch(0, True))
    local = []
    for index, piece in enumerate(flat_get + get[0]):
        copy = piece.local(r.local_sem.at[index])
        copy.start()
        local.append(copy)
    for piece in flat_get:
        piece.start_z()
    own_vectors(p.me, r)
    sums = SumAll((r.vec_send, r.vec_recv), 0, r.vec, r.land_vec, p)
    sums.begin(0)
    r.xs[...] = jnp.zeros_like(r.xs)
    r.gvec[...] = jnp.zeros_like(r.gvec)
    r.total[...] = jnp.zeros_like(r.total)
    for copy in local:
        copy.wait()
    for step in range(3):
        for piece in flat_get:
            piece.stage(step)
        sums.end(step)
        sums.begin(step + 1)
        if step == 0:
            for k in range(1, EXPERTS):
                for piece in get[k]:
                    piece.start_z()
            routing(r)
        if step == 1:
            gather_stage(0, 0)
    sums.end(3)
    spread_router(r)
    for piece in flat_get:
        piece.finish()
    for i in range(SLOTS):
        if i + 1 < SLOTS:
            start(fetch(i + 1, True))
        wait(fetch(i, True))
        attention_forward(i, r)
        event("image", i)
    for k in range(EXPERTS):
        e = p.plane(k)
        dispatch(e, r)
        event("dispatch", k)
        for piece in get[k]:
            piece.finish()
        for half in range(2):
            lax.fori_loop(
                half * 4, half * 4 + 4, lambda f, c: (expert_step(e, f, k, r), c)[1], 0
            )
            event("loop" if half else "middle", k)
        combine(e, r)
        event("combine", k)
    start(fetch(0, False))
    for i in range(SLOTS):
        if i + 1 < SLOTS:
            start(fetch(i + 1, False))
        wait(fetch(i, False))
        if i >= 2:
            wait(emit(i - 2))
        attention_backward(i, r)
        start(emit(i))
        event("back", i)
    sums = SumAll((r.vec_send, r.vec_recv), 1, r.gvec, r.land_gvec, p)
    sums.begin(0)
    weight_grads(r)
    for piece in flat_put:
        piece.stage(0)
    for step in range(1, 4):
        sums.end(step - 1)
        sums.begin(step)
        for piece in flat_put:
            piece.stage(step)
    for k in range(1, EXPERTS):
        for piece in put[k]:
            for copy in piece.along_z():
                copy.wait_recv()
    for piece in put[0]:
        piece.collect()
    sums.end(3)
    for piece in flat_put:
        for copy in piece.along_z():
            copy.wait_recv()
        piece.collect()
    for pieces in put + [flat_put]:
        for piece in pieces:
            piece.drain()
    for i in range(SLOTS - 2, SLOTS):
        wait(emit(i))


def alone_kernel(*refs):
    names = INPUTS + ["pack"] + ["full_" + n for n in SHARDS]
    names += ["blocks", "gimages", "gvec"] + ["out_" + n for n in SHARDS]
    names += list(SCRATCH) + ["vec", "sem"]
    r = Refs(names, refs)

    def move(source, target):
        copy = pltpu.make_async_copy(source, target, r.sem)
        copy.start()
        copy.wait()

    for name in SHARDS:
        move(getattr(r, "full_" + name), getattr(r, name))
    r.vec[...] = r.pack[...]
    r.xs[...] = jnp.zeros_like(r.xs)
    r.gvec[...] = jnp.zeros_like(r.gvec)
    r.total[...] = jnp.zeros_like(r.total)
    spread_router(r)
    routing(r)

    def forward(i, carry):
        move(r.images.at[i], r.image_at.at[i % 2])
        move(r.cotangent.at[i], r.other_at.at[i % 2])
        attention_forward(i, r)
        return carry

    def expert(e, carry):
        dispatch(e, r)
        lax.fori_loop(0, HID // FT, lambda f, c: (expert_step(e, f, e, r), c)[1], 0)
        combine(e, r)
        return carry

    def backward(i, carry):
        move(r.images.at[i], r.image_at.at[i % 2])
        attention_backward(i, r)
        move(r.other_at.at[i % 2], r.blocks.at[i])
        move(r.grad_at.at[i % 2], r.gimages.at[i])
        return carry

    lax.fori_loop(0, SLOTS, forward, 0)
    lax.fori_loop(0, EXPERTS, expert, 0)
    lax.fori_loop(0, SLOTS, backward, 0)
    weight_grads(r)
    for name in SHARDS:
        move(getattr(r, name), getattr(r, "out_" + name))


def alone(inputs, pack, full):
    vmem = pl.BlockSpec(memory_space=pltpu.VMEM)
    hbm = pl.BlockSpec(memory_space=pltpu.HBM)
    smem = pl.BlockSpec(memory_space=pltpu.SMEM)
    shapes = [((SLOTS, SEQ, D), BF16), ((SLOTS, SEQ, D), BF16), ((32, D), F32)]
    shapes += [SCRATCH[name] for name in SHARDS]
    return pl.pallas_call(
        alone_kernel,
        out_shape=[jax.ShapeDtypeStruct(*s) for s in shapes],
        in_specs=[smem] + [hbm] * 2 + [vmem] * 3 + [hbm] * 4,
        out_specs=[hbm] * 2 + [vmem] + [hbm] * 4,
        scratch_shapes=[pltpu.VMEM(*s) for s in SCRATCH.values()]
        + [pltpu.VMEM((32, D), F32), pltpu.SemaphoreType.DMA],
        compiler_params=pltpu.CompilerParams(vmem_limit_bytes=VMEM_LIMIT),
    )(*inputs, pack, *full)


def whole(inputs, pack, shards):
    vmem = pl.BlockSpec(memory_space=pltpu.VMEM)
    hbm = pl.BlockSpec(memory_space=pltpu.HBM)
    smem = pl.BlockSpec(memory_space=pltpu.SMEM)
    shapes = [((SLOTS, SEQ, D), BF16), ((SLOTS, SEQ, D), BF16), ((32, D), F32)]
    shapes += [(s, F32) for s in SHARDS.values()]
    count = len(FLAT_PIECES) + EXPERTS * len(EXPERT_PIECES)
    dma = pltpu.SemaphoreType.DMA
    return pl.pallas_call(
        whole_kernel,
        out_shape=[jax.ShapeDtypeStruct(*s) for s in shapes],
        in_specs=[smem] + [hbm] * 2 + [vmem] * 3 + [hbm] * 4,
        out_specs=[hbm] * 2 + [vmem] * (len(shapes) - 2),
        scratch_shapes=[pltpu.VMEM(*s) for s in SCRATCH.values()]
        + [pltpu.VMEM((32, D), F32)]
        + [pltpu.VMEM((6, 32, D), F32)] * 2
        + [pltpu.VMEM(*s) for s in LANDING.values()]
        + [dma((len(FLAT_PIECES) + len(EXPERT_PIECES),)), dma((2, 7)), dma((2, 7))]
        + [dma((count, 9)), dma((count, 9)), dma((count, 6)), dma((count, 6))]
        + [pltpu.SemaphoreType.REGULAR, dma((2, 2)), dma((2, 2))],
        compiler_params=pltpu.CompilerParams(
            collective_id=0, has_side_effects=True, vmem_limit_bytes=VMEM_LIMIT
        ),
        cost_estimate=pl.CostEstimate(
            flops=40 * 10**9, bytes_accessed=50 * 10**6, transcendentals=10**7
        ),
    )(*inputs, pack, *shards)


def per_device(
    images, cotangent, routes, priority, image_count,
    ln1_gain, ln1_bias, w_qkv, b_qv, w_out, b_out, ln2_gain, ln2_bias,
    w_router, w_in, b_in, w_back, b_back,
):
    me = lax.axis_index("dev")
    route_rows = jnp.pad(
        routes.reshape(SLOTS, SEQ, 2), ((0, 0), (0, ROWS - SEQ), (0, 0)), constant_values=-1
    ).reshape(TOK, 2)
    place = priority[0]
    place = place + (place // SEQ) * (ROWS - SEQ)
    extra = -place.shape[0] % LANES
    place_row = jnp.pad(place, (0, extra), constant_values=-1)[None, :]
    inputs = (image_count, images, cotangent, route_rows, place_row)
    if lax.axis_size("dev") != GROUP:
        return with_collectives(
            inputs, ln1_gain, ln1_bias, w_qkv, b_qv, w_out, b_out, ln2_gain, ln2_bias,
            w_router, w_in, b_in, w_back, b_back,
        )
    small = [ln1_gain, ln1_bias, b_qv, b_out, ln2_gain, ln2_bias, None, w_router, b_back, b_in]
    pack, at = 0.0, 0
    for v in small:
        size = 16 if v is None else v.shape[0]
        if v is not None:
            pack = pack + jnp.pad(v.astype(F32), (at, 8 * LANES - at - size))
        at += size
    shards = [v.reshape(s) for v, s in zip((w_qkv, w_out, w_in, w_back), SHARDS.values())]
    blocks, gimages, gvec, gwqkv, gwout, gwin, gwback = whole(
        inputs, pack.reshape(8, LANES), shards
    )
    cut = lambda v, size: lax.dynamic_slice(v.reshape(-1), (me * size,), (size,))
    return (
        blocks, gimages, cut(gvec[0], 16), cut(gvec[1], 16), gwqkv.reshape(-1),
        cut(gvec[2:4], 32), gwout.reshape(-1), cut(gvec[4], 16), cut(gvec[5], 16),
        cut(gvec[6], 16), cut(gvec[8:12].T, 64), gwin.reshape(-1), cut(gvec[16:32], 256),
        gwback.reshape(-1), cut(gvec[12:16], 64),
    )


def with_collectives(
    inputs, ln1_gain, ln1_bias, w_qkv, b_qv, w_out, b_out, ln2_gain, ln2_bias,
    w_router, w_in, b_in, w_back, b_back,
):
    gather = lambda v: lax.all_gather(v, "dev", axis=0, tiled=True)
    scatter = lambda v: lax.psum_scatter(
        v.astype(F32).reshape(-1), "dev", scatter_dimension=0, tiled=True
    )
    row = lambda v: gather(v).astype(F32).reshape(-1, D)
    zero = jnp.zeros((1, D), F32)
    pack = jnp.concatenate(
        [row(ln1_gain), row(ln1_bias), row(b_qv), row(b_out), row(ln2_gain), row(ln2_bias), zero,
         gather(w_router).astype(F32).reshape(D, EXPERTS).T, row(b_back), row(b_in)]
    )
    full = [
        gather(v).reshape(SCRATCH[name][0]) for v, name in zip((w_qkv, w_out, w_in, w_back), SHARDS)
    ]
    blocks, gimages, gvec, gwqkv, gwout, gwin, gwback = alone(inputs, pack, full)
    return (
        blocks, gimages, scatter(gvec[0]), scatter(gvec[1]), scatter(gwqkv), scatter(gvec[2:4]),
        scatter(gwout), scatter(gvec[4]), scatter(gvec[5]), scatter(gvec[6]),
        scatter(gvec[8:12].T), scatter(gwin), scatter(gvec[16:32]), scatter(gwback),
        scatter(gvec[12:16]),
    )


def solution(mesh):
    split = P("dev")
    return jax.shard_map(
        per_device, mesh=mesh, in_specs=(split,) * 18, out_specs=(split,) * 15, check_vma=False
    )
```

```python
import functools

import jax
import jax.numpy as jnp
from jax import lax
from jax.experimental import pallas as pl
from jax.experimental.pallas import tpu as pltpu
from jax.sharding import PartitionSpec as P

D = 512
HEADS = 8
HID = 2048
EXPERTS = 4
SEQ = 197
SLOTS = 5
HEAD_DIM = 64
CAP = 555
EPSILON = 1e-06

ROWS = -(-SEQ // 16) * 16
TOK = SLOTS * ROWS
CAPP = -(-CAP // 16) * 16
LANES = 128
WIDE = 2 * D + LANES
GROUP = EXPERTS * 2 * 2 * 2
BLOCK_IN = EXPERTS * D // GROUP
BLOCK_BACK = EXPERTS * HID // GROUP
SLOT_TILE = CAPP // 5
FT = 256
VMEM_LIMIT = 63 * 1024 * 1024
MESH = pl.DeviceIdType.MESH
FULL = slice(None)
F32 = jnp.float32
BF16 = jnp.bfloat16


def mm(a, b):
    return lax.dot_general(a, b, (((1,), (0,)), ((), ())), preferred_element_type=F32)


def mm_nt(a, b):
    return lax.dot_general(a, b, (((1,), (1,)), ((), ())), preferred_element_type=F32)


def mm_tn(a, b):
    return lax.dot_general(a, b, (((0,), (0,)), ((), ())), preferred_element_type=F32)


def iota(shape, dim):
    return lax.broadcasted_iota(jnp.int32, shape, dim)


def normalize(inputs):
    centre = inputs - jnp.mean(inputs, axis=-1, keepdims=True)
    inverse = lax.rsqrt(jnp.mean(centre * centre, axis=-1, keepdims=True) + EPSILON)
    return centre * inverse, inverse


def norm_back(grad_normed, scaled, inverse, gain):
    grad_scaled = grad_normed * gain
    return inverse * (
        grad_scaled
        - jnp.mean(grad_scaled, axis=-1, keepdims=True)
        - scaled * jnp.mean(grad_scaled * scaled, axis=-1, keepdims=True)
    )


def gelu_parts(pre):
    size = jnp.abs(pre)
    t = 1.0 / (1.0 + (0.3275911 * 0.7071067811865476) * size)
    bell = jnp.exp(-0.5 * (pre * pre))
    poly = t * (
        0.127414796
        + t * (-0.142248368 + t * (0.7107068705 + t * (-0.7265760135 + t * 0.5307027145)))
    )
    tail = poly * bell
    phi = jnp.where(pre >= 0, 1.0 - tail, tail)
    return pre * phi, phi + pre * (bell * 0.3989422804014327)


def split3(value):
    high = value.astype(BF16).astype(F32)
    rest = value - high
    mid = rest.astype(BF16).astype(F32)
    return high, mid, rest - mid


def image_rows(i):
    return pl.ds(i * ROWS if isinstance(i, int) else pl.multiple_of(i * ROWS, 16), ROWS)


def attention_forward(i, r):
    rows = image_rows(i)
    r.xs[0:SEQ, :] = r.image_at[i % 2].astype(F32)
    hidden = r.xs[...]
    scaled, _ = normalize(hidden)
    normed = (scaled * r.vec[0:1, :] + r.vec[1:2, :]).astype(BF16)
    projected = mm(normed, r.wqkv[...].reshape(D, 3 * D))
    r.qkv[rows, 0:D] = (projected[:, :D] + r.vec[2:3, :]).astype(BF16)
    r.qkv[rows, D : 2 * D] = projected[:, D : 2 * D].astype(BF16)
    r.qkv[rows, 2 * D :] = (projected[:, 2 * D :] + r.vec[3:4, :]).astype(BF16)
    lane = iota((ROWS, LANES), 1)
    column = iota((ROWS, ROWS), 1)
    for pair in range(HEADS // 2):
        at = pair * LANES
        queries = r.qkv[rows, at : at + LANES]
        keys = r.qkv[rows, D + at : D + at + LANES]
        values = r.qkv[rows, 2 * D + at : 2 * D + at + LANES]
        mixes = []
        for half in range(2):
            mine = (lane >= half * HEAD_DIM) & (lane < (half + 1) * HEAD_DIM)
            own = jnp.where(mine, queries, jnp.zeros_like(queries))
            scores = mm_nt(own, keys) * HEAD_DIM**-0.5
            scores = jnp.where(column < SEQ, scores, -1e30)
            expo = jnp.exp(scores - jnp.max(scores, axis=-1, keepdims=True))
            probs = (expo / jnp.sum(expo, axis=-1, keepdims=True)).astype(BF16)
            r.probs[i * HEADS + 2 * pair + half] = probs
            mixes.append(mm(probs, values))
        r.mix[rows, at : at + LANES] = jnp.where(lane < HEAD_DIM, mixes[0], mixes[1]).astype(BF16)
    residual = hidden + mm(r.mix[rows, :], r.wout[...].reshape(D, D)) + r.vec[4:5, :]
    r.residual[rows, :] = residual
    scaled2, _ = normalize(residual)
    normed2 = (scaled2 * r.vec[5:6, :] + r.vec[6:7, :]).astype(BF16)
    r.wide[rows, 0:D] = normed2
    logits = jnp.where(lane < EXPERTS, mm_nt(normed2, r.router[...]), -1e30)
    expo = jnp.exp(logits - jnp.max(logits, axis=-1, keepdims=True))
    gates = expo / jnp.sum(expo, axis=-1, keepdims=True)
    r.gates[rows, :] = gates
    high, mid, low = split3(gates)
    packed = high + pltpu.roll(mid, EXPERTS, 1) + pltpu.roll(low, 2 * EXPERTS, 1)
    r.wide[rows, 2 * D :] = packed.astype(BF16)
    live = jnp.where(i < r.count[0], 1.0, 0.0)
    r.xs[0:SEQ, :] = r.other_at[i % 2].astype(F32) * live
    r.wide[rows, D : 2 * D] = r.xs[...].astype(BF16)


def routing(r):
    limit = r.count[0] * ROWS
    places = r.prow.shape[1]
    lane = iota((ROWS, LANES), 1)

    def find(i, carry):
        rows = image_rows(i)
        place_row, wanted = carry
        seen = r.prow[...] == iota((ROWS, places), 0) + i * ROWS
        place = jnp.sum(
            jnp.where(seen, iota((ROWS, places), 1).astype(F32), 0.0), axis=1, keepdims=True
        )
        r.gates[rows, :] = jnp.broadcast_to(place, (ROWS, LANES))
        same = iota((ROWS, TOK), 0) + i * ROWS == iota((ROWS, TOK), 1)
        place_row = place_row + jnp.sum(jnp.where(same, place, 0.0), axis=0, keepdims=True)
        live = iota((ROWS, LANES), 0) + i * ROWS < limit
        hit0 = jnp.where((r.rcol[rows, 0:1] == lane) & live, 1.0, 0.0)
        hit1 = jnp.where((r.rcol[rows, 1:2] == lane) & live, 1.0, 0.0)
        r.wide[rows, 0:LANES] = hit0.astype(BF16)
        r.wide[rows, LANES : 2 * LANES] = hit1.astype(BF16)
        return place_row, wanted + jnp.sum(hit0, axis=0, keepdims=True)

    place_row, wanted = lax.fori_loop(
        0, SLOTS, find, (jnp.zeros((1, TOK), F32), jnp.zeros((1, LANES), F32))
    )
    r.total[0:LANES, 0:TOK] = jnp.zeros((LANES, TOK), F32)

    def count(i, carry):
        rows = image_rows(i)
        earlier = jnp.where(place_row < r.gates[rows, 0:1], 1.0, 0.0).astype(BF16)
        before = mm(earlier, r.wide[:, 0 : 2 * LANES])
        hit0, hit1 = r.wide[rows, 0:LANES] > 0, r.wide[rows, LANES : 2 * LANES] > 0
        position = jnp.where(
            hit0, before[:, 0:LANES], jnp.where(hit1, before[:, LANES:] + wanted, 1e6)
        )
        position = jnp.where(position < CAP, position, -1.0)
        r.pos_col[rows, :] = position
        same = iota((ROWS, TOK), 0) + i * ROWS == iota((ROWS, TOK), 1)
        same = jnp.where(same, 1.0, 0.0).astype(BF16)
        high = position.astype(BF16)
        low = (position - high.astype(F32)).astype(BF16)
        r.total[0:LANES, 0:TOK] += mm_tn(high, same) + mm_tn(low, same)
        return carry

    lax.fori_loop(0, SLOTS, count, 0)
    r.pos_row[...] = r.total[0:8, 0:TOK]
    r.total[0:LANES, 0:TOK] = jnp.zeros((LANES, TOK), F32)


def nothing(step):
    pass


def dispatch(e, r, beside=nothing):
    wanted = r.pos_row[pl.ds(e, 1), :]
    lane = iota((SLOT_TILE, LANES), 1)

    def tile(m, carry):
        beside(m)
        rows = pl.ds(pl.multiple_of(m * SLOT_TILE, 16), SLOT_TILE)
        slot = (iota((SLOT_TILE, TOK), 0) + m * SLOT_TILE).astype(F32)
        chosen = jnp.where(slot == wanted, 1.0, 0.0).astype(BF16)
        got = mm(chosen, r.wide[...])
        r.disp[rows, :] = got[:, 0:D].astype(BF16)
        r.up[rows, :] = got[:, D : 2 * D].astype(BF16)
        mine = (lane == e) | (lane == e + EXPERTS) | (lane == e + 2 * EXPERTS)
        gate = jnp.sum(jnp.where(mine, got[:, 2 * D :], 0.0), axis=1, keepdims=True)
        r.gate_slot[rows, :] = jnp.broadcast_to(gate, (SLOT_TILE, LANES))
        r.gexp[rows, :] = (gate * got[:, D : 2 * D]).astype(BF16)
        return carry

    lax.fori_loop(0, CAPP // SLOT_TILE, tile, 0)
    r.eo[...] = jnp.zeros_like(r.eo)
    r.gdisp[...] = jnp.zeros_like(r.gdisp)


def expert_step(e, f, k, r):
    cols = pl.ds(pl.multiple_of(f * FT, FT), FT)
    block = (k, f // 4, f // 2 % 2, f % 2)
    w_in = r.win[k, :, :, :, :, cols].reshape(D, FT)
    w_back = r.wback[block]
    disp = r.disp[...]
    gexp = r.gexp[...]
    bias = r.vec[pl.ds(16 + 4 * e + f // 2, 1), pl.ds(pl.multiple_of(f % 2 * FT, FT), FT)]
    pre = mm(disp, w_in) + bias
    grad_active = mm_nt(gexp, w_back)
    active, slope = gelu_parts(pre)
    active = active.astype(BF16)
    grad_inner = (grad_active * slope).astype(BF16)
    r.eo[...] += mm(active, w_back)
    r.gdisp[...] += mm_nt(grad_inner, w_in)
    r.wback[block] = mm_tn(active, gexp).astype(BF16)
    grad_in = mm_tn(disp, grad_inner).astype(BF16)
    r.win[k, :, :, :, :, cols] = grad_in.reshape(2, 2, 2, BLOCK_IN, FT)
    r.gvec[pl.ds(16 + 4 * e + f // 2, 1), pl.ds(pl.multiple_of(f % 2 * FT, FT), FT)] = jnp.sum(
        grad_inner.astype(F32), axis=0, keepdims=True
    )


def combine(e, r, beside=nothing):
    r.gvec[pl.ds(12 + e, 1), :] = jnp.sum(r.gexp[...].astype(F32), axis=0, keepdims=True)
    out = r.eo[...] + r.vec[pl.ds(12 + e, 1), :]
    gate = r.gate_slot[:, 0:1]
    r.disp[...] = (gate * out).astype(BF16)
    r.gexp[...] = r.gdisp[...].astype(BF16)
    high, mid, low = split3(jnp.sum(r.up[...].astype(F32) * out, axis=1, keepdims=True))
    lane = iota((CAPP, LANES), 1)
    parts = jnp.where(
        lane == e,
        high,
        jnp.where(lane == e + EXPERTS, mid, jnp.where(lane == e + 2 * EXPERTS, low, 0.0)),
    )
    r.pairs[...] = parts.astype(BF16)

    def image(i, carry):
        beside(i)
        rows = image_rows(i)
        mine = iota((ROWS, LANES), 1) == e
        wanted = jnp.sum(jnp.where(mine, r.pos_col[rows, :], 0.0), axis=1, keepdims=True)
        chosen = jnp.where(wanted == iota((ROWS, CAPP), 1).astype(F32), 1.0, 0.0).astype(BF16)
        r.total[rows, 0:D] += mm(chosen, r.disp[...])
        r.total[rows, D : 2 * D] += mm(chosen, r.gexp[...])
        r.total[rows, 2 * D :] += mm(chosen, r.pairs[...])
        return carry

    lax.fori_loop(0, SLOTS, image, 0)


def norm_backward(i, r):
    rows = image_rows(i)
    lane = iota((ROWS, LANES), 1)
    live = jnp.where(i < r.count[0], 1.0, 0.0)
    residual = r.residual[rows, :]
    r.other_at[i % 2] = ((residual + r.total[rows, 0:D]) * live)[0:SEQ, :].astype(BF16)
    pairs = r.total[rows, 2 * D :]
    gates = r.gates[rows, :]
    grad_gates = (
        pairs + pltpu.roll(pairs, LANES - EXPERTS, 1) + pltpu.roll(pairs, LANES - 2 * EXPERTS, 1)
    )
    grad_gates = jnp.where(lane < EXPERTS, grad_gates, 0.0)
    grad_logits = (
        gates * (grad_gates - jnp.sum(grad_gates * gates, axis=-1, keepdims=True))
    ).astype(BF16)
    r.gvec[8:12, :] += mm_tn(grad_logits, r.wide[rows, 0:D])[0:EXPERTS, :]
    grad_normed2 = r.total[rows, D : 2 * D] + mm(grad_logits, r.router[...])
    scaled2, inverse2 = normalize(residual)
    r.gvec[5:6, :] += jnp.sum(grad_normed2 * scaled2, axis=0, keepdims=True)
    r.gvec[6:7, :] += jnp.sum(grad_normed2, axis=0, keepdims=True)
    grad_residual = r.wide[rows, D : 2 * D].astype(F32) + norm_back(
        grad_normed2, scaled2, inverse2, r.vec[5:6, :]
    )
    r.residual[rows, :] = grad_residual
    grad_attended = grad_residual.astype(BF16)
    r.wide[rows, D : 2 * D] = grad_attended
    r.gvec[4:5, :] += jnp.sum(grad_attended.astype(F32), axis=0, keepdims=True)
    r.wide[rows, 0:D] = mm_nt(grad_attended, r.wout[...].reshape(D, D)).astype(BF16)


def attention_backward(i, r):
    rows = image_rows(i)
    lane = iota((ROWS, LANES), 1)
    for pair in range(HEADS // 2):
        at = pair * LANES
        queries = r.qkv[rows, at : at + LANES]
        keys = r.qkv[rows, D + at : D + at + LANES]
        values = r.qkv[rows, 2 * D + at : 2 * D + at + LANES]
        from_mix = r.wide[rows, at : at + LANES]
        grad_q, grad_k, grad_v = [], 0.0, 0.0
        for half in range(2):
            mine = (lane >= half * HEAD_DIM) & (lane < (half + 1) * HEAD_DIM)
            own_q = jnp.where(mine, queries, jnp.zeros_like(queries))
            own_g = jnp.where(mine, from_mix, jnp.zeros_like(from_mix))
            probs_low = r.probs[i * HEADS + 2 * pair + half]
            probs = probs_low.astype(F32)
            grad_probs = mm_nt(own_g, values)
            weighted = grad_probs * probs
            grad_scores = (
                weighted - probs * jnp.sum(weighted, axis=-1, keepdims=True)
            ).astype(BF16)
            grad_v = grad_v + mm_tn(probs_low, own_g)
            grad_k = grad_k + mm_tn(grad_scores, own_q)
            grad_q.append(mm(grad_scores, keys))
        scale = HEAD_DIM**-0.5
        joined = jnp.where(lane < HEAD_DIM, grad_q[0], grad_q[1])
        r.qkv[rows, at : at + LANES] = (joined * scale).astype(BF16)
        r.qkv[rows, D + at : D + at + LANES] = (grad_k * scale).astype(BF16)
        r.qkv[rows, 2 * D + at : 2 * D + at + LANES] = grad_v.astype(BF16)
    grads = r.qkv[rows, :]
    r.gvec[2:3, :] += jnp.sum(grads[:, 0:D].astype(F32), axis=0, keepdims=True)
    r.gvec[3:4, :] += jnp.sum(grads[:, 2 * D :].astype(F32), axis=0, keepdims=True)
    grad_normed1 = mm_nt(grads, r.wqkv[...].reshape(D, 3 * D))
    r.xs[0:SEQ, :] = r.image_at[i % 2].astype(F32)
    scaled1, inverse1 = normalize(r.xs[...])
    r.wide[rows, 0:D] = (scaled1 * r.vec[0:1, :] + r.vec[1:2, :]).astype(BF16)
    r.gvec[0:1, :] += jnp.sum(grad_normed1 * scaled1, axis=0, keepdims=True)
    r.gvec[1:2, :] += jnp.sum(grad_normed1, axis=0, keepdims=True)
    grad_in = r.residual[rows, :] + norm_back(grad_normed1, scaled1, inverse1, r.vec[0:1, :])
    r.grad_at[i % 2] = grad_in[0:SEQ, :].astype(BF16)


def wout_grad(r):
    r.wout[...] = mm_tn(r.mix[...], r.wide[:, D : 2 * D]).astype(BF16).reshape(r.wout.shape)


def wqkv_grad(half, r):
    def columns(c, carry):
        cols = pl.ds(pl.multiple_of(c * FT, FT), FT)
        grad = mm_tn(r.wide[:, 0:D], r.qkv[:, cols]).astype(BF16)
        r.wqkv[:, :, :, :, :, cols] = grad.reshape(r.wqkv.shape[:5] + (FT,))
        return carry

    steps = 3 * D // FT // 2
    lax.fori_loop(half * steps, half * steps + steps, columns, 0)


def spread_router(r):
    r.router[...] = jnp.zeros_like(r.router)
    first = r.vec[8:16, :]
    r.router[0:16, :] = jnp.concatenate(
        [jnp.where(iota((8, D), 0) < EXPERTS, first, 0.0), jnp.zeros((8, D), F32)], axis=0
    ).astype(BF16)


def pattern(shape, match):
    return jnp.where(match(iota(shape, 0), iota(shape, 1)), 1.0, 0.0).astype(BF16)


def all_vectors(r):
    packs = r.small[...].reshape(GROUP * 8, LANES).astype(BF16)
    line, column = iota((GROUP * 8, D), 0), iota((GROUP * 8, D), 1)

    def row(match, line_of):
        spread = mm(packs, pattern((LANES, D), match))
        return lambda: jnp.sum(jnp.where(line == line_of, spread, 0.0), axis=0, keepdims=True)

    sixteenth = 8 * (column >> 4)
    for index, start in ((0, 0), (1, 16), (4, 64), (5, 80), (6, 96)):
        r.vec[index : index + 1, :] = row(lambda j, c: j == start + (c & 15), sixteenth)()
    for index in range(2):
        r.vec[2 + index : 3 + index, :] = row(
            lambda j, c: j == 32 + (c & 31), 8 * (16 * index + (column >> 5))
        )()
    r.vec[7:8, :] = jnp.zeros((1, D), F32)
    for e in range(EXPERTS):
        r.vec[8 + e : 9 + e, :] = row(lambda j, c: j == 4 * (c & 15) + e, sixteenth + 1)()
        r.vec[12 + e : 13 + e, :] = row(
            lambda j, c: j == 64 + (c & 63), 8 * (8 * e + (column >> 6)) + 1
        )()
    for device in range(GROUP):
        at = (device // 8, device // 4 % 2, device // 2 % 2, device % 2)
        for line_of in range(2):
            start = device % 2 * 256 + line_of * LANES
            r.vec[16 + device // 2 : 17 + device // 2, start : start + LANES] = r.small[
                at + (slice(2 + line_of, 3 + line_of), FULL)
            ]


def own_vectors(me, r):
    row, column = iota((8, D), 0), iota((8, D), 1)
    lane, line = iota((8, LANES), 1), iota((8, LANES), 0)

    def fold(values, match):
        parts = [v.astype(BF16) for v in split3(values)]
        chosen = pattern((D, LANES), match)
        return sum(mm(v, chosen) for v in parts)

    owner = jnp.where(
        row == 2, column >> 5, jnp.where(row == 3, 16 + (column >> 5), column >> 4)
    )
    top = jnp.where(owner == me, r.gvec[0:8, :], 0.0)
    by16 = fold(top, lambda c, j: (c & 15) == j)
    by32 = fold(top, lambda c, j: (c & 31) == j)
    for name, index in dict(ln1_gain=0, ln1_bias=1, b_out=4, ln2_gain=5, ln2_bias=6).items():
        getattr(r, "out_" + name)[...] = by16[index : index + 1, 0:16]
    r.out_b_qv[...] = by32[2:3, 0:32] + by32[3:4, 0:32]
    owner = jnp.where(row < 4, column >> 4, 8 * (row - 4) + (column >> 6))
    low = jnp.where(owner == me, r.gvec[8:16, :], 0.0)
    router = jnp.where((lane & 3) == line, fold(low, lambda c, j: (c & 15) == (j >> 2)), 0.0)
    r.out_w_router[...] = jnp.sum(jnp.where(line < 4, router, 0.0), axis=0, keepdims=True)[:, 0:64]
    back = jnp.where(line < 4, 0.0, fold(low, lambda c, j: (c & 63) == j))
    r.out_b_back[...] = jnp.sum(back, axis=0, keepdims=True)[:, 0:64]
    row, column = iota((16, D), 0), iota((16, D), 1)
    bias = jnp.where(2 * row + (column >> 8) == me, r.gvec[16:32, :], 0.0)
    bias = jnp.sum(bias, axis=0, keepdims=True)
    r.out_b_in[...] = bias[:, 0:256] + bias[:, 256:512]


class Place:
    def __init__(self):
        me = lax.axis_index("dev")
        self.me, self.c, self.x, self.y, self.z = me, me % 2, me // 2 % 2, me // 4 % 2, me // 8
        self.core = self.device(self.z, self.y, self.x, 1 - self.c)
        self.over_y = self.device(self.z, 1 - self.y, self.x, self.c)
        self.over_x = self.device(self.z, self.y, 1 - self.x, self.c)

    def device(self, z, y, x, c):
        return ((z * 2 + y) * 2 + x) * 2 + c

    def plane(self, k):
        return lax.rem(self.z + k + EXPERTS, EXPERTS)

    def above(self, k):
        return self.device(self.plane(k), self.y, self.x, self.c)

    def greet(self):
        barrier = pltpu.get_barrier_semaphore()
        friends = [self.above(k) for k in range(1, EXPERTS)]
        friends += [self.core, self.over_y, self.over_x]
        for friend in friends:
            pl.semaphore_signal(barrier, inc=1, device_id=(friend,), device_id_type=MESH)
        pl.semaphore_wait(barrier, len(friends))

    def first(self, route):
        return self.over_y if route == 0 else self.over_x

    def second(self, route):
        return self.over_x if route == 0 else self.over_y


class Copies:
    def __init__(self, sems, index):
        self.sems, self.index = sems, index

    def make(self, slot, source, target, device):
        send_sem, recv_sem = self.sems
        return pltpu.make_async_remote_copy(
            src_ref=source, dst_ref=target, send_sem=send_sem.at[self.index, slot],
            recv_sem=recv_sem.at[self.index, slot], device_id=(device,), device_id_type=MESH,
        )


class SumAll(Copies):
    def __init__(self, sems, index, values, landing, place):
        super().__init__(sems, index)
        self.values, self.landing, self.p = values, landing, place

    def stage(self, step):
        p = self.p
        targets = [
            [(k, p.above(k)) for k in range(1, EXPERTS)], [(4, p.over_y)], [(5, p.over_x)],
            [(6, p.core)],
        ][step]
        return [self.make(s, self.values, self.landing.at[s - 1], d) for s, d in targets]

    def begin(self, step):
        for copy in self.stage(step):
            copy.start()

    def end(self, step):
        for copy in self.stage(step):
            copy.wait()
        if step == 0:
            self.values[...] += self.landing[0] + self.landing[1] + self.landing[2]
        else:
            self.values[...] += self.landing[2 + step]


class Gather(Copies):
    def __init__(self, sems, index, shard, full, tail, route, k, place):
        super().__init__(sems, index)
        self.shard, self.full, self.tail, self.route, self.p = shard, full, tail, route, place
        self.k = k

    def at(self, lead, y, x, c):
        return self.full.at[(lead, y, x, c) + self.tail]

    def own(self):
        return self.shard.at[self.tail] if self.tail else self.shard

    def local(self, sem):
        p = self.p
        lead = p.z if self.k is None else 0
        return pltpu.make_async_copy(self.own(), self.at(lead, p.y, p.x, p.c), sem)

    def along_z(self, arriving):
        p = self.p
        if self.k is None:
            return [
                self.make(k, self.own(), self.at(p.plane(-k) if arriving else p.z, p.y, p.x, p.c),
                          p.above(k))
                for k in range(1, EXPERTS)
            ]
        if self.k == 0:
            return []
        return [self.make(1, self.own(), self.at(self.k, p.y, p.x, p.c), p.above(-self.k))]

    def lead(self):
        return FULL if self.k is None else self.k

    def across(self, step, arriving):
        p = self.p
        y, x = p.y, p.x
        if step == 0:
            if arriving:
                y, x = (1 - y, x) if self.route == 0 else (y, 1 - x)
            device = p.first(self.route)
        else:
            if arriving:
                y, x = 1 - y, 1 - x
            y, x = (FULL, x) if self.route == 0 else (y, FULL)
            device = p.second(self.route)
        block = self.at(self.lead(), y, x, p.c)
        return self.make(4 + step, block, block, device)

    def to_core(self, step, arriving):
        p = self.p
        y, x = p.y, p.x
        if step == 1:
            y, x = (1 - y, x) if self.route == 0 else (y, 1 - x)
        elif step == 2:
            y, x = (FULL, 1 - x) if self.route == 0 else (1 - y, FULL)
        block = self.at(self.lead(), y, x, 1 - p.c if arriving else p.c)
        return self.make(6 + step, block, block, p.core)

    def start_z(self):
        for copy in self.along_z(False):
            copy.start()

    def stage(self, step):
        if step == 0:
            for copy in self.along_z(True):
                copy.wait_recv()
        else:
            self.across(step - 1, True).wait_recv()
        if step < 2:
            self.across(step, False).start()
        self.to_core(step, False).start()

    def finish(self):
        for step in range(3):
            self.to_core(step, True).wait_recv()
        for copy in self.along_z(False):
            copy.wait_send()
        for step in range(2):
            self.across(step, False).wait_send()
        for step in range(3):
            self.to_core(step, False).wait_send()


class Scatter(Copies):
    def __init__(self, sems, index, full, landing, out, tail, route, k, place):
        super().__init__(sems, index)
        self.full, self.out, self.tail, self.route, self.p, self.k = (
            full, out, tail, route, place, k,
        )
        self.from_core, self.from_first, self.from_second, self.from_z = landing

    def lead(self):
        return FULL if self.k is None else self.k

    def landed(self, ref, spare):
        if self.k is None:
            return (FULL,) * (1 + spare) + self.tail
        return (self.k % ref.shape[0],) + (FULL,) * spare + self.tail

    def to_core(self):
        p = self.p
        return self.make(0, self.full.at[(self.lead(), FULL, FULL, 1 - p.c) + self.tail],
                         self.from_core.at[self.landed(self.from_core, 2)], p.core)

    def to_first(self):
        p = self.p
        y, x = (FULL, 1 - p.x) if self.route == 0 else (1 - p.y, FULL)
        return self.make(1, self.full.at[(self.lead(), y, x, p.c) + self.tail],
                         self.from_first.at[self.landed(self.from_first, 1)],
                         p.second(self.route))

    def to_second(self):
        p = self.p
        y, x = (1 - p.y, p.x) if self.route == 0 else (p.y, 1 - p.x)
        return self.make(2, self.full.at[(self.lead(), y, x, p.c) + self.tail],
                         self.from_second.at[self.landed(self.from_second, 0)],
                         p.first(self.route))

    def along_z(self):
        p = self.p
        steps = range(1, EXPERTS) if self.k is None else ([self.k] if self.k else [])
        return [
            self.make(2 + k, self.full.at[(p.plane(k) if self.k is None else k, p.y, p.x, p.c) + self.tail],
                      self.from_z.at[(k - 1,) + self.tail], p.above(k))
            for k in steps
        ]

    def add(self, mine, landed):
        def layer(k, carry):
            for at, source in zip(mine(k), landed(k)):
                self.full[at + self.tail] = self.full[at + self.tail] + source
            return carry

        if self.k is None:
            lax.fori_loop(0, EXPERTS, layer, 0)
        else:
            layer(self.k, 0)

    def slot(self, ref, k):
        return k if self.k is None else k % ref.shape[0]

    def stage(self, step):
        p, tail = self.p, self.tail
        if step == 0:
            self.to_core().start()
        elif step == 1:
            self.to_core().wait_recv()
            spots = [(y, x) for y in range(2) for x in range(2)]
            ref = self.from_core
            self.add(lambda k: [(k, y, x, p.c) for y, x in spots],
                     lambda k: [ref[(self.slot(ref, k), y, x) + tail] for y, x in spots])
            self.to_first().start()
        elif step == 2:
            self.to_first().wait_recv()
            ref = self.from_first
            self.add(lambda k: [(k, o, p.x, p.c) if self.route == 0 else (k, p.y, o, p.c) for o in range(2)],
                     lambda k: [ref[(self.slot(ref, k), o) + tail] for o in range(2)])
            self.to_second().start()
        else:
            self.to_second().wait_recv()
            ref = self.from_second
            self.add(lambda k: [(k, p.y, p.x, p.c)],
                     lambda k: [ref[(self.slot(ref, k),) + tail]])
            for copy in self.along_z():
                copy.start()

    def collect(self):
        p, tail = self.p, self.tail
        total = self.full[((p.z if self.k is None else 0), p.y, p.x, p.c) + tail].astype(F32)
        for k in range(EXPERTS - 1):
            total = total + self.from_z[(k,) + tail].astype(F32)
        rows, columns = total.shape
        height, width = self.full.shape[-2:]
        first_row, first_column = tail[0].start or 0, tail[1].start or 0
        step = width // LANES
        for j in range(columns // LANES):
            line = first_row * step + first_column // LANES + j
            self.out[pl.ds(line, rows, stride=step), :] = total[:, j * LANES : (j + 1) * LANES]

    def drain(self):
        self.to_core().wait_send()
        self.to_first().wait_send()
        self.to_second().wait_send()
        for copy in self.along_z():
            copy.wait_send()


class Refs:
    def __init__(self, names, refs):
        for name, ref in zip(names, refs, strict=True):
            setattr(self, name, ref)


SCRATCH = dict(
    image_at=((2, SEQ, D), BF16),
    other_at=((2, SEQ, D), BF16),
    grad_at=((2, SEQ, D), BF16),
    xs=((ROWS, D), F32),
    router=((LANES, D), BF16),
    qkv=((TOK, 3 * D), BF16),
    probs=((SLOTS * HEADS, ROWS, ROWS), BF16),
    mix=((TOK, D), BF16),
    residual=((TOK, D), F32),
    wide=((TOK, WIDE), BF16),
    gates=((TOK, LANES), F32),
    pos_col=((TOK, LANES), F32),
    pos_row=((8, TOK), F32),
    disp=((CAPP, D), BF16),
    up=((CAPP, D), BF16),
    gexp=((CAPP, D), BF16),
    gate_slot=((CAPP, LANES), F32),
    pairs=((CAPP, LANES), BF16),
    eo=((CAPP, D), F32),
    gdisp=((CAPP, D), F32),
    total=((TOK, WIDE), F32),
    wqkv=((EXPERTS, 2, 2, 2, 16, 3 * D), BF16),
    wout=((EXPERTS, 2, 2, 2, 16, D), BF16),
    win=((EXPERTS, 2, 2, 2, BLOCK_IN, HID), BF16),
    wback=((EXPERTS, 2, 2, 2, BLOCK_BACK, D), BF16),
)
SHARDS = dict(wqkv=(16, 3 * D), wout=(16, D), win=(BLOCK_IN, HID), wback=(BLOCK_BACK, D))


def columns_of(width, h):
    return (FULL, slice(h * width // 2, (h + 1) * width // 2))


def rows_of(height, h):
    return (slice(h * height // 2, (h + 1) * height // 2), FULL)


SMALL = dict(
    ln1_gain=16, ln1_bias=16, b_qv=32, b_out=16, ln2_gain=16, ln2_bias=16, w_router=64, b_in=256,
    b_back=64,
)
FLAT_PIECES = [("wqkv", columns_of(3 * D, h), h) for h in range(2)]
FLAT_PIECES += [("wout", columns_of(D, h), h) for h in range(2)]
FLAT_PIECES += [("small", (), 0)]
EXPERT_PIECES = [("win", rows_of(BLOCK_IN, h), h) for h in range(2)]
EXPERT_PIECES += [("wback", rows_of(BLOCK_BACK, h), h) for h in range(2)]
LANDING = {}
for name in ("wqkv", "wout"):
    for part, lead in dict(core=(4, 2, 2), first=(4, 2), second=(4,), z=(3,)).items():
        LANDING[name, part] = (lead + SHARDS[name], BF16)
for name in ("win", "wback"):
    for part, lead in dict(core=(2, 2, 2), first=(4, 2), second=(4,), z=(3,)).items():
        LANDING[name, part] = (lead + SHARDS[name], BF16)
INPUTS = ["count", "images", "cotangent", "rcol", "prow"]


def whole_kernel(*refs):
    names = INPUTS + ["shard_small"] + ["shard_" + n for n in SHARDS]
    names += ["blocks", "gimages"] + ["out_" + n for n in SHARDS] + ["out_" + n for n in SMALL]
    names += list(SCRATCH) + ["vec", "gvec", "small", "land_gvec"]
    names += ["land_" + "_".join(key) for key in LANDING]
    names += ["local_sem", "vec_send", "vec_recv", "get_send", "get_recv", "put_send", "put_recv"]
    names += ["free_sem", "in_sem", "out_sem"]
    r = Refs(names, refs)
    p = Place()
    p.greet()

    def landing(name):
        return [getattr(r, f"land_{name}_{part}") for part in ("core", "first", "second", "z")]

    get_sems, put_sems = (r.get_send, r.get_recv), (r.put_send, r.put_recv)
    flat_get, flat_put = [], []
    for index, (name, tail, route) in enumerate(FLAT_PIECES):
        flat_get.append(
            Gather(get_sems, index, getattr(r, "shard_" + name), getattr(r, name), tail, route, None, p)
        )
        if name != "small":
            flat_put.append(
                Scatter(put_sems, index, getattr(r, name), landing(name), getattr(r, "out_" + name),
                        tail, route, None, p)
            )
    get, put = [], []
    for k in range(EXPERTS):
        get.append([])
        put.append([])
        for index, (name, tail, route) in enumerate(EXPERT_PIECES):
            index += len(FLAT_PIECES) + k * len(EXPERT_PIECES)
            get[k].append(
                Gather(get_sems, index, getattr(r, "shard_" + name), getattr(r, name), tail, route, k, p)
            )
            put[k].append(
                Scatter(put_sems, index, getattr(r, name), landing(name), getattr(r, "out_" + name),
                        tail, route, k, p)
            )

    def part(pieces, which):
        return pieces if which is None else pieces[2 * which : 2 * which + 2]

    def gather_stage(k, step, which=None):
        for piece in part(get[k], which):
            piece.start_z() if step < 0 else piece.stage(step)

    def scatter_stage(k, step, which=None):
        if step == 0 and k >= 2 and which != 1:
            pl.semaphore_wait(r.free_sem, 1)
        for piece in part(put[k], which):
            piece.stage(step)
        if step == 1 and k < 2 and which != 0:
            pl.semaphore_signal(r.free_sem, inc=1, device_id=(p.core,), device_id_type=MESH)

    def wout_stage(step):
        for piece in flat_put[2:4]:
            piece.stage(step)

    events = {
        ("start",): [("get", 0, 0, 1), ("get", 0, 1, 1), ("get", 2, -1, 1)],
        ("flat", 0): [("get", 1, -1, 1)],
        ("flat", 2): [("get", 2, -1, 0), ("get", 0, 0, 0), ("get", 1, -1, 0), ("get", 1, 0, 1)],
        ("flat", 3): [("get", 0, 1, 0)],
        ("forward", 0): [("get", 0, 2, 1), ("get", 1, 1, 1)],
        ("forward", 2): [("get", 1, 0, 0)],
        ("forward", 3): [("get", 0, 2, 0)],
        ("dispatch", 0, 1): [("get", 2, 0, 1)],
        ("dispatch", 0, 2): [("get", 3, -1, 0)],
        ("dispatch", 0, 3): [("get", 3, -1, 1)],
        ("dispatch", 0, 4): [("get", 1, 1, 0)],
        ("expert", 0, 1): [("get", 2, 0, 0)],
        ("expert", 0, 4): [("get", 2, 1, 1)],
        ("expert", 0, 7): [("get", 1, 2, 1)],
        ("combine", 0, 0): [("put", 0, 0, 0)],
        ("combine", 0, 1): [("get", 2, 1, 0)],
        ("combine", 0, 3): [("get", 1, 2, 0)],
        ("dispatch", 1, 2): [("get", 2, 2, 1)],
        ("dispatch", 1, 3): [("get", 3, 0, 1)],
        ("dispatch", 1, 4): [("get", 3, 0, 0)],
        ("expert", 1, 1): [("put", 0, 1, 0), ("put", 0, 0, 1)],
        ("expert", 1, 7): [("get", 3, 1, 1)],
        ("combine", 1, 0): [("get", 3, 1, 0)],
        ("combine", 1, 1): [("get", 2, 2, 0)],
        ("combine", 1, 2): [("put", 1, 0, 0)],
        ("dispatch", 2, 3): [("put", 1, 0, 1)],
        ("dispatch", 2, 4): [("put", 0, 2, 0)],
        ("expert", 2, 1): [("put", 0, 1, 1)],
        ("expert", 2, 3): [("put", 1, 1, 0)],
        ("expert", 2, 5): [("get", 3, 2, 1)],
        ("combine", 2, 0): [("put", 2, 0, 0)],
        ("combine", 2, 1): [("put", 1, 1, 1)],
        ("dispatch", 3, 1): [("get", 3, 2, 0)],
        ("dispatch", 3, 2): [("put", 2, 1, 0)],
        ("dispatch", 3, 3): [("put", 1, 2, 0)],
        ("expert", 3, 0): [("put", 2, 0, 1)],
        ("expert", 3, 2): [("put", 1, 2, 1), ("put", 0, 2, 1)],
        ("expert", 3, 5): [("put", 1, 3, 0)],
        ("expert", 3, 6): [("put", 2, 1, 1)],
        ("combine", 3, 1): [("put", 3, 0, 0)],
        ("combine", 3, 2): [("put", 1, 3, 1)],
        ("combine", 3, 4): [("put", 2, 2, 0)],
        ("norms", 0): [("put", 3, 0, 1), ("put", 2, 2, 1)],
        ("norms", 1): [("put", 3, 1, 0)],
        ("norms", 2): [("put", 2, 3, 0)],
        ("norms", 4): [("put", 3, 1, 1)],
        ("backward", 0): [("put", 2, 3, 1)],
        ("backward", 1): [("put", 0, 3, 0), ("out", 1), ("put", 3, 2, 0)],
        ("backward", 2): [("put", 0, 3, 1), ("put", 3, 2, 1)],
        ("backward", 3): [("out", 2)],
        ("backward", 4): [("put", 3, 3, 1), ("out", 3), ("put", 3, 3, 0)],
    }

    def beside(*key):
        def at(step):
            for (*found, when), todo in events.items():
                if tuple(found) == key:
                    pl.when(step == when)(functools.partial(act, todo))

        return at

    def act(todo):
        for kind, *what in todo:
            dict(get=gather_stage, put=scatter_stage, out=wout_stage)[kind](*what)

    def fetch(i, both):
        copies = [pltpu.make_async_copy(r.images.at[i], r.image_at.at[i % 2], r.in_sem.at[0, i % 2])]
        if both:
            copies.append(
                pltpu.make_async_copy(r.cotangent.at[i], r.other_at.at[i % 2], r.in_sem.at[1, i % 2])
            )
        return copies

    def emit_block(i):
        return [pltpu.make_async_copy(r.other_at.at[i % 2], r.blocks.at[i], r.out_sem.at[0, i % 2])]

    def emit_grad(i):
        return [pltpu.make_async_copy(r.grad_at.at[i % 2], r.gimages.at[i], r.out_sem.at[1, i % 2])]

    def start(copies):
        for copy in copies:
            copy.start()

    def wait(copies):
        for copy in copies:
            copy.wait()

    start(fetch(0, True))
    local = []
    for index, piece in enumerate(flat_get + get[0]):
        copy = piece.local(r.local_sem.at[index])
        copy.start()
        local.append(copy)
    for piece in flat_get:
        piece.start_z()
    for copy in local:
        copy.wait()
    act(events.get(("start",), ()))
    r.xs[...] = jnp.zeros_like(r.xs)
    r.gvec[...] = jnp.zeros_like(r.gvec)
    r.total[...] = jnp.zeros_like(r.total)
    for step in range(3):
        for piece in flat_get:
            piece.stage(step)
        if step == 0:
            routing(r)
        act(events.get(("flat", step), ()))
    for piece in flat_get:
        piece.finish()
    act(events.get(("flat", 3), ()))
    all_vectors(r)
    spread_router(r)

    def forward(i, carry):
        @pl.when(i + 1 < SLOTS)
        def _():
            start(fetch(i + 1, True))

        wait(fetch(i, True))
        attention_forward(i, r)
        beside("forward")(i)
        return carry

    lax.fori_loop(0, SLOTS, forward, 0)
    for k in range(EXPERTS):
        e = p.plane(k)
        dispatch(e, r, beside("dispatch", k))
        for piece in get[k]:
            piece.finish()

        def step(f, carry):
            beside("expert", k)(f)
            expert_step(e, f, k, r)
            return carry

        lax.fori_loop(0, HID // FT, step, 0)
        combine(e, r, beside("combine", k))
    start(fetch(0, False))

    def norms(i, carry):
        @pl.when(i >= 2)
        def _():
            wait(emit_block(i - 2))

        norm_backward(i, r)
        start(emit_block(i))
        beside("norms")(i)
        return carry

    lax.fori_loop(0, SLOTS, norms, 0)
    wout_grad(r)
    wqkv_put, wout_put = flat_put[0:2], flat_put[2:4]
    for piece in wout_put:
        piece.stage(0)

    def backward(i, carry):
        @pl.when(i + 1 < SLOTS)
        def _():
            start(fetch(i + 1, False))

        wait(fetch(i, False))

        @pl.when(i >= 2)
        def _():
            wait(emit_grad(i - 2))

        attention_backward(i, r)
        start(emit_grad(i))
        beside("backward")(i)
        return carry

    lax.fori_loop(0, SLOTS, backward, 0)
    sums = SumAll((r.vec_send, r.vec_recv), 0, r.gvec, r.land_gvec, p)
    sums.begin(0)
    wqkv_grad(0, r)
    wqkv_put[0].stage(0)
    wqkv_grad(1, r)
    wqkv_put[1].stage(0)
    for step in range(1, 4):
        sums.end(step - 1)
        sums.begin(step)
        for piece in wqkv_put:
            piece.stage(step)
    for k in range(1, EXPERTS):
        for piece in put[k]:
            for copy in piece.along_z():
                copy.wait_recv()
    for piece in put[0]:
        piece.collect()
    for piece in wout_put:
        for copy in piece.along_z():
            copy.wait_recv()
        piece.collect()
    sums.end(3)
    own_vectors(p.me, r)
    for piece in wqkv_put:
        for copy in piece.along_z():
            copy.wait_recv()
        piece.collect()
    for pieces in put + [flat_put]:
        for piece in pieces:
            piece.drain()
    for i in range(SLOTS - 2, SLOTS):
        wait(emit_block(i))
        wait(emit_grad(i))


def alone_kernel(*refs):
    names = INPUTS + ["pack"] + ["full_" + n for n in SHARDS]
    names += ["blocks", "gimages", "gvec"] + ["out_" + n for n in SHARDS]
    names += list(SCRATCH) + ["vec", "sem"]
    r = Refs(names, refs)

    def move(source, target):
        copy = pltpu.make_async_copy(source, target, r.sem)
        copy.start()
        copy.wait()

    for name in SHARDS:
        move(getattr(r, "full_" + name), getattr(r, name))
    r.vec[...] = r.pack[...]
    r.xs[...] = jnp.zeros_like(r.xs)
    r.gvec[...] = jnp.zeros_like(r.gvec)
    r.total[...] = jnp.zeros_like(r.total)
    spread_router(r)
    routing(r)

    def forward(i, carry):
        move(r.images.at[i], r.image_at.at[i % 2])
        move(r.cotangent.at[i], r.other_at.at[i % 2])
        attention_forward(i, r)
        return carry

    def expert(e, carry):
        dispatch(e, r)
        lax.fori_loop(0, HID // FT, lambda f, c: (expert_step(e, f, e, r), c)[1], 0)
        combine(e, r)
        return carry

    def norms(i, carry):
        norm_backward(i, r)
        move(r.other_at.at[i % 2], r.blocks.at[i])
        return carry

    def backward(i, carry):
        move(r.images.at[i], r.image_at.at[i % 2])
        attention_backward(i, r)
        move(r.grad_at.at[i % 2], r.gimages.at[i])
        return carry

    lax.fori_loop(0, SLOTS, forward, 0)
    lax.fori_loop(0, EXPERTS, expert, 0)
    lax.fori_loop(0, SLOTS, norms, 0)
    wout_grad(r)
    lax.fori_loop(0, SLOTS, backward, 0)
    for half in range(2):
        wqkv_grad(half, r)
    for name in SHARDS:
        move(getattr(r, name), getattr(r, "out_" + name))


def alone(inputs, pack, full):
    vmem = pl.BlockSpec(memory_space=pltpu.VMEM)
    hbm = pl.BlockSpec(memory_space=pltpu.HBM)
    smem = pl.BlockSpec(memory_space=pltpu.SMEM)
    shapes = [((SLOTS, SEQ, D), BF16), ((SLOTS, SEQ, D), BF16), ((32, D), F32)]
    shapes += [SCRATCH[name] for name in SHARDS]
    return pl.pallas_call(
        alone_kernel,
        out_shape=[jax.ShapeDtypeStruct(*s) for s in shapes],
        in_specs=[smem] + [hbm] * 2 + [vmem] * 3 + [hbm] * 4,
        out_specs=[hbm] * 2 + [vmem] + [hbm] * 4,
        scratch_shapes=[pltpu.VMEM(*s) for s in SCRATCH.values()]
        + [pltpu.VMEM((32, D), F32), pltpu.SemaphoreType.DMA],
        compiler_params=pltpu.CompilerParams(vmem_limit_bytes=VMEM_LIMIT),
    )(*inputs, pack, *full)


def whole(inputs, pack, shards):
    vmem = pl.BlockSpec(memory_space=pltpu.VMEM)
    hbm = pl.BlockSpec(memory_space=pltpu.HBM)
    smem = pl.BlockSpec(memory_space=pltpu.SMEM)
    shapes = [((SLOTS, SEQ, D), BF16), ((SLOTS, SEQ, D), BF16)]
    shapes += [((rows * columns // LANES, LANES), F32) for rows, columns in SHARDS.values()]
    shapes += [((1, size), F32) for size in SMALL.values()]
    count = len(FLAT_PIECES) + EXPERTS * len(EXPERT_PIECES)
    dma = pltpu.SemaphoreType.DMA
    return pl.pallas_call(
        whole_kernel,
        out_shape=[jax.ShapeDtypeStruct(*s) for s in shapes],
        in_specs=[smem] + [hbm] * 2 + [vmem] * 2 + [hbm] * 5,
        out_specs=[hbm] * 2 + [vmem] * (len(shapes) - 2),
        scratch_shapes=[pltpu.VMEM(*s) for s in SCRATCH.values()]
        + [pltpu.VMEM((32, D), F32)] * 2
        + [pltpu.VMEM((EXPERTS, 2, 2, 2, 8, LANES), F32), pltpu.VMEM((6, 32, D), F32)]
        + [pltpu.VMEM(*s) for s in LANDING.values()]
        + [dma((len(FLAT_PIECES) + len(EXPERT_PIECES),)), dma((1, 7)), dma((1, 7))]
        + [dma((count, 9)), dma((count, 9)), dma((count, 6)), dma((count, 6))]
        + [pltpu.SemaphoreType.REGULAR, dma((2, 2)), dma((2, 2))],
        compiler_params=pltpu.CompilerParams(
            collective_id=0, has_side_effects=True, vmem_limit_bytes=VMEM_LIMIT
        ),
        cost_estimate=pl.CostEstimate(
            flops=40 * 10**9, bytes_accessed=50 * 10**6, transcendentals=10**7
        ),
    )(*inputs, pack, *shards)


def per_device(
    images, cotangent, routes, priority, image_count,
    ln1_gain, ln1_bias, w_qkv, b_qv, w_out, b_out, ln2_gain, ln2_bias,
    w_router, w_in, b_in, w_back, b_back,
):
    route_rows = jnp.pad(
        routes.reshape(SLOTS, SEQ, 2), ((0, 0), (0, ROWS - SEQ), (0, 0)), constant_values=-1
    ).reshape(TOK, 2)
    place = priority[0]
    place = place + (place // SEQ) * (ROWS - SEQ)
    extra = -place.shape[0] % LANES
    place_row = jnp.pad(place, (0, extra), constant_values=-1)[None, :]
    inputs = (image_count, images, cotangent, route_rows, place_row)
    if lax.axis_size("dev") != GROUP:
        return with_collectives(
            inputs, ln1_gain, ln1_bias, w_qkv, b_qv, w_out, b_out, ln2_gain, ln2_bias,
            w_router, w_in, b_in, w_back, b_back,
        )
    small = [ln1_gain, ln1_bias, b_qv, b_out, ln2_gain, ln2_bias, None, w_router, b_back, b_in]
    pack, at = 0.0, 0
    for v in small:
        size = 16 if v is None else v.shape[0]
        if v is not None:
            pack = pack + jnp.pad(v.astype(F32), (at, 8 * LANES - at - size))
        at += size
    shards = [v.reshape(s) for v, s in zip((w_qkv, w_out, w_in, w_back), SHARDS.values())]
    blocks, gimages, *grads = whole(inputs, pack.reshape(8, LANES), shards)
    grads = dict(zip(["w_qkv", "w_out", "w_in", "w_back"] + list(SMALL), grads))
    order = ["ln1_gain", "ln1_bias", "w_qkv", "b_qv", "w_out", "b_out", "ln2_gain", "ln2_bias"]
    order += ["w_router", "w_in", "b_in", "w_back", "b_back"]
    return (blocks, gimages) + tuple(grads[name].reshape(-1) for name in order)


def with_collectives(
    inputs, ln1_gain, ln1_bias, w_qkv, b_qv, w_out, b_out, ln2_gain, ln2_bias,
    w_router, w_in, b_in, w_back, b_back,
):
    gather = lambda v: lax.all_gather(v, "dev", axis=0, tiled=True)
    scatter = lambda v: lax.psum_scatter(
        v.astype(F32).reshape(-1), "dev", scatter_dimension=0, tiled=True
    )
    row = lambda v: gather(v).astype(F32).reshape(-1, D)
    zero = jnp.zeros((1, D), F32)
    pack = jnp.concatenate(
        [row(ln1_gain), row(ln1_bias), row(b_qv), row(b_out), row(ln2_gain), row(ln2_bias), zero,
         gather(w_router).astype(F32).reshape(D, EXPERTS).T, row(b_back), row(b_in)]
    )
    full = [
        gather(v).reshape(SCRATCH[name][0]) for v, name in zip((w_qkv, w_out, w_in, w_back), SHARDS)
    ]
    blocks, gimages, gvec, gwqkv, gwout, gwin, gwback = alone(inputs, pack, full)
    return (
        blocks, gimages, scatter(gvec[0]), scatter(gvec[1]), scatter(gwqkv), scatter(gvec[2:4]),
        scatter(gwout), scatter(gvec[4]), scatter(gvec[5]), scatter(gvec[6]),
        scatter(gvec[8:12].T), scatter(gwin), scatter(gvec[16:32]), scatter(gwback),
        scatter(gvec[12:16]),
    )


def solution(mesh):
    split = P("dev")
    return jax.shard_map(
        per_device, mesh=mesh, in_specs=(split,) * 18, out_specs=(split,) * 15, check_vma=False
    )
```

```python
import functools

import jax
import jax.numpy as jnp
from jax import lax
from jax.experimental import pallas as pl
from jax.experimental.pallas import tpu as pltpu
from jax.sharding import PartitionSpec as P

D = 512
HEADS = 8
HID = 2048
EXPERTS = 4
SEQ = 197
SLOTS = 5
HEAD_DIM = 64
CAP = 555
EPSILON = 1e-06

ROWS = -(-SEQ // 16) * 16
TOK = SLOTS * ROWS
CAPP = -(-CAP // 16) * 16
LANES = 128
WIDE = 2 * D + LANES
GROUP = EXPERTS * 2 * 2 * 2
BLOCK_IN = EXPERTS * D // GROUP
BLOCK_BACK = EXPERTS * HID // GROUP
SLOT_TILE = CAPP // 5
FT = 512
QKV_PARTS = 4
VMEM_LIMIT = 65000 * 1024
MESH = pl.DeviceIdType.MESH
FULL = slice(None)
F32 = jnp.float32
BF16 = jnp.bfloat16


def mm(a, b):
    return lax.dot_general(a, b, (((1,), (0,)), ((), ())), preferred_element_type=F32)


def mm_nt(a, b):
    return lax.dot_general(a, b, (((1,), (1,)), ((), ())), preferred_element_type=F32)


def mm_tn(a, b):
    return lax.dot_general(a, b, (((0,), (0,)), ((), ())), preferred_element_type=F32)


def iota(shape, dim):
    return lax.broadcasted_iota(jnp.int32, shape, dim)


def normalize(inputs):
    centre = inputs - jnp.mean(inputs, axis=-1, keepdims=True)
    inverse = lax.rsqrt(jnp.mean(centre * centre, axis=-1, keepdims=True) + EPSILON)
    return centre * inverse, inverse


def norm_back(grad_normed, scaled, inverse, gain):
    grad_scaled = grad_normed * gain
    return inverse * (
        grad_scaled
        - jnp.mean(grad_scaled, axis=-1, keepdims=True)
        - scaled * jnp.mean(grad_scaled * scaled, axis=-1, keepdims=True)
    )


def gelu_parts(pre):
    size = jnp.abs(pre)
    t = 1.0 / (1.0 + (0.3275911 * 0.7071067811865476) * size)
    bell = jnp.exp(-0.5 * (pre * pre))
    poly = t * (
        0.127414796
        + t * (-0.142248368 + t * (0.7107068705 + t * (-0.7265760135 + t * 0.5307027145)))
    )
    tail = poly * bell
    phi = jnp.where(pre >= 0, 1.0 - tail, tail)
    return pre * phi, phi + pre * (bell * 0.3989422804014327)


def split3(value):
    high = value.astype(BF16).astype(F32)
    rest = value - high
    mid = rest.astype(BF16).astype(F32)
    return high, mid, rest - mid


def image_rows(i):
    return pl.ds(i * ROWS if isinstance(i, int) else pl.multiple_of(i * ROWS, 16), ROWS)


def two_heads(block):
    first = iota(block.shape, 1) < HEAD_DIM
    zero = jnp.zeros_like(block)
    return jnp.concatenate([jnp.where(first, block, zero), jnp.where(first, zero, block)], axis=0)


def attention_forward(i, r):
    rows = image_rows(i)
    r.xs[0:SEQ, :] = r.image_at[i % 2].astype(F32)
    hidden = r.xs[...]
    scaled, _ = normalize(hidden)
    normed = (scaled * r.vec[0:1, :] + r.vec[1:2, :]).astype(BF16)
    projected = mm(normed, r.wqkv[...].reshape(D, 3 * D))
    r.qkv[rows, 0:D] = (projected[:, :D] + r.vec[2:3, :]).astype(BF16)
    r.qkv[rows, D : 2 * D] = projected[:, D : 2 * D].astype(BF16)
    r.qkv[rows, 2 * D :] = (projected[:, 2 * D :] + r.vec[3:4, :]).astype(BF16)
    lane = iota((ROWS, LANES), 1)
    column = iota((2 * ROWS, ROWS), 1)
    for pair in range(HEADS // 2):
        at = pair * LANES
        queries = r.qkv[rows, at : at + LANES]
        keys = r.qkv[rows, D + at : D + at + LANES]
        values = r.qkv[rows, 2 * D + at : 2 * D + at + LANES]
        both = two_heads(queries)
        scores = mm_nt(both, keys) * HEAD_DIM**-0.5
        scores = jnp.where(column < SEQ, scores, -1e30)
        expo = jnp.exp(scores - jnp.max(scores, axis=-1, keepdims=True))
        probs = (expo / jnp.sum(expo, axis=-1, keepdims=True)).astype(BF16)
        r.probs[i * (HEADS // 2) + pair] = probs
        mixed = mm(probs, values)
        r.mix[rows, at : at + LANES] = jnp.where(
            lane < HEAD_DIM, mixed[:ROWS], mixed[ROWS:]
        ).astype(BF16)
    residual = hidden + mm(r.mix[rows, :], r.wout[...].reshape(D, D)) + r.vec[4:5, :]
    r.residual[rows, :] = residual
    scaled2, _ = normalize(residual)
    normed2 = (scaled2 * r.vec[5:6, :] + r.vec[6:7, :]).astype(BF16)
    r.wide[rows, 0:D] = normed2
    logits = jnp.where(lane < EXPERTS, mm_nt(normed2, r.router[...]), -1e30)
    expo = jnp.exp(logits - jnp.max(logits, axis=-1, keepdims=True))
    gates = expo / jnp.sum(expo, axis=-1, keepdims=True)
    r.gates[rows, :] = gates
    high, mid, low = split3(gates)
    packed = high + pltpu.roll(mid, EXPERTS, 1) + pltpu.roll(low, 2 * EXPERTS, 1)
    r.wide[rows, 2 * D :] = packed.astype(BF16)
    live = jnp.where(i < r.count[0], 1.0, 0.0)
    r.xs[0:SEQ, :] = r.other_at[i % 2].astype(F32) * live
    r.wide[rows, D : 2 * D] = r.xs[...].astype(BF16)


def routing(r):
    limit = r.count[0] * ROWS
    order = r.order[...]
    places = order.shape[1]
    for image in range(1, SLOTS):
        order = order + jnp.where(r.order[...] >= image * SEQ, ROWS - SEQ, 0)
    lane = iota((ROWS, LANES), 1)

    def find(i, carry):
        rows = image_rows(i)
        place_row, wanted = carry
        seen = order == iota((ROWS, places), 0) + i * ROWS
        place = jnp.sum(
            jnp.where(seen, iota((ROWS, places), 1).astype(F32), 0.0), axis=1, keepdims=True
        )
        r.gates[rows, :] = jnp.broadcast_to(place, (ROWS, LANES))
        same = iota((ROWS, TOK), 0) + i * ROWS == iota((ROWS, TOK), 1)
        place_row = place_row + jnp.sum(jnp.where(same, place, 0.0), axis=0, keepdims=True)
        row = iota((ROWS, LANES), 0)
        live = (row + i * ROWS < limit) & (row < SEQ)
        own = iota((ROWS, places), 0) + i * SEQ == iota((ROWS, places), 1)
        first = jnp.sum(jnp.where(own, r.routes[0:1, :], 0), axis=1, keepdims=True)
        second = jnp.sum(jnp.where(own, r.routes[1:2, :], 0), axis=1, keepdims=True)
        hit0 = jnp.where((first == lane) & live, 1.0, 0.0)
        hit1 = jnp.where((second == lane) & live, 1.0, 0.0)
        r.wide[rows, 0:LANES] = hit0.astype(BF16)
        r.wide[rows, LANES : 2 * LANES] = hit1.astype(BF16)
        return place_row, wanted + jnp.sum(hit0, axis=0, keepdims=True)

    place_row, wanted = lax.fori_loop(
        0, SLOTS, find, (jnp.zeros((1, TOK), F32), jnp.zeros((1, LANES), F32))
    )
    r.total[0:LANES, 0:TOK] = jnp.zeros((LANES, TOK), F32)

    def count(i, carry):
        rows = image_rows(i)
        earlier = jnp.where(place_row < r.gates[rows, 0:1], 1.0, 0.0).astype(BF16)
        before = mm(earlier, r.wide[:, 0 : 2 * LANES])
        hit0, hit1 = r.wide[rows, 0:LANES] > 0, r.wide[rows, LANES : 2 * LANES] > 0
        position = jnp.where(
            hit0, before[:, 0:LANES], jnp.where(hit1, before[:, LANES:] + wanted, 1e6)
        )
        position = jnp.where(position < CAP, position, -1.0)
        r.pos_col[rows, :] = position
        same = iota((ROWS, TOK), 0) + i * ROWS == iota((ROWS, TOK), 1)
        same = jnp.where(same, 1.0, 0.0).astype(BF16)
        high = position.astype(BF16)
        low = (position - high.astype(F32)).astype(BF16)
        r.total[0:LANES, 0:TOK] += mm_tn(high, same) + mm_tn(low, same)
        return carry

    lax.fori_loop(0, SLOTS, count, 0)
    r.pos_row[...] = r.total[0:8, 0:TOK]
    r.total[0:LANES, 0:TOK] = jnp.zeros((LANES, TOK), F32)


def nothing(step):
    pass


def dispatch(e, r, beside=nothing):
    wanted = r.pos_row[pl.ds(e, 1), :]
    lane = iota((SLOT_TILE, LANES), 1)

    def tile(m, carry):
        beside(m)
        rows = pl.ds(pl.multiple_of(m * SLOT_TILE, 16), SLOT_TILE)
        slot = (iota((SLOT_TILE, TOK), 0) + m * SLOT_TILE).astype(F32)
        chosen = jnp.where(slot == wanted, 1.0, 0.0).astype(BF16)
        got = mm(chosen, r.wide[...])
        r.disp[rows, :] = got[:, 0:D].astype(BF16)
        r.up[rows, :] = got[:, D : 2 * D].astype(BF16)
        mine = (lane == e) | (lane == e + EXPERTS) | (lane == e + 2 * EXPERTS)
        gate = jnp.sum(jnp.where(mine, got[:, 2 * D :], 0.0), axis=1, keepdims=True)
        r.gate_slot[rows, :] = jnp.broadcast_to(gate, (SLOT_TILE, LANES))
        r.gexp[rows, :] = (gate * got[:, D : 2 * D]).astype(BF16)
        return carry

    lax.fori_loop(0, CAPP // SLOT_TILE, tile, 0)
    r.eo[...] = jnp.zeros_like(r.eo)
    r.gdisp[...] = jnp.zeros_like(r.gdisp)


def expert_step(e, f, k, r):
    cols = pl.ds(pl.multiple_of(f * FT, FT), FT)
    block = (k, f // 2, f % 2)
    w_in = r.win[k, :, :, :, :, cols].reshape(D, FT)
    w_back = r.wback[block].reshape(FT, D)
    disp = r.disp[...]
    gexp = r.gexp[...]
    bias = r.vec[pl.ds(16 + 4 * e + f, 1), :]
    pre = mm(disp, w_in) + bias
    grad_active = mm_nt(gexp, w_back)
    active, slope = gelu_parts(pre)
    active = active.astype(BF16)
    grad_inner = (grad_active * slope).astype(BF16)
    r.eo[...] += mm(active, w_back)
    r.gdisp[...] += mm_nt(grad_inner, w_in)
    r.wback[block] = mm_tn(active, gexp).astype(BF16).reshape(2, BLOCK_BACK, D)
    grad_in = mm_tn(disp, grad_inner).astype(BF16)
    r.win[k, :, :, :, :, cols] = grad_in.reshape(2, 2, 2, BLOCK_IN, FT)
    r.gvec[pl.ds(16 + 4 * e + f, 1), :] = jnp.sum(
        grad_inner.astype(F32), axis=0, keepdims=True
    )


def combine(e, r, beside=nothing):
    r.gvec[pl.ds(12 + e, 1), :] = jnp.sum(r.gexp[...].astype(F32), axis=0, keepdims=True)
    out = r.eo[...] + r.vec[pl.ds(12 + e, 1), :]
    gate = r.gate_slot[:, 0:1]
    r.disp[...] = (gate * out).astype(BF16)
    r.gexp[...] = r.gdisp[...].astype(BF16)
    high, mid, low = split3(jnp.sum(r.up[...].astype(F32) * out, axis=1, keepdims=True))
    lane = iota((CAPP, LANES), 1)
    parts = jnp.where(
        lane == e,
        high,
        jnp.where(lane == e + EXPERTS, mid, jnp.where(lane == e + 2 * EXPERTS, low, 0.0)),
    )
    r.pairs[...] = parts.astype(BF16)

    def image(i, carry):
        beside(i)
        rows = image_rows(i)
        mine = iota((ROWS, LANES), 1) == e
        wanted = jnp.sum(jnp.where(mine, r.pos_col[rows, :], 0.0), axis=1, keepdims=True)
        chosen = jnp.where(wanted == iota((ROWS, CAPP), 1).astype(F32), 1.0, 0.0).astype(BF16)
        r.total[rows, 0:D] += mm(chosen, r.disp[...])
        r.total[rows, D : 2 * D] += mm(chosen, r.gexp[...])
        r.total[rows, 2 * D :] += mm(chosen, r.pairs[...])
        return carry

    lax.fori_loop(0, SLOTS, image, 0)


def norm_backward(i, r):
    rows = image_rows(i)
    lane = iota((ROWS, LANES), 1)
    live = jnp.where(i < r.count[0], 1.0, 0.0)
    residual = r.residual[rows, :]
    r.other_at[i % 2] = ((residual + r.total[rows, 0:D]) * live)[0:SEQ, :].astype(BF16)
    pairs = r.total[rows, 2 * D :]
    gates = r.gates[rows, :]
    grad_gates = (
        pairs + pltpu.roll(pairs, LANES - EXPERTS, 1) + pltpu.roll(pairs, LANES - 2 * EXPERTS, 1)
    )
    grad_gates = jnp.where(lane < EXPERTS, grad_gates, 0.0)
    grad_logits = (
        gates * (grad_gates - jnp.sum(grad_gates * gates, axis=-1, keepdims=True))
    ).astype(BF16)
    r.gvec[8:12, :] += mm_tn(grad_logits, r.wide[rows, 0:D])[0:EXPERTS, :]
    grad_normed2 = r.total[rows, D : 2 * D] + mm(grad_logits, r.router[...])
    scaled2, inverse2 = normalize(residual)
    r.gvec[5:6, :] += jnp.sum(grad_normed2 * scaled2, axis=0, keepdims=True)
    r.gvec[6:7, :] += jnp.sum(grad_normed2, axis=0, keepdims=True)
    grad_residual = r.wide[rows, D : 2 * D].astype(F32) + norm_back(
        grad_normed2, scaled2, inverse2, r.vec[5:6, :]
    )
    r.residual[rows, :] = grad_residual
    grad_attended = grad_residual.astype(BF16)
    r.wide[rows, D : 2 * D] = grad_attended
    r.gvec[4:5, :] += jnp.sum(grad_attended.astype(F32), axis=0, keepdims=True)
    r.wide[rows, 0:D] = mm_nt(grad_attended, r.wout[...].reshape(D, D)).astype(BF16)


def attention_backward(i, r):
    rows = image_rows(i)
    lane = iota((ROWS, LANES), 1)
    for pair in range(HEADS // 2):
        at = pair * LANES
        queries = r.qkv[rows, at : at + LANES]
        keys = r.qkv[rows, D + at : D + at + LANES]
        values = r.qkv[rows, 2 * D + at : 2 * D + at + LANES]
        from_mix = r.wide[rows, at : at + LANES]
        from_both = two_heads(from_mix)
        probs_low = r.probs[i * (HEADS // 2) + pair]
        probs = probs_low.astype(F32)
        weighted = mm_nt(from_both, values) * probs
        grad_scores = (
            weighted - probs * jnp.sum(weighted, axis=-1, keepdims=True)
        ).astype(BF16)
        grad_q = mm(grad_scores, keys)
        scale = HEAD_DIM**-0.5
        joined = jnp.where(lane < HEAD_DIM, grad_q[:ROWS], grad_q[ROWS:])
        r.qkv[rows, at : at + LANES] = (joined * scale).astype(BF16)
        grad_k = mm_tn(grad_scores, two_heads(queries))
        r.qkv[rows, D + at : D + at + LANES] = (grad_k * scale).astype(BF16)
        grad_v = mm_tn(probs_low, from_both)
        r.qkv[rows, 2 * D + at : 2 * D + at + LANES] = grad_v.astype(BF16)
    grads = r.qkv[rows, :]
    r.gvec[2:3, :] += jnp.sum(grads[:, 0:D].astype(F32), axis=0, keepdims=True)
    r.gvec[3:4, :] += jnp.sum(grads[:, 2 * D :].astype(F32), axis=0, keepdims=True)
    grad_normed1 = mm_nt(grads, r.wqkv[...].reshape(D, 3 * D))
    r.xs[0:SEQ, :] = r.image_at[i % 2].astype(F32)
    scaled1, inverse1 = normalize(r.xs[...])
    r.wide[rows, 0:D] = (scaled1 * r.vec[0:1, :] + r.vec[1:2, :]).astype(BF16)
    r.gvec[0:1, :] += jnp.sum(grad_normed1 * scaled1, axis=0, keepdims=True)
    r.gvec[1:2, :] += jnp.sum(grad_normed1, axis=0, keepdims=True)
    grad_in = r.residual[rows, :] + norm_back(grad_normed1, scaled1, inverse1, r.vec[0:1, :])
    r.grad_at[i % 2] = grad_in[0:SEQ, :].astype(BF16)


def wout_grad(r):
    r.wout[...] = mm_tn(r.mix[...], r.wide[:, D : 2 * D]).astype(BF16).reshape(r.wout.shape)


def wqkv_grad(part, r):
    width = 3 * D // QKV_PARTS
    cols = slice(part * width, (part + 1) * width)
    grad = mm_tn(r.wide[:, 0:D], r.qkv[:, cols]).astype(BF16)
    r.wqkv[:, :, :, :, :, cols] = grad.reshape(r.wqkv.shape[:5] + (width,))


def spread_router(r):
    r.router[...] = jnp.zeros_like(r.router)
    first = r.vec[8:16, :]
    r.router[0:16, :] = jnp.concatenate(
        [jnp.where(iota((8, D), 0) < EXPERTS, first, 0.0), jnp.zeros((8, D), F32)], axis=0
    ).astype(BF16)


def pattern(shape, match):
    return jnp.where(match(iota(shape, 0), iota(shape, 1)), 1.0, 0.0).astype(BF16)


def all_vectors(r):
    packs = r.small[...].reshape(GROUP * 8, LANES).astype(BF16)
    line, column = iota((GROUP * 8, D), 0), iota((GROUP * 8, D), 1)

    def row(match, line_of):
        spread = mm(packs, pattern((LANES, D), match))
        return lambda: jnp.sum(jnp.where(line == line_of, spread, 0.0), axis=0, keepdims=True)

    sixteenth = 8 * (column >> 4)
    for index, start in ((0, 0), (1, 16), (4, 64), (5, 80), (6, 96)):
        r.vec[index : index + 1, :] = row(lambda j, c: j == start + (c & 15), sixteenth)()
    for index in range(2):
        r.vec[2 + index : 3 + index, :] = row(
            lambda j, c: j == 32 + (c & 31), 8 * (16 * index + (column >> 5))
        )()
    r.vec[7:8, :] = jnp.zeros((1, D), F32)
    for e in range(EXPERTS):
        r.vec[8 + e : 9 + e, :] = row(lambda j, c: j == 4 * (c & 15) + e, sixteenth + 1)()
        r.vec[12 + e : 13 + e, :] = row(
            lambda j, c: j == 64 + (c & 63), 8 * (8 * e + (column >> 6)) + 1
        )()
    for device in range(GROUP):
        at = (device // 8, device // 4 % 2, device // 2 % 2, device % 2)
        for line_of in range(2):
            start = device % 2 * 256 + line_of * LANES
            r.vec[16 + device // 2 : 17 + device // 2, start : start + LANES] = r.small[
                at + (slice(2 + line_of, 3 + line_of), FULL)
            ]


def own_vectors(me, r):
    row, column = iota((8, D), 0), iota((8, D), 1)
    lane, line = iota((8, LANES), 1), iota((8, LANES), 0)

    def fold(values, match):
        parts = [v.astype(BF16) for v in split3(values)]
        chosen = pattern((D, LANES), match)
        return sum(mm(v, chosen) for v in parts)

    owner = jnp.where(
        row == 2, column >> 5, jnp.where(row == 3, 16 + (column >> 5), column >> 4)
    )
    top = jnp.where(owner == me, r.gvec[0:8, :], 0.0)
    by16 = fold(top, lambda c, j: (c & 15) == j)
    by32 = fold(top, lambda c, j: (c & 31) == j)
    for name, index in dict(ln1_gain=0, ln1_bias=1, b_out=4, ln2_gain=5, ln2_bias=6).items():
        getattr(r, "out_" + name)[...] = by16[index : index + 1, 0:16]
    r.out_b_qv[...] = by32[2:3, 0:32] + by32[3:4, 0:32]
    owner = jnp.where(row < 4, column >> 4, 8 * (row - 4) + (column >> 6))
    low = jnp.where(owner == me, r.gvec[8:16, :], 0.0)
    router = jnp.where((lane & 3) == line, fold(low, lambda c, j: (c & 15) == (j >> 2)), 0.0)
    r.out_w_router[...] = jnp.sum(jnp.where(line < 4, router, 0.0), axis=0, keepdims=True)[:, 0:64]
    back = jnp.where(line < 4, 0.0, fold(low, lambda c, j: (c & 63) == j))
    r.out_b_back[...] = jnp.sum(back, axis=0, keepdims=True)[:, 0:64]
    row, column = iota((16, D), 0), iota((16, D), 1)
    bias = jnp.where(2 * row + (column >> 8) == me, r.gvec[16:32, :], 0.0)
    bias = jnp.sum(bias, axis=0, keepdims=True)
    r.out_b_in[...] = bias[:, 0:256] + bias[:, 256:512]


class Place:
    def __init__(self):
        me = lax.axis_index("dev")
        self.me, self.c, self.x, self.y, self.z = me, me % 2, me // 2 % 2, me // 4 % 2, me // 8
        self.core = self.device(self.z, self.y, self.x, 1 - self.c)
        self.over_y = self.device(self.z, 1 - self.y, self.x, self.c)
        self.over_x = self.device(self.z, self.y, 1 - self.x, self.c)

    def device(self, z, y, x, c):
        return ((z * 2 + y) * 2 + x) * 2 + c

    def plane(self, k):
        return lax.rem(self.z + k + EXPERTS, EXPERTS)

    def above(self, k):
        return self.device(self.plane(k), self.y, self.x, self.c)

    def greet(self):
        barrier = pltpu.get_barrier_semaphore()
        friends = [self.above(k) for k in range(1, EXPERTS)]
        friends += [self.core, self.over_y, self.over_x]
        for friend in friends:
            pl.semaphore_signal(barrier, inc=1, device_id=(friend,), device_id_type=MESH)
        pl.semaphore_wait(barrier, len(friends))

    def first(self, route):
        return self.over_y if route == 0 else self.over_x

    def second(self, route):
        return self.over_x if route == 0 else self.over_y


class Copies:
    def __init__(self, sems, index):
        self.sems, self.index = sems, index

    def make(self, slot, source, target, device):
        send_sem, recv_sem = self.sems
        return pltpu.make_async_remote_copy(
            src_ref=source, dst_ref=target, send_sem=send_sem.at[self.index, slot],
            recv_sem=recv_sem.at[self.index, slot], device_id=(device,), device_id_type=MESH,
        )


class SumAll(Copies):
    def __init__(self, sems, index, values, landing, place):
        super().__init__(sems, index)
        self.values, self.landing, self.p = values, landing, place

    def stage(self, step):
        p = self.p
        targets = [
            [(k, p.above(k)) for k in range(1, EXPERTS)], [(4, p.over_y)], [(5, p.over_x)],
            [(6, p.core)],
        ][step]
        return [self.make(s, self.values, self.landing.at[s - 1], d) for s, d in targets]

    def begin(self, step):
        for copy in self.stage(step):
            copy.start()

    def end(self, step):
        for copy in self.stage(step):
            copy.wait()
        if step == 0:
            self.values[...] += self.landing[0] + self.landing[1] + self.landing[2]
        else:
            self.values[...] += self.landing[2 + step]


class Gather(Copies):
    def __init__(self, sems, index, shard, full, tail, route, k, place):
        super().__init__(sems, index)
        self.shard, self.full, self.tail, self.route, self.p = shard, full, tail, route, place
        self.k = k

    def at(self, lead, y, x, c):
        return self.full.at[(lead, y, x, c) + self.tail]

    def own(self):
        return self.shard.at[self.tail] if self.tail else self.shard

    def local(self, sem):
        p = self.p
        lead = p.z if self.k is None else 0
        return pltpu.make_async_copy(self.own(), self.at(lead, p.y, p.x, p.c), sem)

    def along_z(self, arriving):
        p = self.p
        if self.k is None:
            return [
                self.make(k, self.own(), self.at(p.plane(-k) if arriving else p.z, p.y, p.x, p.c),
                          p.above(k))
                for k in range(1, EXPERTS)
            ]
        if self.k == 0:
            return []
        return [self.make(1, self.own(), self.at(self.k, p.y, p.x, p.c), p.above(-self.k))]

    def lead(self):
        return FULL if self.k is None else self.k

    def across(self, step, arriving):
        p = self.p
        y, x = p.y, p.x
        if step == 0:
            if arriving:
                y, x = (1 - y, x) if self.route == 0 else (y, 1 - x)
            device = p.first(self.route)
        else:
            if arriving:
                y, x = 1 - y, 1 - x
            y, x = (FULL, x) if self.route == 0 else (y, FULL)
            device = p.second(self.route)
        block = self.at(self.lead(), y, x, p.c)
        return self.make(4 + step, block, block, device)

    def to_core(self, step, arriving):
        p = self.p
        y, x = p.y, p.x
        if step == 1:
            y, x = (1 - y, x) if self.route == 0 else (y, 1 - x)
        elif step == 2:
            y, x = (FULL, 1 - x) if self.route == 0 else (1 - y, FULL)
        block = self.at(self.lead(), y, x, 1 - p.c if arriving else p.c)
        return self.make(6 + step, block, block, p.core)

    def start_z(self):
        for copy in self.along_z(False):
            copy.start()

    def stage(self, step):
        if step == 0:
            for copy in self.along_z(True):
                copy.wait_recv()
        else:
            self.across(step - 1, True).wait_recv()
        if step < 2:
            self.across(step, False).start()
        self.to_core(step, False).start()

    def finish(self):
        for step in range(3):
            self.to_core(step, True).wait_recv()
        for copy in self.along_z(False):
            copy.wait_send()
        for step in range(2):
            self.across(step, False).wait_send()
        for step in range(3):
            self.to_core(step, False).wait_send()


class Scatter(Copies):
    def __init__(self, sems, index, full, landing, out, tail, route, k, place):
        super().__init__(sems, index)
        self.full, self.out, self.tail, self.route, self.p, self.k = (
            full, out, tail, route, place, k,
        )
        self.from_core, self.from_first, self.from_second, self.from_z = landing

    def lead(self):
        return FULL if self.k is None else self.k

    def landed(self, ref, spare):
        if self.k is None:
            return (FULL,) * (1 + spare) + self.tail
        return (self.k % ref.shape[0],) + (FULL,) * spare + self.tail

    def to_core(self):
        p = self.p
        return self.make(0, self.full.at[(self.lead(), FULL, FULL, 1 - p.c) + self.tail],
                         self.from_core.at[self.landed(self.from_core, 2)], p.core)

    def to_first(self):
        p = self.p
        y, x = (FULL, 1 - p.x) if self.route == 0 else (1 - p.y, FULL)
        return self.make(1, self.full.at[(self.lead(), y, x, p.c) + self.tail],
                         self.from_first.at[self.landed(self.from_first, 1)],
                         p.second(self.route))

    def to_second(self):
        p = self.p
        y, x = (1 - p.y, p.x) if self.route == 0 else (p.y, 1 - p.x)
        return self.make(2, self.full.at[(self.lead(), y, x, p.c) + self.tail],
                         self.from_second.at[self.landed(self.from_second, 0)],
                         p.first(self.route))

    def along_z(self):
        p = self.p
        steps = range(1, EXPERTS) if self.k is None else ([self.k] if self.k else [])
        return [
            self.make(2 + k, self.full.at[(p.plane(k) if self.k is None else k, p.y, p.x, p.c) + self.tail],
                      self.from_z.at[(k - 1,) + self.tail], p.above(k))
            for k in steps
        ]

    def add(self, mine, landed):
        def layer(k, carry):
            for at, source in zip(mine(k), landed(k)):
                self.full[at + self.tail] = self.full[at + self.tail] + source
            return carry

        if self.k is None:
            lax.fori_loop(0, EXPERTS, layer, 0)
        else:
            layer(self.k, 0)

    def slot(self, ref, k):
        return k if self.k is None else k % ref.shape[0]

    def stage(self, step):
        p, tail = self.p, self.tail
        if step == 0:
            self.to_core().start()
        elif step == 1:
            self.to_core().wait_recv()
            spots = [(y, x) for y in range(2) for x in range(2)]
            ref = self.from_core
            self.add(lambda k: [(k, y, x, p.c) for y, x in spots],
                     lambda k: [ref[(self.slot(ref, k), y, x) + tail] for y, x in spots])
            self.to_first().start()
        elif step == 2:
            self.to_first().wait_recv()
            ref = self.from_first
            self.add(lambda k: [(k, o, p.x, p.c) if self.route == 0 else (k, p.y, o, p.c) for o in range(2)],
                     lambda k: [ref[(self.slot(ref, k), o) + tail] for o in range(2)])
            self.to_second().start()
        else:
            self.to_second().wait_recv()
            ref = self.from_second
            self.add(lambda k: [(k, p.y, p.x, p.c)],
                     lambda k: [ref[(self.slot(ref, k),) + tail]])
            for copy in self.along_z():
                copy.start()

    def collect(self):
        p, tail = self.p, self.tail
        total = self.full[((p.z if self.k is None else 0), p.y, p.x, p.c) + tail].astype(F32)
        for k in range(EXPERTS - 1):
            total = total + self.from_z[(k,) + tail].astype(F32)
        rows, columns = total.shape
        height, width = self.full.shape[-2:]
        first_row, first_column = tail[0].start or 0, tail[1].start or 0
        step = width // LANES
        for j in range(columns // LANES):
            line = first_row * step + first_column // LANES + j
            self.out[pl.ds(line, rows, stride=step), :] = total[:, j * LANES : (j + 1) * LANES]

    def drain(self):
        self.to_core().wait_send()
        self.to_first().wait_send()
        self.to_second().wait_send()
        for copy in self.along_z():
            copy.wait_send()


class Refs:
    def __init__(self, names, refs):
        for name, ref in zip(names, refs, strict=True):
            setattr(self, name, ref)


SCRATCH = dict(
    image_at=((2, SEQ, D), BF16),
    other_at=((2, SEQ, D), BF16),
    grad_at=((2, SEQ, D), BF16),
    xs=((ROWS, D), F32),
    router=((LANES, D), BF16),
    qkv=((TOK, 3 * D), BF16),
    probs=((SLOTS * HEADS // 2, 2 * ROWS, ROWS), BF16),
    mix=((TOK, D), BF16),
    residual=((TOK, D), F32),
    wide=((TOK, WIDE), BF16),
    gates=((TOK, LANES), F32),
    pos_col=((TOK, LANES), F32),
    pos_row=((8, TOK), F32),
    disp=((CAPP, D), BF16),
    up=((CAPP, D), BF16),
    gexp=((CAPP, D), BF16),
    gate_slot=((CAPP, LANES), F32),
    pairs=((CAPP, LANES), BF16),
    eo=((CAPP, D), F32),
    gdisp=((CAPP, D), F32),
    total=((TOK, WIDE), F32),
    wqkv=((EXPERTS, 2, 2, 2, 16, 3 * D), BF16),
    wout=((EXPERTS, 2, 2, 2, 16, D), BF16),
    win=((EXPERTS, 2, 2, 2, BLOCK_IN, HID), BF16),
    wback=((EXPERTS, 2, 2, 2, BLOCK_BACK, D), BF16),
)
SHARDS = dict(wqkv=(16, 3 * D), wout=(16, D), win=(BLOCK_IN, HID), wback=(BLOCK_BACK, D))


def columns_of(width, h, parts=2):
    return (FULL, slice(h * width // parts, (h + 1) * width // parts))


def rows_of(height, h):
    return (slice(h * height // 2, (h + 1) * height // 2), FULL)


SMALL = dict(
    ln1_gain=16, ln1_bias=16, b_qv=32, b_out=16, ln2_gain=16, ln2_bias=16, w_router=64, b_in=256,
    b_back=64,
)
FLAT_PIECES = [("wqkv", columns_of(3 * D, h, QKV_PARTS), h % 2) for h in range(QKV_PARTS)]
FLAT_PIECES += [("wout", columns_of(D, h), h) for h in range(2)]
FLAT_PIECES += [("small", (), 0)]
EXPERT_PIECES = [("win", rows_of(BLOCK_IN, h), h) for h in range(2)]
EXPERT_PIECES += [("wback", rows_of(BLOCK_BACK, h), h) for h in range(2)]
LANDING = {}
for name in ("wqkv", "wout"):
    for part, lead in dict(core=(4, 2, 2), first=(4, 2), second=(4,), z=(3,)).items():
        LANDING[name, part] = (lead + SHARDS[name], BF16)
for name in ("win", "wback"):
    for part, lead in dict(core=(2, 2, 2), first=(4, 2), second=(4,), z=(3,)).items():
        LANDING[name, part] = (lead + SHARDS[name], BF16)
INPUTS = ["count", "images", "cotangent", "routes", "order"]


def whole_kernel(*refs):
    names = INPUTS + ["shard_small"] + ["shard_" + n for n in SHARDS]
    names += ["blocks", "gimages"] + ["out_" + n for n in SHARDS] + ["out_" + n for n in SMALL]
    names += list(SCRATCH) + ["vec", "gvec", "small", "land_gvec"]
    names += ["land_" + "_".join(key) for key in LANDING]
    names += ["local_sem", "vec_send", "vec_recv", "get_send", "get_recv", "put_send", "put_recv"]
    names += ["free_sem", "in_sem", "out_sem"]
    r = Refs(names, refs)
    p = Place()
    p.greet()

    def landing(name):
        return [getattr(r, f"land_{name}_{part}") for part in ("core", "first", "second", "z")]

    get_sems, put_sems = (r.get_send, r.get_recv), (r.put_send, r.put_recv)
    flat_get, flat_put = [], []
    for index, (name, tail, route) in enumerate(FLAT_PIECES):
        flat_get.append(
            Gather(get_sems, index, getattr(r, "shard_" + name), getattr(r, name), tail, route, None, p)
        )
        if name != "small":
            flat_put.append(
                Scatter(put_sems, index, getattr(r, name), landing(name), getattr(r, "out_" + name),
                        tail, route, None, p)
            )
    get, put = [], []
    for k in range(EXPERTS):
        get.append([])
        put.append([])
        for index, (name, tail, route) in enumerate(EXPERT_PIECES):
            index += len(FLAT_PIECES) + k * len(EXPERT_PIECES)
            get[k].append(
                Gather(get_sems, index, getattr(r, "shard_" + name), getattr(r, name), tail, route, k, p)
            )
            put[k].append(
                Scatter(put_sems, index, getattr(r, name), landing(name), getattr(r, "out_" + name),
                        tail, route, k, p)
            )

    def part(pieces, which):
        return pieces if which is None else pieces[2 * which : 2 * which + 2]

    def gather_stage(k, step, which=None):
        for piece in part(get[k], which):
            piece.start_z() if step < 0 else piece.stage(step)

    def scatter_stage(k, step, which=None):
        if step == 0 and k >= 2 and which != 1:
            pl.semaphore_wait(r.free_sem, 1)
        for piece in part(put[k], which):
            piece.stage(step)
        if step == 1 and k < 2 and which != 0:
            pl.semaphore_signal(r.free_sem, inc=1, device_id=(p.core,), device_id_type=MESH)

    def wout_stage(step):
        for piece in flat_put[QKV_PARTS:]:
            piece.stage(step)

    events = {
        ("start",): [("get", 0, 0, 1), ("get", 0, 1, 1)],
        ("flat", 0): [("get", 3, -1, 0)],
        ("flat", 1): [("get", 3, 0, 0), ("get", 1, -1, 0)],
        ("flat", 2): [("get", 1, -1, 1), ("get", 0, 0, 0), ("get", 3, 1, 0), ("get", 0, 2, 1), ("get", 2, -1, 0)],
        ("forward", 0): [("get", 0, 1, 0)],
        ("forward", 2): [("get", 1, 0, 0)],
        ("forward", 4): [("get", 1, 0, 1)],
        ("dispatch", 0, 0): [("get", 0, 2, 0)],
        ("dispatch", 0, 2): [("get", 2, -1, 1)],
        ("dispatch", 0, 3): [("get", 1, 1, 0)],
        ("dispatch", 0, 4): [("get", 3, 2, 0)],
        ("expert", 0, 3): [("get", 1, 1, 1)],
        ("expert", 0, 7): [("get", 1, 2, 0)],
        ("combine", 0, 2): [("get", 2, 0, 0), ("get", 1, 2, 1), ("get", 3, -1, 1)],
        ("combine", 0, 3): [("get", 2, 0, 1)],
        ("combine", 0, 4): [("put", 0, 0, 0)],
        ("dispatch", 1, 4): [("get", 2, 1, 0)],
        ("expert", 1, 3): [("put", 0, 0, 1)],
        ("expert", 1, 5): [("get", 3, 0, 1)],
        ("expert", 1, 6): [("get", 2, 2, 0)],
        ("expert", 1, 7): [("get", 2, 1, 1)],
        ("combine", 1, 0): [("put", 1, 0, 0)],
        ("combine", 1, 3): [("get", 3, 1, 1)],
        ("dispatch", 2, 1): [("get", 2, 2, 1), ("put", 0, 1, 0)],
        ("dispatch", 2, 4): [("put", 1, 0, 1), ("put", 1, 1, 0)],
        ("expert", 2, 6): [("put", 0, 1, 1)],
        ("expert", 2, 7): [("get", 3, 2, 1)],
        ("combine", 2, 2): [("put", 2, 0, 0)],
        ("combine", 2, 4): [("put", 0, 2, 0)],
        ("dispatch", 3, 0): [("put", 1, 2, 0)],
        ("dispatch", 3, 3): [("put", 2, 0, 1)],
        ("expert", 3, 0): [("put", 2, 1, 0)],
        ("expert", 3, 3): [("put", 1, 3, 0)],
        ("expert", 3, 4): [("put", 2, 1, 1)],
        ("expert", 3, 6): [("put", 0, 3, 0)],
        ("expert", 3, 7): [("put", 2, 2, 0)],
        ("combine", 3, 1): [("put", 1, 1, 1)],
        ("combine", 3, 3): [("put", 3, 0, 0)],
        ("norms", 0): [("put", 2, 3, 0)],
        ("norms", 1): [("put", 2, 2, 1)],
        ("norms", 2): [("put", 3, 1, 0)],
        ("norms", 3): [("put", 0, 2, 1)],
        ("backward", 0): [("put", 2, 3, 1)],
        ("backward", 1): [("put", 3, 0, 1), ("out", 1), ("put", 1, 2, 1)],
        ("backward", 2): [("put", 3, 2, 0)],
        ("backward", 3): [("out", 2)],
        ("backward", 4): [("put", 3, 1, 1), ("put", 1, 3, 1)],
        ("tail", 0): [("out", 3)],
        ("tail", 2): [("put", 3, 3, 0)],
        ("tail", 3): [("put", 3, 2, 1), ("put", 0, 3, 1)],
        ("tail", 4): [("put", 3, 3, 1)],
    }

    def beside(*key):
        def at(step):
            for (*found, when), todo in events.items():
                if tuple(found) == key:
                    pl.when(step == when)(functools.partial(act, todo))

        return at

    def act(todo):
        for kind, *what in todo:
            dict(get=gather_stage, put=scatter_stage, out=wout_stage)[kind](*what)

    def fetch(i, both):
        copies = [pltpu.make_async_copy(r.images.at[i], r.image_at.at[i % 2], r.in_sem.at[0, i % 2])]
        if both:
            copies.append(
                pltpu.make_async_copy(r.cotangent.at[i], r.other_at.at[i % 2], r.in_sem.at[1, i % 2])
            )
        return copies

    def emit_block(i):
        return [pltpu.make_async_copy(r.other_at.at[i % 2], r.blocks.at[i], r.out_sem.at[0, i % 2])]

    def emit_grad(i):
        return [pltpu.make_async_copy(r.grad_at.at[i % 2], r.gimages.at[i], r.out_sem.at[1, i % 2])]

    def start(copies):
        for copy in copies:
            copy.start()

    def wait(copies):
        for copy in copies:
            copy.wait()

    start(fetch(0, True))
    local = []
    for index, piece in enumerate(flat_get + get[0]):
        copy = piece.local(r.local_sem.at[index])
        copy.start()
        local.append(copy)
    for piece in flat_get:
        piece.start_z()
    for copy in local:
        copy.wait()
    act(events.get(("start",), ()))
    r.xs[...] = jnp.zeros_like(r.xs)
    r.gvec[...] = jnp.zeros_like(r.gvec)
    r.total[...] = jnp.zeros_like(r.total)
    for step in range(3):
        for piece in flat_get:
            piece.stage(step)
        if step == 0:
            routing(r)
        act(events.get(("flat", step), ()))
    for piece in flat_get:
        piece.finish()
    act(events.get(("flat", 3), ()))
    all_vectors(r)
    spread_router(r)

    def forward(i, carry):
        @pl.when(i + 1 < SLOTS)
        def _():
            start(fetch(i + 1, True))

        wait(fetch(i, True))
        attention_forward(i, r)
        beside("forward")(i)
        return carry

    lax.fori_loop(0, SLOTS, forward, 0)
    for k in range(EXPERTS):
        e = p.plane(k)
        dispatch(e, r, beside("dispatch", k))
        for piece in get[k]:
            piece.finish()

        def step(f, carry):
            beside("expert", k)(2 * f)
            beside("expert", k)(2 * f + 1)
            expert_step(e, f, k, r)
            return carry

        lax.fori_loop(0, HID // FT, step, 0)
        combine(e, r, beside("combine", k))
    start(fetch(0, False))

    def norms(i, carry):
        @pl.when(i >= 2)
        def _():
            wait(emit_block(i - 2))

        norm_backward(i, r)
        start(emit_block(i))
        beside("norms")(i)
        return carry

    lax.fori_loop(0, SLOTS, norms, 0)
    wout_grad(r)
    wqkv_put, wout_put = flat_put[:QKV_PARTS], flat_put[QKV_PARTS:]
    for piece in wout_put:
        piece.stage(0)

    def backward(i, carry):
        @pl.when(i + 1 < SLOTS)
        def _():
            start(fetch(i + 1, False))

        wait(fetch(i, False))

        @pl.when(i >= 2)
        def _():
            wait(emit_grad(i - 2))

        attention_backward(i, r)
        start(emit_grad(i))
        beside("backward")(i)
        return carry

    lax.fori_loop(0, SLOTS, backward, 0)
    sums = SumAll((r.vec_send, r.vec_recv), 0, r.gvec, r.land_gvec, p)
    sums.begin(0)
    for part_of in range(QKV_PARTS):
        wqkv_grad(part_of, r)
        wqkv_put[part_of].stage(0)
        if part_of % 2:
            act(events.get(("tail", part_of // 2), ()))
    for step in range(1, 4):
        sums.end(step - 1)
        sums.begin(step)
        for piece in wqkv_put:
            piece.stage(step)
        act(events.get(("tail", step + 1), ()))
    for k in range(1, EXPERTS):
        for piece in put[k]:
            for copy in piece.along_z():
                copy.wait_recv()
    for piece in put[0]:
        piece.collect()
    for piece in wout_put:
        for copy in piece.along_z():
            copy.wait_recv()
        piece.collect()
    sums.end(3)
    own_vectors(p.me, r)
    for piece in wqkv_put:
        for copy in piece.along_z():
            copy.wait_recv()
        piece.collect()
    for pieces in put + [flat_put]:
        for piece in pieces:
            piece.drain()
    for i in range(SLOTS - 2, SLOTS):
        wait(emit_block(i))
        wait(emit_grad(i))


def alone_kernel(*refs):
    names = INPUTS + ["pack"] + ["full_" + n for n in SHARDS]
    names += ["blocks", "gimages", "gvec"] + ["out_" + n for n in SHARDS]
    names += list(SCRATCH) + ["vec", "sem"]
    r = Refs(names, refs)

    def move(source, target):
        copy = pltpu.make_async_copy(source, target, r.sem)
        copy.start()
        copy.wait()

    for name in SHARDS:
        move(getattr(r, "full_" + name), getattr(r, name))
    r.vec[...] = r.pack[...]
    r.xs[...] = jnp.zeros_like(r.xs)
    r.gvec[...] = jnp.zeros_like(r.gvec)
    r.total[...] = jnp.zeros_like(r.total)
    spread_router(r)
    routing(r)

    def forward(i, carry):
        move(r.images.at[i], r.image_at.at[i % 2])
        move(r.cotangent.at[i], r.other_at.at[i % 2])
        attention_forward(i, r)
        return carry

    def expert(e, carry):
        dispatch(e, r)
        lax.fori_loop(0, HID // FT, lambda f, c: (expert_step(e, f, e, r), c)[1], 0)
        combine(e, r)
        return carry

    def norms(i, carry):
        norm_backward(i, r)
        move(r.other_at.at[i % 2], r.blocks.at[i])
        return carry

    def backward(i, carry):
        move(r.images.at[i], r.image_at.at[i % 2])
        attention_backward(i, r)
        move(r.grad_at.at[i % 2], r.gimages.at[i])
        return carry

    lax.fori_loop(0, SLOTS, forward, 0)
    lax.fori_loop(0, EXPERTS, expert, 0)
    lax.fori_loop(0, SLOTS, norms, 0)
    wout_grad(r)
    lax.fori_loop(0, SLOTS, backward, 0)
    for part in range(QKV_PARTS):
        wqkv_grad(part, r)
    for name in SHARDS:
        move(getattr(r, name), getattr(r, "out_" + name))


def alone(inputs, pack, full):
    vmem = pl.BlockSpec(memory_space=pltpu.VMEM)
    hbm = pl.BlockSpec(memory_space=pltpu.HBM)
    smem = pl.BlockSpec(memory_space=pltpu.SMEM)
    shapes = [((SLOTS, SEQ, D), BF16), ((SLOTS, SEQ, D), BF16), ((32, D), F32)]
    shapes += [SCRATCH[name] for name in SHARDS]
    return pl.pallas_call(
        alone_kernel,
        out_shape=[jax.ShapeDtypeStruct(*s) for s in shapes],
        in_specs=[smem] + [hbm] * 2 + [vmem] * 3 + [hbm] * 4,
        out_specs=[hbm] * 2 + [vmem] + [hbm] * 4,
        scratch_shapes=[pltpu.VMEM(*s) for s in SCRATCH.values()]
        + [pltpu.VMEM((32, D), F32), pltpu.SemaphoreType.DMA],
        compiler_params=pltpu.CompilerParams(vmem_limit_bytes=VMEM_LIMIT),
    )(*inputs, pack, *full)


def whole(inputs, pack, shards):
    vmem = pl.BlockSpec(memory_space=pltpu.VMEM)
    hbm = pl.BlockSpec(memory_space=pltpu.HBM)
    smem = pl.BlockSpec(memory_space=pltpu.SMEM)
    shapes = [((SLOTS, SEQ, D), BF16), ((SLOTS, SEQ, D), BF16)]
    shapes += [((rows * columns // LANES, LANES), F32) for rows, columns in SHARDS.values()]
    shapes += [((1, size), F32) for size in SMALL.values()]
    count = len(FLAT_PIECES) + EXPERTS * len(EXPERT_PIECES)
    dma = pltpu.SemaphoreType.DMA
    return pl.pallas_call(
        whole_kernel,
        out_shape=[jax.ShapeDtypeStruct(*s) for s in shapes],
        in_specs=[smem] + [hbm] * 2 + [vmem] * 2 + [hbm] * 5,
        out_specs=[hbm] * 2 + [vmem] * (len(shapes) - 2),
        scratch_shapes=[pltpu.VMEM(*s) for s in SCRATCH.values()]
        + [pltpu.VMEM((32, D), F32)] * 2
        + [pltpu.VMEM((EXPERTS, 2, 2, 2, 8, LANES), F32), pltpu.VMEM((6, 32, D), F32)]
        + [pltpu.VMEM(*s) for s in LANDING.values()]
        + [dma((len(FLAT_PIECES) + len(EXPERT_PIECES),)), dma((1, 7)), dma((1, 7))]
        + [dma((count, 9)), dma((count, 9)), dma((count, 6)), dma((count, 6))]
        + [pltpu.SemaphoreType.REGULAR, dma((2, 2)), dma((2, 2))],
        compiler_params=pltpu.CompilerParams(
            collective_id=0, has_side_effects=True, vmem_limit_bytes=VMEM_LIMIT
        ),
        cost_estimate=pl.CostEstimate(
            flops=40 * 10**9, bytes_accessed=50 * 10**6, transcendentals=10**7
        ),
    )(*inputs, pack, *shards)


def per_device(
    images, cotangent, routes, priority, image_count,
    ln1_gain, ln1_bias, w_qkv, b_qv, w_out, b_out, ln2_gain, ln2_bias,
    w_router, w_in, b_in, w_back, b_back,
):
    inputs = (image_count, images, cotangent, routes.T, priority)
    if lax.axis_size("dev") != GROUP:
        return with_collectives(
            inputs, ln1_gain, ln1_bias, w_qkv, b_qv, w_out, b_out, ln2_gain, ln2_bias,
            w_router, w_in, b_in, w_back, b_back,
        )
    small = [ln1_gain, ln1_bias, b_qv, b_out, ln2_gain, ln2_bias, None, w_router, b_back, b_in]
    pack, at = 0.0, 0
    for v in small:
        size = 16 if v is None else v.shape[0]
        if v is not None:
            pack = pack + jnp.pad(v.astype(F32), (at, 8 * LANES - at - size))
        at += size
    shards = [v.reshape(s) for v, s in zip((w_qkv, w_out, w_in, w_back), SHARDS.values())]
    blocks, gimages, *grads = whole(inputs, pack.reshape(8, LANES), shards)
    grads = dict(zip(["w_qkv", "w_out", "w_in", "w_back"] + list(SMALL), grads))
    order = ["ln1_gain", "ln1_bias", "w_qkv", "b_qv", "w_out", "b_out", "ln2_gain", "ln2_bias"]
    order += ["w_router", "w_in", "b_in", "w_back", "b_back"]
    return (blocks, gimages) + tuple(grads[name].reshape(-1) for name in order)


def with_collectives(
    inputs, ln1_gain, ln1_bias, w_qkv, b_qv, w_out, b_out, ln2_gain, ln2_bias,
    w_router, w_in, b_in, w_back, b_back,
):
    gather = lambda v: lax.all_gather(v, "dev", axis=0, tiled=True)
    scatter = lambda v: lax.psum_scatter(
        v.astype(F32).reshape(-1), "dev", scatter_dimension=0, tiled=True
    )
    row = lambda v: gather(v).astype(F32).reshape(-1, D)
    zero = jnp.zeros((1, D), F32)
    pack = jnp.concatenate(
        [row(ln1_gain), row(ln1_bias), row(b_qv), row(b_out), row(ln2_gain), row(ln2_bias), zero,
         gather(w_router).astype(F32).reshape(D, EXPERTS).T, row(b_back), row(b_in)]
    )
    full = [
        gather(v).reshape(SCRATCH[name][0]) for v, name in zip((w_qkv, w_out, w_in, w_back), SHARDS)
    ]
    blocks, gimages, gvec, gwqkv, gwout, gwin, gwback = alone(inputs, pack, full)
    return (
        blocks, gimages, scatter(gvec[0]), scatter(gvec[1]), scatter(gwqkv), scatter(gvec[2:4]),
        scatter(gwout), scatter(gvec[4]), scatter(gvec[5]), scatter(gvec[6]),
        scatter(gvec[8:12].T), scatter(gwin), scatter(gvec[16:32]), scatter(gwback),
        scatter(gvec[12:16]),
    )


def solution(mesh):
    split = P("dev")
    return jax.shard_map(
        per_device, mesh=mesh, in_specs=(split,) * 18, out_specs=(split,) * 15, check_vma=False
    )
```

```python
import functools

import jax
import jax.numpy as jnp
from jax import lax
from jax.experimental import pallas as pl
from jax.experimental.pallas import tpu as pltpu
from jax.sharding import PartitionSpec as P

D = 512
HEADS = 8
HID = 2048
EXPERTS = 4
SEQ = 197
SLOTS = 5
HEAD_DIM = 64
CAP = 555
EPSILON = 1e-06

ROWS = -(-SEQ // 16) * 16
TOK = SLOTS * ROWS
CAPP = -(-CAP // 16) * 16
LANES = 128
WIDE = 2 * D + LANES
GROUP = EXPERTS * 2 * 2 * 2
BLOCK_IN = EXPERTS * D // GROUP
BLOCK_BACK = EXPERTS * HID // GROUP
SLOT_TILE = CAPP // 5
FT = 512
QKV_PARTS = 4
VMEM_LIMIT = 65000 * 1024
MESH = pl.DeviceIdType.MESH
FULL = slice(None)
F32 = jnp.float32
BF16 = jnp.bfloat16


def mm(a, b):
    return lax.dot_general(a, b, (((1,), (0,)), ((), ())), preferred_element_type=F32)


def mm_nt(a, b):
    return lax.dot_general(a, b, (((1,), (1,)), ((), ())), preferred_element_type=F32)


def mm_tn(a, b):
    return lax.dot_general(a, b, (((0,), (0,)), ((), ())), preferred_element_type=F32)


def iota(shape, dim):
    return lax.broadcasted_iota(jnp.int32, shape, dim)


def normalize(inputs):
    centre = inputs - jnp.mean(inputs, axis=-1, keepdims=True)
    inverse = lax.rsqrt(jnp.mean(centre * centre, axis=-1, keepdims=True) + EPSILON)
    return centre * inverse, inverse


def norm_back(grad_normed, scaled, inverse, gain):
    grad_scaled = grad_normed * gain
    return inverse * (
        grad_scaled
        - jnp.mean(grad_scaled, axis=-1, keepdims=True)
        - scaled * jnp.mean(grad_scaled * scaled, axis=-1, keepdims=True)
    )


def gelu_parts(pre):
    size = jnp.abs(pre)
    t = 1.0 / (1.0 + (0.3275911 * 0.7071067811865476) * size)
    bell = jnp.exp(-0.5 * (pre * pre))
    poly = t * (
        0.127414796
        + t * (-0.142248368 + t * (0.7107068705 + t * (-0.7265760135 + t * 0.5307027145)))
    )
    tail = poly * bell
    phi = jnp.where(pre >= 0, 1.0 - tail, tail)
    return pre * phi, phi + pre * (bell * 0.3989422804014327)


def split3(value):
    high = value.astype(BF16).astype(F32)
    rest = value - high
    mid = rest.astype(BF16).astype(F32)
    return high, mid, rest - mid


def image_rows(i):
    return pl.ds(i * ROWS if isinstance(i, int) else pl.multiple_of(i * ROWS, 16), ROWS)


def two_heads(block):
    first = iota(block.shape, 1) < HEAD_DIM
    zero = jnp.zeros_like(block)
    return jnp.concatenate([jnp.where(first, block, zero), jnp.where(first, zero, block)], axis=0)


def attention_forward(i, r):
    rows = image_rows(i)
    r.xs[0:SEQ, :] = r.image_at[i % 2].astype(F32)
    hidden = r.xs[...]
    scaled, _ = normalize(hidden)
    normed = (scaled * r.vec[0:1, :] + r.vec[1:2, :]).astype(BF16)
    projected = mm(normed, r.wqkv[...].reshape(D, 3 * D))
    r.qkv[rows, 0:D] = (projected[:, :D] + r.vec[2:3, :]).astype(BF16)
    r.qkv[rows, D : 2 * D] = projected[:, D : 2 * D].astype(BF16)
    r.qkv[rows, 2 * D :] = (projected[:, 2 * D :] + r.vec[3:4, :]).astype(BF16)
    lane = iota((ROWS, LANES), 1)
    column = iota((2 * ROWS, ROWS), 1)
    for pair in range(HEADS // 2):
        at = pair * LANES
        queries = r.qkv[rows, at : at + LANES]
        keys = r.qkv[rows, D + at : D + at + LANES]
        values = r.qkv[rows, 2 * D + at : 2 * D + at + LANES]
        both = two_heads(queries)
        scores = mm_nt(both, keys) * HEAD_DIM**-0.5
        scores = jnp.where(column < SEQ, scores, -1e30)
        expo = jnp.exp(scores - jnp.max(scores, axis=-1, keepdims=True))
        probs = (expo / jnp.sum(expo, axis=-1, keepdims=True)).astype(BF16)
        r.probs[i * (HEADS // 2) + pair] = probs
        mixed = mm(probs, values)
        r.mix[rows, at : at + LANES] = jnp.where(
            lane < HEAD_DIM, mixed[:ROWS], mixed[ROWS:]
        ).astype(BF16)
    residual = hidden + mm(r.mix[rows, :], r.wout[...].reshape(D, D)) + r.vec[4:5, :]
    r.residual[rows, :] = residual
    scaled2, _ = normalize(residual)
    normed2 = (scaled2 * r.vec[5:6, :] + r.vec[6:7, :]).astype(BF16)
    r.wide[rows, 0:D] = normed2
    logits = jnp.where(lane < EXPERTS, mm_nt(normed2, r.router[...]), -1e30)
    expo = jnp.exp(logits - jnp.max(logits, axis=-1, keepdims=True))
    gates = expo / jnp.sum(expo, axis=-1, keepdims=True)
    r.gates[rows, :] = gates
    high, mid, low = split3(gates)
    packed = high + pltpu.roll(mid, EXPERTS, 1) + pltpu.roll(low, 2 * EXPERTS, 1)
    r.wide[rows, 2 * D :] = packed.astype(BF16)
    live = jnp.where(i < r.count[0], 1.0, 0.0)
    r.xs[0:SEQ, :] = r.other_at[i % 2].astype(F32) * live
    r.wide[rows, D : 2 * D] = r.xs[...].astype(BF16)


def routing(r):
    limit = r.count[0] * ROWS
    order = r.order[...]
    places = order.shape[1]
    for image in range(1, SLOTS):
        order = order + jnp.where(r.order[...] >= image * SEQ, ROWS - SEQ, 0)
    lane = iota((ROWS, LANES), 1)

    def find(i, carry):
        rows = image_rows(i)
        place_row, wanted = carry
        seen = order == iota((ROWS, places), 0) + i * ROWS
        place = jnp.sum(
            jnp.where(seen, iota((ROWS, places), 1).astype(F32), 0.0), axis=1, keepdims=True
        )
        r.gates[rows, :] = jnp.broadcast_to(place, (ROWS, LANES))
        same = iota((ROWS, TOK), 0) + i * ROWS == iota((ROWS, TOK), 1)
        place_row = place_row + jnp.sum(jnp.where(same, place, 0.0), axis=0, keepdims=True)
        row = iota((ROWS, LANES), 0)
        live = (row + i * ROWS < limit) & (row < SEQ)
        own = iota((ROWS, places), 0) + i * SEQ == iota((ROWS, places), 1)
        first = jnp.sum(jnp.where(own, r.routes[0:1, :], 0), axis=1, keepdims=True)
        second = jnp.sum(jnp.where(own, r.routes[1:2, :], 0), axis=1, keepdims=True)
        hit0 = jnp.where((first == lane) & live, 1.0, 0.0)
        hit1 = jnp.where((second == lane) & live, 1.0, 0.0)
        r.wide[rows, 0:LANES] = hit0.astype(BF16)
        r.wide[rows, LANES : 2 * LANES] = hit1.astype(BF16)
        return place_row, wanted + jnp.sum(hit0, axis=0, keepdims=True)

    place_row, wanted = lax.fori_loop(
        0, SLOTS, find, (jnp.zeros((1, TOK), F32), jnp.zeros((1, LANES), F32))
    )
    r.total[0:LANES, 0:TOK] = jnp.zeros((LANES, TOK), F32)

    def count(i, carry):
        rows = image_rows(i)
        earlier = jnp.where(place_row < r.gates[rows, 0:1], 1.0, 0.0).astype(BF16)
        before = mm(earlier, r.wide[:, 0 : 2 * LANES])
        hit0, hit1 = r.wide[rows, 0:LANES] > 0, r.wide[rows, LANES : 2 * LANES] > 0
        position = jnp.where(
            hit0, before[:, 0:LANES], jnp.where(hit1, before[:, LANES:] + wanted, 1e6)
        )
        position = jnp.where(position < CAP, position, -1.0)
        r.pos_col[rows, :] = position
        same = iota((ROWS, TOK), 0) + i * ROWS == iota((ROWS, TOK), 1)
        same = jnp.where(same, 1.0, 0.0).astype(BF16)
        high = position.astype(BF16)
        low = (position - high.astype(F32)).astype(BF16)
        r.total[0:LANES, 0:TOK] += mm_tn(high, same) + mm_tn(low, same)
        return carry

    lax.fori_loop(0, SLOTS, count, 0)
    r.pos_row[...] = r.total[0:8, 0:TOK]
    r.total[0:LANES, 0:TOK] = jnp.zeros((LANES, TOK), F32)


def nothing(step):
    pass


def dispatch(e, r, beside=nothing):
    wanted = r.pos_row[pl.ds(e, 1), :]
    lane = iota((SLOT_TILE, LANES), 1)

    def tile(m, carry):
        beside(m)
        rows = pl.ds(pl.multiple_of(m * SLOT_TILE, 16), SLOT_TILE)
        slot = (iota((SLOT_TILE, TOK), 0) + m * SLOT_TILE).astype(F32)
        chosen = jnp.where(slot == wanted, 1.0, 0.0).astype(BF16)
        got = mm(chosen, r.wide[...])
        r.disp[rows, :] = got[:, 0:D].astype(BF16)
        r.up[rows, :] = got[:, D : 2 * D].astype(BF16)
        mine = (lane == e) | (lane == e + EXPERTS) | (lane == e + 2 * EXPERTS)
        gate = jnp.sum(jnp.where(mine, got[:, 2 * D :], 0.0), axis=1, keepdims=True)
        r.gate_slot[rows, :] = jnp.broadcast_to(gate, (SLOT_TILE, LANES))
        r.gexp[rows, :] = (gate * got[:, D : 2 * D]).astype(BF16)
        return carry

    lax.fori_loop(0, CAPP // SLOT_TILE, tile, 0)
    r.eo[...] = jnp.zeros_like(r.eo)
    r.gdisp[...] = jnp.zeros_like(r.gdisp)


def expert_step(e, f, k, r):
    cols = pl.ds(pl.multiple_of(f * FT, FT), FT)
    block = (k, f // 2, f % 2)
    w_in = r.win[k, :, :, :, :, cols].reshape(D, FT)
    w_back = r.wback[block].reshape(FT, D)
    disp = r.disp[...]
    gexp = r.gexp[...]
    bias = r.vec[pl.ds(16 + 4 * e + f, 1), :]
    pre = mm(disp, w_in) + bias
    grad_active = mm_nt(gexp, w_back)
    active, slope = gelu_parts(pre)
    active = active.astype(BF16)
    grad_inner = (grad_active * slope).astype(BF16)
    r.eo[...] += mm(active, w_back)
    r.gdisp[...] += mm_nt(grad_inner, w_in)
    r.wback[block] = mm_tn(active, gexp).astype(BF16).reshape(2, BLOCK_BACK, D)
    grad_in = mm_tn(disp, grad_inner).astype(BF16)
    r.win[k, :, :, :, :, cols] = grad_in.reshape(2, 2, 2, BLOCK_IN, FT)
    r.gvec[pl.ds(16 + 4 * e + f, 1), :] = jnp.sum(
        grad_inner.astype(F32), axis=0, keepdims=True
    )


def combine(e, r, beside=nothing):
    r.gvec[pl.ds(12 + e, 1), :] = jnp.sum(r.gexp[...].astype(F32), axis=0, keepdims=True)
    out = r.eo[...] + r.vec[pl.ds(12 + e, 1), :]
    gate = r.gate_slot[:, 0:1]
    r.disp[...] = (gate * out).astype(BF16)
    r.gexp[...] = r.gdisp[...].astype(BF16)
    high, mid, low = split3(jnp.sum(r.up[...].astype(F32) * out, axis=1, keepdims=True))
    lane = iota((CAPP, LANES), 1)
    parts = jnp.where(
        lane == e,
        high,
        jnp.where(lane == e + EXPERTS, mid, jnp.where(lane == e + 2 * EXPERTS, low, 0.0)),
    )
    r.pairs[...] = parts.astype(BF16)

    def image(i, carry):
        beside(i)
        rows = image_rows(i)
        mine = iota((ROWS, LANES), 1) == e
        wanted = jnp.sum(jnp.where(mine, r.pos_col[rows, :], 0.0), axis=1, keepdims=True)
        chosen = jnp.where(wanted == iota((ROWS, CAPP), 1).astype(F32), 1.0, 0.0).astype(BF16)
        r.total[rows, 0:D] += mm(chosen, r.disp[...])
        r.total[rows, D : 2 * D] += mm(chosen, r.gexp[...])
        r.total[rows, 2 * D :] += mm(chosen, r.pairs[...])
        return carry

    lax.fori_loop(0, SLOTS, image, 0)


def norm_backward(i, r):
    rows = image_rows(i)
    lane = iota((ROWS, LANES), 1)
    live = jnp.where(i < r.count[0], 1.0, 0.0)
    residual = r.residual[rows, :]
    r.other_at[i % 2] = ((residual + r.total[rows, 0:D]) * live)[0:SEQ, :].astype(BF16)
    pairs = r.total[rows, 2 * D :]
    gates = r.gates[rows, :]
    grad_gates = (
        pairs + pltpu.roll(pairs, LANES - EXPERTS, 1) + pltpu.roll(pairs, LANES - 2 * EXPERTS, 1)
    )
    grad_gates = jnp.where(lane < EXPERTS, grad_gates, 0.0)
    grad_logits = (
        gates * (grad_gates - jnp.sum(grad_gates * gates, axis=-1, keepdims=True))
    ).astype(BF16)
    r.gvec[8:12, :] += mm_tn(grad_logits, r.wide[rows, 0:D])[0:EXPERTS, :]
    grad_normed2 = r.total[rows, D : 2 * D] + mm(grad_logits, r.router[...])
    scaled2, inverse2 = normalize(residual)
    r.gvec[5:6, :] += jnp.sum(grad_normed2 * scaled2, axis=0, keepdims=True)
    r.gvec[6:7, :] += jnp.sum(grad_normed2, axis=0, keepdims=True)
    grad_residual = r.wide[rows, D : 2 * D].astype(F32) + norm_back(
        grad_normed2, scaled2, inverse2, r.vec[5:6, :]
    )
    r.residual[rows, :] = grad_residual
    grad_attended = grad_residual.astype(BF16)
    r.wide[rows, D : 2 * D] = grad_attended
    r.gvec[4:5, :] += jnp.sum(grad_attended.astype(F32), axis=0, keepdims=True)
    r.wide[rows, 0:D] = mm_nt(grad_attended, r.wout[...].reshape(D, D)).astype(BF16)


def attention_backward(i, r):
    rows = image_rows(i)
    lane = iota((ROWS, LANES), 1)
    for pair in range(HEADS // 2):
        at = pair * LANES
        queries = r.qkv[rows, at : at + LANES]
        keys = r.qkv[rows, D + at : D + at + LANES]
        values = r.qkv[rows, 2 * D + at : 2 * D + at + LANES]
        from_mix = r.wide[rows, at : at + LANES]
        from_both = two_heads(from_mix)
        probs_low = r.probs[i * (HEADS // 2) + pair]
        probs = probs_low.astype(F32)
        weighted = mm_nt(from_both, values) * probs
        grad_scores = (
            weighted - probs * jnp.sum(weighted, axis=-1, keepdims=True)
        ).astype(BF16)
        grad_q = mm(grad_scores, keys)
        scale = HEAD_DIM**-0.5
        joined = jnp.where(lane < HEAD_DIM, grad_q[:ROWS], grad_q[ROWS:])
        r.qkv[rows, at : at + LANES] = (joined * scale).astype(BF16)
        grad_k = mm_tn(grad_scores, two_heads(queries))
        r.qkv[rows, D + at : D + at + LANES] = (grad_k * scale).astype(BF16)
        grad_v = mm_tn(probs_low, from_both)
        r.qkv[rows, 2 * D + at : 2 * D + at + LANES] = grad_v.astype(BF16)
    grads = r.qkv[rows, :]
    r.gvec[2:3, :] += jnp.sum(grads[:, 0:D].astype(F32), axis=0, keepdims=True)
    r.gvec[3:4, :] += jnp.sum(grads[:, 2 * D :].astype(F32), axis=0, keepdims=True)
    grad_normed1 = mm_nt(grads, r.wqkv[...].reshape(D, 3 * D))
    r.xs[0:SEQ, :] = r.image_at[i % 2].astype(F32)
    scaled1, inverse1 = normalize(r.xs[...])
    r.wide[rows, 0:D] = (scaled1 * r.vec[0:1, :] + r.vec[1:2, :]).astype(BF16)
    r.gvec[0:1, :] += jnp.sum(grad_normed1 * scaled1, axis=0, keepdims=True)
    r.gvec[1:2, :] += jnp.sum(grad_normed1, axis=0, keepdims=True)
    grad_in = r.residual[rows, :] + norm_back(grad_normed1, scaled1, inverse1, r.vec[0:1, :])
    r.grad_at[i % 2] = grad_in[0:SEQ, :].astype(BF16)


def wout_grad(r):
    r.wout[...] = mm_tn(r.mix[...], r.wide[:, D : 2 * D]).astype(BF16).reshape(r.wout.shape)


def wqkv_grad(part, r):
    width = 3 * D // QKV_PARTS
    cols = slice(part * width, (part + 1) * width)
    grad = mm_tn(r.wide[:, 0:D], r.qkv[:, cols]).astype(BF16)
    r.wqkv[:, :, :, :, :, cols] = grad.reshape(r.wqkv.shape[:5] + (width,))


def spread_router(r):
    r.router[...] = jnp.zeros_like(r.router)
    first = r.vec[8:16, :]
    r.router[0:16, :] = jnp.concatenate(
        [jnp.where(iota((8, D), 0) < EXPERTS, first, 0.0), jnp.zeros((8, D), F32)], axis=0
    ).astype(BF16)


def pattern(shape, match):
    return jnp.where(match(iota(shape, 0), iota(shape, 1)), 1.0, 0.0).astype(BF16)


def all_vectors(r):
    packs = r.small[...].reshape(GROUP * 8, LANES).astype(BF16)
    line, column = iota((GROUP * 8, D), 0), iota((GROUP * 8, D), 1)

    def row(match, line_of):
        spread = mm(packs, pattern((LANES, D), match))
        return lambda: jnp.sum(jnp.where(line == line_of, spread, 0.0), axis=0, keepdims=True)

    sixteenth = 8 * (column >> 4)
    for index, start in ((0, 0), (1, 16), (4, 64), (5, 80), (6, 96)):
        r.vec[index : index + 1, :] = row(lambda j, c: j == start + (c & 15), sixteenth)()
    for index in range(2):
        r.vec[2 + index : 3 + index, :] = row(
            lambda j, c: j == 32 + (c & 31), 8 * (16 * index + (column >> 5))
        )()
    r.vec[7:8, :] = jnp.zeros((1, D), F32)
    for e in range(EXPERTS):
        r.vec[8 + e : 9 + e, :] = row(lambda j, c: j == 4 * (c & 15) + e, sixteenth + 1)()
        r.vec[12 + e : 13 + e, :] = row(
            lambda j, c: j == 64 + (c & 63), 8 * (8 * e + (column >> 6)) + 1
        )()
    for device in range(GROUP):
        at = (device // 8, device // 4 % 2, device // 2 % 2, device % 2)
        for line_of in range(2):
            start = device % 2 * 256 + line_of * LANES
            r.vec[16 + device // 2 : 17 + device // 2, start : start + LANES] = r.small[
                at + (slice(2 + line_of, 3 + line_of), FULL)
            ]


def own_vectors(me, r):
    row, column = iota((8, D), 0), iota((8, D), 1)
    lane, line = iota((8, LANES), 1), iota((8, LANES), 0)

    def fold(values, match):
        parts = [v.astype(BF16) for v in split3(values)]
        chosen = pattern((D, LANES), match)
        return sum(mm(v, chosen) for v in parts)

    owner = jnp.where(
        row == 2, column >> 5, jnp.where(row == 3, 16 + (column >> 5), column >> 4)
    )
    top = jnp.where(owner == me, r.gvec[0:8, :], 0.0)
    by16 = fold(top, lambda c, j: (c & 15) == j)
    by32 = fold(top, lambda c, j: (c & 31) == j)
    for name, index in dict(ln1_gain=0, ln1_bias=1, b_out=4, ln2_gain=5, ln2_bias=6).items():
        getattr(r, "out_" + name)[...] = by16[index : index + 1, 0:16]
    r.out_b_qv[...] = by32[2:3, 0:32] + by32[3:4, 0:32]
    owner = jnp.where(row < 4, column >> 4, 8 * (row - 4) + (column >> 6))
    low = jnp.where(owner == me, r.gvec[8:16, :], 0.0)
    router = jnp.where((lane & 3) == line, fold(low, lambda c, j: (c & 15) == (j >> 2)), 0.0)
    r.out_w_router[...] = jnp.sum(jnp.where(line < 4, router, 0.0), axis=0, keepdims=True)[:, 0:64]
    back = jnp.where(line < 4, 0.0, fold(low, lambda c, j: (c & 63) == j))
    r.out_b_back[...] = jnp.sum(back, axis=0, keepdims=True)[:, 0:64]
    row, column = iota((16, D), 0), iota((16, D), 1)
    bias = jnp.where(2 * row + (column >> 8) == me, r.gvec[16:32, :], 0.0)
    bias = jnp.sum(bias, axis=0, keepdims=True)
    r.out_b_in[...] = bias[:, 0:256] + bias[:, 256:512]


class Place:
    def __init__(self):
        me = lax.axis_index("dev")
        self.me, self.c, self.x, self.y, self.z = me, me % 2, me // 2 % 2, me // 4 % 2, me // 8
        self.core = self.device(self.z, self.y, self.x, 1 - self.c)
        self.over_y = self.device(self.z, 1 - self.y, self.x, self.c)
        self.over_x = self.device(self.z, self.y, 1 - self.x, self.c)

    def device(self, z, y, x, c):
        return ((z * 2 + y) * 2 + x) * 2 + c

    def plane(self, k):
        return lax.rem(self.z + k + EXPERTS, EXPERTS)

    def above(self, k):
        return self.device(self.plane(k), self.y, self.x, self.c)

    def greet(self):
        barrier = pltpu.get_barrier_semaphore()
        friends = [self.above(k) for k in range(1, EXPERTS)]
        friends += [self.core, self.over_y, self.over_x]
        for friend in friends:
            pl.semaphore_signal(barrier, inc=1, device_id=(friend,), device_id_type=MESH)
        pl.semaphore_wait(barrier, len(friends))

    def first(self, route):
        return self.over_y if route == 0 else self.over_x

    def second(self, route):
        return self.over_x if route == 0 else self.over_y


class Copies:
    def __init__(self, sems, index):
        self.sems, self.index = sems, index

    def make(self, slot, source, target, device):
        send_sem, recv_sem = self.sems
        return pltpu.make_async_remote_copy(
            src_ref=source, dst_ref=target, send_sem=send_sem.at[self.index, slot],
            recv_sem=recv_sem.at[self.index, slot], device_id=(device,), device_id_type=MESH,
        )


class SumAll(Copies):
    def __init__(self, sems, index, values, landing, place):
        super().__init__(sems, index)
        self.values, self.landing, self.p = values, landing, place

    def stage(self, step):
        p = self.p
        targets = [
            [(k, p.above(k)) for k in range(1, EXPERTS)], [(4, p.over_y)], [(5, p.over_x)],
            [(6, p.core)],
        ][step]
        return [self.make(s, self.values, self.landing.at[s - 1], d) for s, d in targets]

    def begin(self, step):
        for copy in self.stage(step):
            copy.start()

    def end(self, step):
        for copy in self.stage(step):
            copy.wait()
        if step == 0:
            self.values[...] += self.landing[0] + self.landing[1] + self.landing[2]
        else:
            self.values[...] += self.landing[2 + step]


class Gather(Copies):
    def __init__(self, sems, index, shard, full, tail, route, k, place):
        super().__init__(sems, index)
        self.shard, self.full, self.tail, self.route, self.p = shard, full, tail, route, place
        self.k = k

    def at(self, lead, y, x, c):
        return self.full.at[(lead, y, x, c) + self.tail]

    def own(self):
        return self.shard.at[self.tail] if self.tail else self.shard

    def local(self, sem):
        p = self.p
        lead = p.z if self.k is None else 0
        return pltpu.make_async_copy(self.own(), self.at(lead, p.y, p.x, p.c), sem)

    def along_z(self, arriving):
        p = self.p
        if self.k is None:
            return [
                self.make(k, self.own(), self.at(p.plane(-k) if arriving else p.z, p.y, p.x, p.c),
                          p.above(k))
                for k in range(1, EXPERTS)
            ]
        if self.k == 0:
            return []
        return [self.make(1, self.own(), self.at(self.k, p.y, p.x, p.c), p.above(-self.k))]

    def lead(self):
        return FULL if self.k is None else self.k

    def across(self, step, arriving):
        p = self.p
        y, x = p.y, p.x
        if step == 0:
            if arriving:
                y, x = (1 - y, x) if self.route == 0 else (y, 1 - x)
            device = p.first(self.route)
        else:
            if arriving:
                y, x = 1 - y, 1 - x
            y, x = (FULL, x) if self.route == 0 else (y, FULL)
            device = p.second(self.route)
        block = self.at(self.lead(), y, x, p.c)
        return self.make(4 + step, block, block, device)

    def to_core(self, step, arriving):
        p = self.p
        y, x = p.y, p.x
        if step == 1:
            y, x = (1 - y, x) if self.route == 0 else (y, 1 - x)
        elif step == 2:
            y, x = (FULL, 1 - x) if self.route == 0 else (1 - y, FULL)
        block = self.at(self.lead(), y, x, 1 - p.c if arriving else p.c)
        return self.make(6 + step, block, block, p.core)

    def start_z(self):
        for copy in self.along_z(False):
            copy.start()

    def stage(self, step):
        if step == 0:
            for copy in self.along_z(True):
                copy.wait_recv()
        else:
            self.across(step - 1, True).wait_recv()
        if step < 2:
            self.across(step, False).start()
        self.to_core(step, False).start()

    def finish(self):
        for step in range(3):
            self.to_core(step, True).wait_recv()
        for copy in self.along_z(False):
            copy.wait_send()
        for step in range(2):
            self.across(step, False).wait_send()
        for step in range(3):
            self.to_core(step, False).wait_send()


class Scatter(Copies):
    def __init__(self, sems, index, full, landing, out, tail, route, k, place):
        super().__init__(sems, index)
        self.full, self.out, self.tail, self.route, self.p, self.k = (
            full, out, tail, route, place, k,
        )
        self.from_core, self.from_first, self.from_second, self.from_z = landing

    def lead(self):
        return FULL if self.k is None else self.k

    def landed(self, ref, spare):
        if self.k is None:
            return (FULL,) * (1 + spare) + self.tail
        return (self.k % ref.shape[0],) + (FULL,) * spare + self.tail

    def to_core(self):
        p = self.p
        return self.make(0, self.full.at[(self.lead(), FULL, FULL, 1 - p.c) + self.tail],
                         self.from_core.at[self.landed(self.from_core, 2)], p.core)

    def to_first(self):
        p = self.p
        y, x = (FULL, 1 - p.x) if self.route == 0 else (1 - p.y, FULL)
        return self.make(1, self.full.at[(self.lead(), y, x, p.c) + self.tail],
                         self.from_first.at[self.landed(self.from_first, 1)],
                         p.second(self.route))

    def to_second(self):
        p = self.p
        y, x = (1 - p.y, p.x) if self.route == 0 else (p.y, 1 - p.x)
        return self.make(2, self.full.at[(self.lead(), y, x, p.c) + self.tail],
                         self.from_second.at[self.landed(self.from_second, 0)],
                         p.first(self.route))

    def along_z(self):
        p = self.p
        steps = range(1, EXPERTS) if self.k is None else ([self.k] if self.k else [])
        return [
            self.make(2 + k, self.full.at[(p.plane(k) if self.k is None else k, p.y, p.x, p.c) + self.tail],
                      self.from_z.at[(k - 1,) + self.tail], p.above(k))
            for k in steps
        ]

    def add(self, mine, landed):
        def layer(k, carry):
            for at, source in zip(mine(k), landed(k)):
                self.full[at + self.tail] = self.full[at + self.tail] + source
            return carry

        if self.k is None:
            lax.fori_loop(0, EXPERTS, layer, 0)
        else:
            layer(self.k, 0)

    def slot(self, ref, k):
        return k if self.k is None else k % ref.shape[0]

    def stage(self, step):
        p, tail = self.p, self.tail
        if step == 0:
            self.to_core().start()
        elif step == 1:
            self.to_core().wait_recv()
            spots = [(y, x) for y in range(2) for x in range(2)]
            ref = self.from_core
            self.add(lambda k: [(k, y, x, p.c) for y, x in spots],
                     lambda k: [ref[(self.slot(ref, k), y, x) + tail] for y, x in spots])
            self.to_first().start()
        elif step == 2:
            self.to_first().wait_recv()
            ref = self.from_first
            self.add(lambda k: [(k, o, p.x, p.c) if self.route == 0 else (k, p.y, o, p.c) for o in range(2)],
                     lambda k: [ref[(self.slot(ref, k), o) + tail] for o in range(2)])
            self.to_second().start()
        else:
            self.to_second().wait_recv()
            ref = self.from_second
            self.add(lambda k: [(k, p.y, p.x, p.c)],
                     lambda k: [ref[(self.slot(ref, k),) + tail]])
            for copy in self.along_z():
                copy.start()

    def collect(self):
        p, tail = self.p, self.tail
        total = self.full[((p.z if self.k is None else 0), p.y, p.x, p.c) + tail].astype(F32)
        for k in range(EXPERTS - 1):
            total = total + self.from_z[(k,) + tail].astype(F32)
        rows, columns = total.shape
        height, width = self.full.shape[-2:]
        first_row, first_column = tail[0].start or 0, tail[1].start or 0
        step = width // LANES
        for j in range(columns // LANES):
            line = first_row * step + first_column // LANES + j
            self.out[pl.ds(line, rows, stride=step), :] = total[:, j * LANES : (j + 1) * LANES]

    def drain(self):
        self.to_core().wait_send()
        self.to_first().wait_send()
        self.to_second().wait_send()
        for copy in self.along_z():
            copy.wait_send()


class Refs:
    def __init__(self, names, refs):
        for name, ref in zip(names, refs, strict=True):
            setattr(self, name, ref)


SCRATCH = dict(
    image_at=((2, SEQ, D), BF16),
    other_at=((2, SEQ, D), BF16),
    grad_at=((2, SEQ, D), BF16),
    xs=((ROWS, D), F32),
    router=((LANES, D), BF16),
    qkv=((TOK, 3 * D), BF16),
    probs=((SLOTS * HEADS // 2, 2 * ROWS, ROWS), BF16),
    mix=((TOK, D), BF16),
    residual=((TOK, D), F32),
    wide=((TOK, WIDE), BF16),
    gates=((TOK, LANES), F32),
    pos_col=((TOK, LANES), F32),
    pos_row=((8, TOK), F32),
    disp=((CAPP, D), BF16),
    up=((CAPP, D), BF16),
    gexp=((CAPP, D), BF16),
    gate_slot=((CAPP, LANES), F32),
    pairs=((CAPP, LANES), BF16),
    eo=((CAPP, D), F32),
    gdisp=((CAPP, D), F32),
    total=((TOK, WIDE), F32),
    wqkv=((EXPERTS, 2, 2, 2, 16, 3 * D), BF16),
    wout=((EXPERTS, 2, 2, 2, 16, D), BF16),
    win=((EXPERTS, 2, 2, 2, BLOCK_IN, HID), BF16),
    wback=((EXPERTS, 2, 2, 2, BLOCK_BACK, D), BF16),
)
SHARDS = dict(wqkv=(16, 3 * D), wout=(16, D), win=(BLOCK_IN, HID), wback=(BLOCK_BACK, D))


def columns_of(width, h, parts=2):
    return (FULL, slice(h * width // parts, (h + 1) * width // parts))


def rows_of(height, h):
    return (slice(h * height // 2, (h + 1) * height // 2), FULL)


SMALL = dict(
    ln1_gain=16, ln1_bias=16, b_qv=32, b_out=16, ln2_gain=16, ln2_bias=16, w_router=64, b_in=256,
    b_back=64,
)
FLAT_PIECES = [("wqkv", columns_of(3 * D, h, QKV_PARTS), h % 2) for h in range(QKV_PARTS)]
FLAT_PIECES += [("wout", columns_of(D, h), h) for h in range(2)]
FLAT_PIECES += [("small", (), 0)]
EXPERT_PIECES = [("win", rows_of(BLOCK_IN, h), h) for h in range(2)]
EXPERT_PIECES += [("wback", rows_of(BLOCK_BACK, h), h) for h in range(2)]
LANDING = {}
for name in ("wqkv", "wout"):
    for part, lead in dict(core=(4, 2, 2), first=(4, 2), second=(4,), z=(3,)).items():
        LANDING[name, part] = (lead + SHARDS[name], BF16)
for name in ("win", "wback"):
    for part, lead in dict(core=(2, 2, 2), first=(4, 2), second=(4,), z=(3,)).items():
        LANDING[name, part] = (lead + SHARDS[name], BF16)
INPUTS = ["count", "images", "cotangent", "routes", "order"]


def whole_kernel(*refs):
    names = INPUTS + ["shard_small"] + ["shard_" + n for n in SHARDS]
    names += ["blocks", "gimages"] + ["out_" + n for n in SHARDS] + ["out_" + n for n in SMALL]
    names += list(SCRATCH) + ["vec", "gvec", "small", "land_gvec"]
    names += ["land_" + "_".join(key) for key in LANDING]
    names += ["local_sem", "vec_send", "vec_recv", "get_send", "get_recv", "put_send", "put_recv"]
    names += ["free_sem", "in_sem", "out_sem"]
    r = Refs(names, refs)
    p = Place()
    p.greet()

    def landing(name):
        return [getattr(r, f"land_{name}_{part}") for part in ("core", "first", "second", "z")]

    get_sems, put_sems = (r.get_send, r.get_recv), (r.put_send, r.put_recv)
    flat_get, flat_put = [], []
    for index, (name, tail, route) in enumerate(FLAT_PIECES):
        flat_get.append(
            Gather(get_sems, index, getattr(r, "shard_" + name), getattr(r, name), tail, route, None, p)
        )
        if name != "small":
            flat_put.append(
                Scatter(put_sems, index, getattr(r, name), landing(name), getattr(r, "out_" + name),
                        tail, route, None, p)
            )
    get, put = [], []
    for k in range(EXPERTS):
        get.append([])
        put.append([])
        for index, (name, tail, route) in enumerate(EXPERT_PIECES):
            index += len(FLAT_PIECES) + k * len(EXPERT_PIECES)
            get[k].append(
                Gather(get_sems, index, getattr(r, "shard_" + name), getattr(r, name), tail, route, k, p)
            )
            put[k].append(
                Scatter(put_sems, index, getattr(r, name), landing(name), getattr(r, "out_" + name),
                        tail, route, k, p)
            )

    def part(pieces, which):
        return pieces if which is None else pieces[2 * which : 2 * which + 2]

    def gather_stage(k, step, which=None):
        for piece in part(get[k], which):
            piece.start_z() if step < 0 else piece.stage(step)

    def scatter_stage(k, step, which=None):
        if step == 0 and k >= 2 and which != 1:
            pl.semaphore_wait(r.free_sem, 1)
        for piece in part(put[k], which):
            piece.stage(step)
        if step == 1 and k < 2 and which != 0:
            pl.semaphore_signal(r.free_sem, inc=1, device_id=(p.core,), device_id_type=MESH)

    def wout_stage(step):
        for piece in flat_put[QKV_PARTS:]:
            piece.stage(step)

    events = {
        ("start",): [("get", 0, 0, 1), ("get", 0, 1, 1)],
        ("flat", 0): [("get", 3, -1, 0)],
        ("flat", 1): [("get", 3, 0, 0), ("get", 1, -1, 0)],
        ("flat", 2): [("get", 1, -1, 1), ("get", 0, 0, 0), ("get", 3, 1, 0), ("get", 0, 2, 1), ("get", 2, -1, 0)],
        ("forward", 0): [("get", 0, 1, 0)],
        ("forward", 2): [("get", 1, 0, 0)],
        ("forward", 4): [("get", 1, 0, 1)],
        ("dispatch", 0, 0): [("get", 0, 2, 0)],
        ("dispatch", 0, 2): [("get", 2, -1, 1)],
        ("dispatch", 0, 3): [("get", 1, 1, 0)],
        ("dispatch", 0, 4): [("get", 3, 2, 0)],
        ("expert", 0, 3): [("get", 1, 1, 1)],
        ("expert", 0, 7): [("get", 1, 2, 0)],
        ("combine", 0, 2): [("get", 2, 0, 0), ("get", 1, 2, 1), ("get", 3, -1, 1)],
        ("combine", 0, 3): [("get", 2, 0, 1)],
        ("combine", 0, 4): [("put", 0, 0, 0)],
        ("dispatch", 1, 4): [("get", 2, 1, 0)],
        ("expert", 1, 3): [("put", 0, 0, 1)],
        ("expert", 1, 5): [("get", 3, 0, 1)],
        ("expert", 1, 6): [("get", 2, 2, 0)],
        ("expert", 1, 7): [("get", 2, 1, 1)],
        ("combine", 1, 0): [("put", 1, 0, 0)],
        ("combine", 1, 3): [("get", 3, 1, 1)],
        ("dispatch", 2, 1): [("get", 2, 2, 1), ("put", 0, 1, 0)],
        ("dispatch", 2, 4): [("put", 1, 0, 1), ("put", 1, 1, 0)],
        ("expert", 2, 6): [("put", 0, 1, 1)],
        ("expert", 2, 7): [("get", 3, 2, 1)],
        ("combine", 2, 2): [("put", 2, 0, 0)],
        ("combine", 2, 4): [("put", 0, 2, 0)],
        ("dispatch", 3, 0): [("put", 1, 2, 0)],
        ("dispatch", 3, 3): [("put", 2, 0, 1)],
        ("expert", 3, 0): [("put", 2, 1, 0)],
        ("expert", 3, 3): [("put", 1, 3, 0)],
        ("expert", 3, 4): [("put", 2, 1, 1)],
        ("expert", 3, 6): [("put", 0, 3, 0)],
        ("expert", 3, 7): [("put", 2, 2, 0)],
        ("combine", 3, 1): [("put", 1, 1, 1)],
        ("combine", 3, 3): [("put", 3, 0, 0)],
        ("norms", 0): [("put", 2, 3, 0)],
        ("norms", 1): [("put", 2, 2, 1)],
        ("norms", 2): [("put", 3, 1, 0)],
        ("norms", 3): [("put", 0, 2, 1)],
        ("backward", 0): [("put", 2, 3, 1)],
        ("backward", 1): [("put", 3, 0, 1), ("out", 1), ("put", 1, 2, 1)],
        ("backward", 2): [("put", 3, 2, 0)],
        ("backward", 3): [("out", 2)],
        ("backward", 4): [("put", 3, 1, 1), ("put", 1, 3, 1)],
        ("tail", 0): [("out", 3)],
        ("tail", 2): [("put", 3, 3, 0)],
        ("tail", 3): [("put", 3, 2, 1), ("put", 0, 3, 1)],
        ("tail", 4): [("put", 3, 3, 1)],
    }

    def beside(*key):
        def at(step):
            for (*found, when), todo in events.items():
                if tuple(found) == key:
                    pl.when(step == when)(functools.partial(act, todo))

        return at

    def act(todo):
        for kind, *what in todo:
            dict(get=gather_stage, put=scatter_stage, out=wout_stage)[kind](*what)

    def fetch(i, both):
        copies = [pltpu.make_async_copy(r.images.at[i], r.image_at.at[i % 2], r.in_sem.at[0, i % 2])]
        if both:
            copies.append(
                pltpu.make_async_copy(r.cotangent.at[i], r.other_at.at[i % 2], r.in_sem.at[1, i % 2])
            )
        return copies

    def emit_block(i):
        return [pltpu.make_async_copy(r.other_at.at[i % 2], r.blocks.at[i], r.out_sem.at[0, i % 2])]

    def emit_grad(i):
        return [pltpu.make_async_copy(r.grad_at.at[i % 2], r.gimages.at[i], r.out_sem.at[1, i % 2])]

    def start(copies):
        for copy in copies:
            copy.start()

    def wait(copies):
        for copy in copies:
            copy.wait()

    start(fetch(0, True))
    local = []
    for index, piece in enumerate(flat_get + get[0]):
        copy = piece.local(r.local_sem.at[index])
        copy.start()
        local.append(copy)
    for piece in flat_get:
        piece.start_z()
    for copy in local:
        copy.wait()
    act(events.get(("start",), ()))
    r.xs[...] = jnp.zeros_like(r.xs)
    r.gvec[...] = jnp.zeros_like(r.gvec)
    r.total[...] = jnp.zeros_like(r.total)
    for step in range(3):
        for piece in flat_get:
            piece.stage(step)
        if step == 0:
            routing(r)
        act(events.get(("flat", step), ()))
    for piece in flat_get:
        piece.finish()
    act(events.get(("flat", 3), ()))
    all_vectors(r)
    spread_router(r)

    def forward(i, carry):
        @pl.when(i + 1 < SLOTS)
        def _():
            start(fetch(i + 1, True))

        wait(fetch(i, True))
        attention_forward(i, r)
        beside("forward")(i)
        return carry

    lax.fori_loop(0, SLOTS, forward, 0)
    for k in range(EXPERTS):
        e = p.plane(k)
        dispatch(e, r, beside("dispatch", k))
        for piece in get[k]:
            piece.finish()

        def step(f, carry):
            beside("expert", k)(2 * f)
            beside("expert", k)(2 * f + 1)
            expert_step(e, f, k, r)
            return carry

        lax.fori_loop(0, HID // FT, step, 0)
        combine(e, r, beside("combine", k))
    start(fetch(0, False))

    def norms(i, carry):
        @pl.when(i >= 2)
        def _():
            wait(emit_block(i - 2))

        norm_backward(i, r)
        start(emit_block(i))
        beside("norms")(i)
        return carry

    lax.fori_loop(0, SLOTS, norms, 0)
    wout_grad(r)
    wqkv_put, wout_put = flat_put[:QKV_PARTS], flat_put[QKV_PARTS:]
    for piece in wout_put:
        piece.stage(0)

    def backward(i, carry):
        @pl.when(i + 1 < SLOTS)
        def _():
            start(fetch(i + 1, False))

        wait(fetch(i, False))

        @pl.when(i >= 2)
        def _():
            wait(emit_grad(i - 2))

        attention_backward(i, r)
        start(emit_grad(i))
        beside("backward")(i)
        return carry

    lax.fori_loop(0, SLOTS, backward, 0)
    sums = SumAll((r.vec_send, r.vec_recv), 0, r.gvec, r.land_gvec, p)
    sums.begin(0)
    for part_of in range(QKV_PARTS):
        wqkv_grad(part_of, r)
        wqkv_put[part_of].stage(0)
        if part_of % 2:
            act(events.get(("tail", part_of // 2), ()))
    for step in range(1, 4):
        sums.end(step - 1)
        sums.begin(step)
        for piece in wqkv_put:
            piece.stage(step)
        act(events.get(("tail", step + 1), ()))
    for k in range(1, EXPERTS):
        for piece in put[k]:
            for copy in piece.along_z():
                copy.wait_recv()
    for piece in put[0]:
        piece.collect()
    for piece in wout_put:
        for copy in piece.along_z():
            copy.wait_recv()
        piece.collect()
    sums.end(3)
    own_vectors(p.me, r)
    for piece in wqkv_put:
        for copy in piece.along_z():
            copy.wait_recv()
        piece.collect()
    for pieces in put + [flat_put]:
        for piece in pieces:
            piece.drain()
    for i in range(SLOTS - 2, SLOTS):
        wait(emit_block(i))
        wait(emit_grad(i))


def alone_kernel(*refs):
    names = INPUTS + ["pack"] + ["full_" + n for n in SHARDS]
    names += ["blocks", "gimages", "gvec"] + ["out_" + n for n in SHARDS]
    names += list(SCRATCH) + ["vec", "sem"]
    r = Refs(names, refs)

    def move(source, target):
        copy = pltpu.make_async_copy(source, target, r.sem)
        copy.start()
        copy.wait()

    for name in SHARDS:
        move(getattr(r, "full_" + name), getattr(r, name))
    r.vec[...] = r.pack[...]
    r.xs[...] = jnp.zeros_like(r.xs)
    r.gvec[...] = jnp.zeros_like(r.gvec)
    r.total[...] = jnp.zeros_like(r.total)
    spread_router(r)
    routing(r)

    def forward(i, carry):
        move(r.images.at[i], r.image_at.at[i % 2])
        move(r.cotangent.at[i], r.other_at.at[i % 2])
        attention_forward(i, r)
        return carry

    def expert(e, carry):
        dispatch(e, r)
        lax.fori_loop(0, HID // FT, lambda f, c: (expert_step(e, f, e, r), c)[1], 0)
        combine(e, r)
        return carry

    def norms(i, carry):
        norm_backward(i, r)
        move(r.other_at.at[i % 2], r.blocks.at[i])
        return carry

    def backward(i, carry):
        move(r.images.at[i], r.image_at.at[i % 2])
        attention_backward(i, r)
        move(r.grad_at.at[i % 2], r.gimages.at[i])
        return carry

    lax.fori_loop(0, SLOTS, forward, 0)
    lax.fori_loop(0, EXPERTS, expert, 0)
    lax.fori_loop(0, SLOTS, norms, 0)
    wout_grad(r)
    lax.fori_loop(0, SLOTS, backward, 0)
    for part in range(QKV_PARTS):
        wqkv_grad(part, r)
    for name in SHARDS:
        move(getattr(r, name), getattr(r, "out_" + name))


def alone(inputs, pack, full):
    vmem = pl.BlockSpec(memory_space=pltpu.VMEM)
    hbm = pl.BlockSpec(memory_space=pltpu.HBM)
    smem = pl.BlockSpec(memory_space=pltpu.SMEM)
    shapes = [((SLOTS, SEQ, D), BF16), ((SLOTS, SEQ, D), BF16), ((32, D), F32)]
    shapes += [SCRATCH[name] for name in SHARDS]
    return pl.pallas_call(
        alone_kernel,
        out_shape=[jax.ShapeDtypeStruct(*s) for s in shapes],
        in_specs=[smem] + [hbm] * 2 + [vmem] * 3 + [hbm] * 4,
        out_specs=[hbm] * 2 + [vmem] + [hbm] * 4,
        scratch_shapes=[pltpu.VMEM(*s) for s in SCRATCH.values()]
        + [pltpu.VMEM((32, D), F32), pltpu.SemaphoreType.DMA],
        compiler_params=pltpu.CompilerParams(vmem_limit_bytes=VMEM_LIMIT),
    )(*inputs, pack, *full)


def whole(inputs, pack, shards):
    vmem = pl.BlockSpec(memory_space=pltpu.VMEM)
    hbm = pl.BlockSpec(memory_space=pltpu.HBM)
    smem = pl.BlockSpec(memory_space=pltpu.SMEM)
    shapes = [((SLOTS, SEQ, D), BF16), ((SLOTS, SEQ, D), BF16)]
    shapes += [((rows * columns // LANES, LANES), F32) for rows, columns in SHARDS.values()]
    shapes += [((1, size), F32) for size in SMALL.values()]
    count = len(FLAT_PIECES) + EXPERTS * len(EXPERT_PIECES)
    dma = pltpu.SemaphoreType.DMA
    return pl.pallas_call(
        whole_kernel,
        out_shape=[jax.ShapeDtypeStruct(*s) for s in shapes],
        in_specs=[smem] + [hbm] * 2 + [vmem] * 2 + [hbm] * 5,
        out_specs=[hbm] * 2 + [vmem] * (len(shapes) - 2),
        scratch_shapes=[pltpu.VMEM(*s) for s in SCRATCH.values()]
        + [pltpu.VMEM((32, D), F32)] * 2
        + [pltpu.VMEM((EXPERTS, 2, 2, 2, 8, LANES), F32), pltpu.VMEM((6, 32, D), F32)]
        + [pltpu.VMEM(*s) for s in LANDING.values()]
        + [dma((len(FLAT_PIECES) + len(EXPERT_PIECES),)), dma((1, 7)), dma((1, 7))]
        + [dma((count, 9)), dma((count, 9)), dma((count, 6)), dma((count, 6))]
        + [pltpu.SemaphoreType.REGULAR, dma((2, 2)), dma((2, 2))],
        compiler_params=pltpu.CompilerParams(
            collective_id=0, has_side_effects=True, vmem_limit_bytes=VMEM_LIMIT
        ),
        cost_estimate=pl.CostEstimate(
            flops=40 * 10**9, bytes_accessed=50 * 10**6, transcendentals=10**7
        ),
    )(*inputs, pack, *shards)


def arrange_kernel(*refs):
    lines = refs[-1]
    for flat, shard in zip(refs[: len(SHARDS)], refs[len(SHARDS) : -1]):
        rows, columns = shard.shape
        step = columns // LANES
        lines[0 : rows * step, :] = flat[...].astype(F32)
        for j in range(step):
            shard[:, j * LANES : (j + 1) * LANES] = lines[
                pl.ds(j, rows, stride=step), :
            ].astype(BF16)


def arrange(flat):
    vmem = pl.BlockSpec(memory_space=pltpu.VMEM)
    longest = max(v.shape[0] for v in flat)
    return pl.pallas_call(
        arrange_kernel,
        out_shape=[jax.ShapeDtypeStruct(s, BF16) for s in SHARDS.values()],
        in_specs=[vmem] * len(flat),
        out_specs=[vmem] * len(flat),
        scratch_shapes=[pltpu.VMEM((longest, LANES), F32)],
    )(*flat)


def settle_kernel(*refs):
    count = (len(refs) - 1) // 3
    sources, targets, held, sems = refs[:count], refs[count : 2 * count], refs[2 * count : -1], refs[-1]
    coming = [pltpu.make_async_copy(sources[k], held[k], sems.at[0, k]) for k in range(count)]
    going = [pltpu.make_async_copy(held[k], targets[k], sems.at[1, k]) for k in range(count)]
    for copy in coming:
        copy.start()
    for arrived, leaving in zip(coming, going):
        arrived.wait()
        leaving.start()
    for copy in going:
        copy.wait()


def settle(arrays):
    hbm = pl.BlockSpec(memory_space=pltpu.HBM)
    return pl.pallas_call(
        settle_kernel,
        out_shape=[jax.ShapeDtypeStruct(a.shape, a.dtype) for a in arrays],
        in_specs=[hbm] * len(arrays),
        out_specs=[hbm] * len(arrays),
        scratch_shapes=[pltpu.VMEM(a.shape, a.dtype) for a in arrays]
        + [pltpu.SemaphoreType.DMA((2, len(arrays)))],
        compiler_params=pltpu.CompilerParams(vmem_limit_bytes=VMEM_LIMIT),
    )(*arrays)


def per_device(
    images, cotangent, routes, priority, image_count,
    ln1_gain, ln1_bias, w_qkv, b_qv, w_out, b_out, ln2_gain, ln2_bias,
    w_router, w_in, b_in, w_back, b_back,
):
    inputs = (image_count, images, cotangent, routes.T, priority)
    if lax.axis_size("dev") != GROUP:
        return with_collectives(
            inputs, ln1_gain, ln1_bias, w_qkv, b_qv, w_out, b_out, ln2_gain, ln2_bias,
            w_router, w_in, b_in, w_back, b_back,
        )
    small = [ln1_gain, ln1_bias, b_qv, b_out, ln2_gain, ln2_bias, None, w_router, b_back, b_in]
    pack, at = 0.0, 0
    for v in small:
        size = 16 if v is None else v.shape[0]
        if v is not None:
            pack = pack + jnp.pad(v.astype(F32), (at, 8 * LANES - at - size))
        at += size
    shards = arrange([v.reshape(-1, LANES) for v in (w_qkv, w_out, w_in, w_back)])
    blocks, gimages, *grads = settle(whole(inputs, pack.reshape(8, LANES), shards))
    grads = dict(zip(["w_qkv", "w_out", "w_in", "w_back"] + list(SMALL), grads))
    order = ["ln1_gain", "ln1_bias", "w_qkv", "b_qv", "w_out", "b_out", "ln2_gain", "ln2_bias"]
    order += ["w_router", "w_in", "b_in", "w_back", "b_back"]
    return (blocks, gimages) + tuple(grads[name].reshape(-1) for name in order)


def with_collectives(
    inputs, ln1_gain, ln1_bias, w_qkv, b_qv, w_out, b_out, ln2_gain, ln2_bias,
    w_router, w_in, b_in, w_back, b_back,
):
    gather = lambda v: lax.all_gather(v, "dev", axis=0, tiled=True)
    scatter = lambda v: lax.psum_scatter(
        v.astype(F32).reshape(-1), "dev", scatter_dimension=0, tiled=True
    )
    row = lambda v: gather(v).astype(F32).reshape(-1, D)
    zero = jnp.zeros((1, D), F32)
    pack = jnp.concatenate(
        [row(ln1_gain), row(ln1_bias), row(b_qv), row(b_out), row(ln2_gain), row(ln2_bias), zero,
         gather(w_router).astype(F32).reshape(D, EXPERTS).T, row(b_back), row(b_in)]
    )
    full = [
        gather(v).reshape(SCRATCH[name][0]) for v, name in zip((w_qkv, w_out, w_in, w_back), SHARDS)
    ]
    blocks, gimages, gvec, gwqkv, gwout, gwin, gwback = alone(inputs, pack, full)
    return (
        blocks, gimages, scatter(gvec[0]), scatter(gvec[1]), scatter(gwqkv), scatter(gvec[2:4]),
        scatter(gwout), scatter(gvec[4]), scatter(gvec[5]), scatter(gvec[6]),
        scatter(gvec[8:12].T), scatter(gwin), scatter(gvec[16:32]), scatter(gwback),
        scatter(gvec[12:16]),
    )


def solution(mesh):
    split = P("dev")
    return jax.shard_map(
        per_device, mesh=mesh, in_specs=(split,) * 18, out_specs=(split,) * 15, check_vma=False
    )
```

```python
import functools

import jax
import jax.numpy as jnp
from jax import lax
from jax.experimental import pallas as pl
from jax.experimental.pallas import tpu as pltpu
from jax.sharding import PartitionSpec as P

D = 512
HEADS = 8
HID = 2048
EXPERTS = 4
SEQ = 197
SLOTS = 5
HEAD_DIM = 64
CAP = 555
EPSILON = 1e-06

ROWS = -(-SEQ // 16) * 16
TOK = SLOTS * ROWS
CAPP = -(-CAP // 16) * 16
LANES = 128
WIDE = 2 * D + LANES
GROUP = EXPERTS * 2 * 2 * 2
BLOCK_IN = EXPERTS * D // GROUP
BLOCK_BACK = EXPERTS * HID // GROUP
SLOT_TILE = CAPP // 5
FT = 512
QKV_PARTS = 4
VMEM_LIMIT = 65000 * 1024
MESH = pl.DeviceIdType.MESH
FULL = slice(None)
F32 = jnp.float32
BF16 = jnp.bfloat16


def mm(a, b):
    return lax.dot_general(a, b, (((1,), (0,)), ((), ())), preferred_element_type=F32)


def mm_nt(a, b):
    return lax.dot_general(a, b, (((1,), (1,)), ((), ())), preferred_element_type=F32)


def mm_tn(a, b):
    return lax.dot_general(a, b, (((0,), (0,)), ((), ())), preferred_element_type=F32)


def iota(shape, dim):
    return lax.broadcasted_iota(jnp.int32, shape, dim)


def normalize(inputs):
    centre = inputs - jnp.mean(inputs, axis=-1, keepdims=True)
    inverse = lax.rsqrt(jnp.mean(centre * centre, axis=-1, keepdims=True) + EPSILON)
    return centre * inverse, inverse


def norm_back(grad_normed, scaled, inverse, gain):
    grad_scaled = grad_normed * gain
    return inverse * (
        grad_scaled
        - jnp.mean(grad_scaled, axis=-1, keepdims=True)
        - scaled * jnp.mean(grad_scaled * scaled, axis=-1, keepdims=True)
    )


def gelu_parts(pre):
    size = jnp.abs(pre)
    t = 1.0 / (1.0 + (0.3275911 * 0.7071067811865476) * size)
    bell = jnp.exp(-0.5 * (pre * pre))
    poly = t * (
        0.127414796
        + t * (-0.142248368 + t * (0.7107068705 + t * (-0.7265760135 + t * 0.5307027145)))
    )
    tail = poly * bell
    phi = jnp.where(pre >= 0, 1.0 - tail, tail)
    return pre * phi, phi + pre * (bell * 0.3989422804014327)


def split3(value):
    high = value.astype(BF16).astype(F32)
    rest = value - high
    mid = rest.astype(BF16).astype(F32)
    return high, mid, rest - mid


def image_rows(i):
    return pl.ds(i * ROWS if isinstance(i, int) else pl.multiple_of(i * ROWS, 16), ROWS)


def two_heads(block):
    first = iota(block.shape, 1) < HEAD_DIM
    zero = jnp.zeros_like(block)
    return jnp.concatenate([jnp.where(first, block, zero), jnp.where(first, zero, block)], axis=0)


def attention_forward(i, r):
    rows = image_rows(i)
    r.xs[0:SEQ, :] = r.image_at[i % 2].astype(F32)
    hidden = r.xs[...]
    scaled, _ = normalize(hidden)
    normed = (scaled * r.vec[0:1, :] + r.vec[1:2, :]).astype(BF16)
    projected = mm(normed, r.wqkv[...].reshape(D, 3 * D))
    r.qkv[rows, 0:D] = (projected[:, :D] + r.vec[2:3, :]).astype(BF16)
    r.qkv[rows, D : 2 * D] = projected[:, D : 2 * D].astype(BF16)
    r.qkv[rows, 2 * D :] = (projected[:, 2 * D :] + r.vec[3:4, :]).astype(BF16)
    lane = iota((ROWS, LANES), 1)
    column = iota((2 * ROWS, ROWS), 1)
    for pair in range(HEADS // 2):
        at = pair * LANES
        queries = r.qkv[rows, at : at + LANES]
        keys = r.qkv[rows, D + at : D + at + LANES]
        values = r.qkv[rows, 2 * D + at : 2 * D + at + LANES]
        both = two_heads(queries)
        scores = mm_nt(both, keys) * HEAD_DIM**-0.5
        scores = jnp.where(column < SEQ, scores, -1e30)
        expo = jnp.exp(scores - jnp.max(scores, axis=-1, keepdims=True))
        probs = (expo / jnp.sum(expo, axis=-1, keepdims=True)).astype(BF16)
        r.probs[i * (HEADS // 2) + pair] = probs
        mixed = mm(probs, values)
        r.mix[rows, at : at + LANES] = jnp.where(
            lane < HEAD_DIM, mixed[:ROWS], mixed[ROWS:]
        ).astype(BF16)
    residual = hidden + mm(r.mix[rows, :], r.wout[...].reshape(D, D)) + r.vec[4:5, :]
    r.residual[rows, :] = residual
    scaled2, _ = normalize(residual)
    normed2 = (scaled2 * r.vec[5:6, :] + r.vec[6:7, :]).astype(BF16)
    r.wide[rows, 0:D] = normed2
    logits = jnp.where(lane < EXPERTS, mm_nt(normed2, r.router[...]), -1e30)
    expo = jnp.exp(logits - jnp.max(logits, axis=-1, keepdims=True))
    gates = expo / jnp.sum(expo, axis=-1, keepdims=True)
    r.gates[rows, :] = gates
    high, mid, low = split3(gates)
    packed = high + pltpu.roll(mid, EXPERTS, 1) + pltpu.roll(low, 2 * EXPERTS, 1)
    r.wide[rows, 2 * D :] = packed.astype(BF16)
    live = jnp.where(i < r.count[0], 1.0, 0.0)
    r.xs[0:SEQ, :] = r.other_at[i % 2].astype(F32) * live
    r.wide[rows, D : 2 * D] = r.xs[...].astype(BF16)


def routing(r):
    limit = r.count[0] * ROWS
    order = r.order[...]
    places = order.shape[1]
    for image in range(1, SLOTS):
        order = order + jnp.where(r.order[...] >= image * SEQ, ROWS - SEQ, 0)
    lane = iota((ROWS, LANES), 1)

    def find(i, carry):
        rows = image_rows(i)
        place_row, wanted = carry
        seen = order == iota((ROWS, places), 0) + i * ROWS
        place = jnp.sum(
            jnp.where(seen, iota((ROWS, places), 1).astype(F32), 0.0), axis=1, keepdims=True
        )
        r.gates[rows, :] = jnp.broadcast_to(place, (ROWS, LANES))
        same = iota((ROWS, TOK), 0) + i * ROWS == iota((ROWS, TOK), 1)
        place_row = place_row + jnp.sum(jnp.where(same, place, 0.0), axis=0, keepdims=True)
        row = iota((ROWS, LANES), 0)
        live = (row + i * ROWS < limit) & (row < SEQ)
        own = iota((ROWS, places), 0) + i * SEQ == iota((ROWS, places), 1)
        first = jnp.sum(jnp.where(own, r.routes[0:1, :], 0), axis=1, keepdims=True)
        second = jnp.sum(jnp.where(own, r.routes[1:2, :], 0), axis=1, keepdims=True)
        hit0 = jnp.where((first == lane) & live, 1.0, 0.0)
        hit1 = jnp.where((second == lane) & live, 1.0, 0.0)
        r.wide[rows, 0:LANES] = hit0.astype(BF16)
        r.wide[rows, LANES : 2 * LANES] = hit1.astype(BF16)
        return place_row, wanted + jnp.sum(hit0, axis=0, keepdims=True)

    place_row, wanted = lax.fori_loop(
        0, SLOTS, find, (jnp.zeros((1, TOK), F32), jnp.zeros((1, LANES), F32))
    )
    r.total[0:LANES, 0:TOK] = jnp.zeros((LANES, TOK), F32)

    def count(i, carry):
        rows = image_rows(i)
        earlier = jnp.where(place_row < r.gates[rows, 0:1], 1.0, 0.0).astype(BF16)
        before = mm(earlier, r.wide[:, 0 : 2 * LANES])
        hit0, hit1 = r.wide[rows, 0:LANES] > 0, r.wide[rows, LANES : 2 * LANES] > 0
        position = jnp.where(
            hit0, before[:, 0:LANES], jnp.where(hit1, before[:, LANES:] + wanted, 1e6)
        )
        position = jnp.where(position < CAP, position, -1.0)
        r.pos_col[rows, :] = position
        same = iota((ROWS, TOK), 0) + i * ROWS == iota((ROWS, TOK), 1)
        same = jnp.where(same, 1.0, 0.0).astype(BF16)
        high = position.astype(BF16)
        low = (position - high.astype(F32)).astype(BF16)
        r.total[0:LANES, 0:TOK] += mm_tn(high, same) + mm_tn(low, same)
        return carry

    lax.fori_loop(0, SLOTS, count, 0)
    r.pos_row[...] = r.total[0:8, 0:TOK]
    r.total[0:LANES, 0:TOK] = jnp.zeros((LANES, TOK), F32)


def nothing(step):
    pass


def dispatch(e, r, beside=nothing):
    wanted = r.pos_row[pl.ds(e, 1), :]
    lane = iota((SLOT_TILE, LANES), 1)

    def tile(m, carry):
        beside(m)
        rows = pl.ds(pl.multiple_of(m * SLOT_TILE, 16), SLOT_TILE)
        slot = (iota((SLOT_TILE, TOK), 0) + m * SLOT_TILE).astype(F32)
        chosen = jnp.where(slot == wanted, 1.0, 0.0).astype(BF16)
        got = mm(chosen, r.wide[...])
        r.disp[rows, :] = got[:, 0:D].astype(BF16)
        r.up[rows, :] = got[:, D : 2 * D].astype(BF16)
        mine = (lane == e) | (lane == e + EXPERTS) | (lane == e + 2 * EXPERTS)
        gate = jnp.sum(jnp.where(mine, got[:, 2 * D :], 0.0), axis=1, keepdims=True)
        r.gate_slot[rows, :] = jnp.broadcast_to(gate, (SLOT_TILE, LANES))
        r.gexp[rows, :] = (gate * got[:, D : 2 * D]).astype(BF16)
        return carry

    lax.fori_loop(0, CAPP // SLOT_TILE, tile, 0)
    r.eo[...] = jnp.zeros_like(r.eo)
    r.gdisp[...] = jnp.zeros_like(r.gdisp)


def expert_step(e, f, k, r):
    cols = pl.ds(pl.multiple_of(f * FT, FT), FT)
    block = (k, f // 2, f % 2)
    w_in = r.win[k, :, :, :, :, cols].reshape(D, FT)
    w_back = r.wback[block].reshape(FT, D)
    disp = r.disp[...]
    gexp = r.gexp[...]
    bias = r.vec[pl.ds(16 + 4 * e + f, 1), :]
    pre = mm(disp, w_in) + bias
    grad_active = mm_nt(gexp, w_back)
    active, slope = gelu_parts(pre)
    active = active.astype(BF16)
    grad_inner = (grad_active * slope).astype(BF16)
    r.eo[...] += mm(active, w_back)
    r.gdisp[...] += mm_nt(grad_inner, w_in)
    r.wback[block] = mm_tn(active, gexp).astype(BF16).reshape(2, BLOCK_BACK, D)
    grad_in = mm_tn(disp, grad_inner).astype(BF16)
    r.win[k, :, :, :, :, cols] = grad_in.reshape(2, 2, 2, BLOCK_IN, FT)
    r.gvec[pl.ds(16 + 4 * e + f, 1), :] = jnp.sum(
        grad_inner.astype(F32), axis=0, keepdims=True
    )


def combine(e, r, beside=nothing):
    r.gvec[pl.ds(12 + e, 1), :] = jnp.sum(r.gexp[...].astype(F32), axis=0, keepdims=True)
    out = r.eo[...] + r.vec[pl.ds(12 + e, 1), :]
    gate = r.gate_slot[:, 0:1]
    r.disp[...] = (gate * out).astype(BF16)
    r.gexp[...] = r.gdisp[...].astype(BF16)
    high, mid, low = split3(jnp.sum(r.up[...].astype(F32) * out, axis=1, keepdims=True))
    lane = iota((CAPP, LANES), 1)
    parts = jnp.where(
        lane == e,
        high,
        jnp.where(lane == e + EXPERTS, mid, jnp.where(lane == e + 2 * EXPERTS, low, 0.0)),
    )
    r.pairs[...] = parts.astype(BF16)

    def image(i, carry):
        beside(i)
        rows = image_rows(i)
        mine = iota((ROWS, LANES), 1) == e
        wanted = jnp.sum(jnp.where(mine, r.pos_col[rows, :], 0.0), axis=1, keepdims=True)
        chosen = jnp.where(wanted == iota((ROWS, CAPP), 1).astype(F32), 1.0, 0.0).astype(BF16)
        r.total[rows, 0:D] += mm(chosen, r.disp[...])
        r.total[rows, D : 2 * D] += mm(chosen, r.gexp[...])
        r.total[rows, 2 * D :] += mm(chosen, r.pairs[...])
        return carry

    lax.fori_loop(0, SLOTS, image, 0)


def norm_backward(i, r):
    rows = image_rows(i)
    lane = iota((ROWS, LANES), 1)
    live = jnp.where(i < r.count[0], 1.0, 0.0)
    residual = r.residual[rows, :]
    r.other_at[i % 2] = ((residual + r.total[rows, 0:D]) * live)[0:SEQ, :].astype(BF16)
    pairs = r.total[rows, 2 * D :]
    gates = r.gates[rows, :]
    grad_gates = (
        pairs + pltpu.roll(pairs, LANES - EXPERTS, 1) + pltpu.roll(pairs, LANES - 2 * EXPERTS, 1)
    )
    grad_gates = jnp.where(lane < EXPERTS, grad_gates, 0.0)
    grad_logits = (
        gates * (grad_gates - jnp.sum(grad_gates * gates, axis=-1, keepdims=True))
    ).astype(BF16)
    r.gvec[8:12, :] += mm_tn(grad_logits, r.wide[rows, 0:D])[0:EXPERTS, :]
    grad_normed2 = r.total[rows, D : 2 * D] + mm(grad_logits, r.router[...])
    scaled2, inverse2 = normalize(residual)
    r.gvec[5:6, :] += jnp.sum(grad_normed2 * scaled2, axis=0, keepdims=True)
    r.gvec[6:7, :] += jnp.sum(grad_normed2, axis=0, keepdims=True)
    grad_residual = r.wide[rows, D : 2 * D].astype(F32) + norm_back(
        grad_normed2, scaled2, inverse2, r.vec[5:6, :]
    )
    r.residual[rows, :] = grad_residual
    grad_attended = grad_residual.astype(BF16)
    r.wide[rows, D : 2 * D] = grad_attended
    r.gvec[4:5, :] += jnp.sum(grad_attended.astype(F32), axis=0, keepdims=True)
    r.wide[rows, 0:D] = mm_nt(grad_attended, r.wout[...].reshape(D, D)).astype(BF16)


def attention_backward(i, r):
    rows = image_rows(i)
    lane = iota((ROWS, LANES), 1)
    for pair in range(HEADS // 2):
        at = pair * LANES
        queries = r.qkv[rows, at : at + LANES]
        keys = r.qkv[rows, D + at : D + at + LANES]
        values = r.qkv[rows, 2 * D + at : 2 * D + at + LANES]
        from_mix = r.wide[rows, at : at + LANES]
        from_both = two_heads(from_mix)
        probs_low = r.probs[i * (HEADS // 2) + pair]
        probs = probs_low.astype(F32)
        weighted = mm_nt(from_both, values) * probs
        grad_scores = (
            weighted - probs * jnp.sum(weighted, axis=-1, keepdims=True)
        ).astype(BF16)
        grad_q = mm(grad_scores, keys)
        scale = HEAD_DIM**-0.5
        joined = jnp.where(lane < HEAD_DIM, grad_q[:ROWS], grad_q[ROWS:])
        r.qkv[rows, at : at + LANES] = (joined * scale).astype(BF16)
        grad_k = mm_tn(grad_scores, two_heads(queries))
        r.qkv[rows, D + at : D + at + LANES] = (grad_k * scale).astype(BF16)
        grad_v = mm_tn(probs_low, from_both)
        r.qkv[rows, 2 * D + at : 2 * D + at + LANES] = grad_v.astype(BF16)
    grads = r.qkv[rows, :]
    r.gvec[2:3, :] += jnp.sum(grads[:, 0:D].astype(F32), axis=0, keepdims=True)
    r.gvec[3:4, :] += jnp.sum(grads[:, 2 * D :].astype(F32), axis=0, keepdims=True)
    grad_normed1 = mm_nt(grads, r.wqkv[...].reshape(D, 3 * D))
    r.xs[0:SEQ, :] = r.image_at[i % 2].astype(F32)
    scaled1, inverse1 = normalize(r.xs[...])
    r.wide[rows, 0:D] = (scaled1 * r.vec[0:1, :] + r.vec[1:2, :]).astype(BF16)
    r.gvec[0:1, :] += jnp.sum(grad_normed1 * scaled1, axis=0, keepdims=True)
    r.gvec[1:2, :] += jnp.sum(grad_normed1, axis=0, keepdims=True)
    grad_in = r.residual[rows, :] + norm_back(grad_normed1, scaled1, inverse1, r.vec[0:1, :])
    r.grad_at[i % 2] = grad_in[0:SEQ, :].astype(BF16)


def wout_grad(r):
    r.wout[...] = mm_tn(r.mix[...], r.wide[:, D : 2 * D]).astype(BF16).reshape(r.wout.shape)


def wqkv_grad(part, r):
    width = 3 * D // QKV_PARTS
    cols = slice(part * width, (part + 1) * width)
    grad = mm_tn(r.wide[:, 0:D], r.qkv[:, cols]).astype(BF16)
    r.wqkv[:, :, :, :, :, cols] = grad.reshape(r.wqkv.shape[:5] + (width,))


def spread_router(r):
    r.router[...] = jnp.zeros_like(r.router)
    first = r.vec[8:16, :]
    r.router[0:16, :] = jnp.concatenate(
        [jnp.where(iota((8, D), 0) < EXPERTS, first, 0.0), jnp.zeros((8, D), F32)], axis=0
    ).astype(BF16)


def pattern(shape, match):
    return jnp.where(match(iota(shape, 0), iota(shape, 1)), 1.0, 0.0).astype(BF16)


def all_vectors(r):
    packs = r.small[...].reshape(GROUP * 8, LANES).astype(BF16)
    line, column = iota((GROUP * 8, D), 0), iota((GROUP * 8, D), 1)

    def row(match, line_of):
        spread = mm(packs, pattern((LANES, D), match))
        return lambda: jnp.sum(jnp.where(line == line_of, spread, 0.0), axis=0, keepdims=True)

    sixteenth = 8 * (column >> 4)
    for index, start in ((0, 0), (1, 16), (4, 64), (5, 80), (6, 96)):
        r.vec[index : index + 1, :] = row(lambda j, c: j == start + (c & 15), sixteenth)()
    for index in range(2):
        r.vec[2 + index : 3 + index, :] = row(
            lambda j, c: j == 32 + (c & 31), 8 * (16 * index + (column >> 5))
        )()
    r.vec[7:8, :] = jnp.zeros((1, D), F32)
    for e in range(EXPERTS):
        r.vec[8 + e : 9 + e, :] = row(lambda j, c: j == 4 * (c & 15) + e, sixteenth + 1)()
        r.vec[12 + e : 13 + e, :] = row(
            lambda j, c: j == 64 + (c & 63), 8 * (8 * e + (column >> 6)) + 1
        )()
    for device in range(GROUP):
        at = (device // 8, device // 4 % 2, device // 2 % 2, device % 2)
        for line_of in range(2):
            start = device % 2 * 256 + line_of * LANES
            r.vec[16 + device // 2 : 17 + device // 2, start : start + LANES] = r.small[
                at + (slice(2 + line_of, 3 + line_of), FULL)
            ]


def own_vectors(me, r):
    row, column = iota((8, D), 0), iota((8, D), 1)
    lane, line = iota((8, LANES), 1), iota((8, LANES), 0)

    def fold(values, match):
        parts = [v.astype(BF16) for v in split3(values)]
        chosen = pattern((D, LANES), match)
        return sum(mm(v, chosen) for v in parts)

    owner = jnp.where(
        row == 2, column >> 5, jnp.where(row == 3, 16 + (column >> 5), column >> 4)
    )
    top = jnp.where(owner == me, r.gvec[0:8, :], 0.0)
    by16 = fold(top, lambda c, j: (c & 15) == j)
    by32 = fold(top, lambda c, j: (c & 31) == j)
    for name, index in dict(ln1_gain=0, ln1_bias=1, b_out=4, ln2_gain=5, ln2_bias=6).items():
        getattr(r, "out_" + name)[...] = by16[index : index + 1, 0:16]
    r.out_b_qv[...] = by32[2:3, 0:32] + by32[3:4, 0:32]
    owner = jnp.where(row < 4, column >> 4, 8 * (row - 4) + (column >> 6))
    low = jnp.where(owner == me, r.gvec[8:16, :], 0.0)
    router = jnp.where((lane & 3) == line, fold(low, lambda c, j: (c & 15) == (j >> 2)), 0.0)
    r.out_w_router[...] = jnp.sum(jnp.where(line < 4, router, 0.0), axis=0, keepdims=True)[:, 0:64]
    back = jnp.where(line < 4, 0.0, fold(low, lambda c, j: (c & 63) == j))
    r.out_b_back[...] = jnp.sum(back, axis=0, keepdims=True)[:, 0:64]
    row, column = iota((16, D), 0), iota((16, D), 1)
    bias = jnp.where(2 * row + (column >> 8) == me, r.gvec[16:32, :], 0.0)
    bias = jnp.sum(bias, axis=0, keepdims=True)
    r.out_b_in[...] = bias[:, 0:256] + bias[:, 256:512]


class Place:
    def __init__(self):
        me = lax.axis_index("dev")
        self.me, self.c, self.x, self.y, self.z = me, me % 2, me // 2 % 2, me // 4 % 2, me // 8
        self.core = self.device(self.z, self.y, self.x, 1 - self.c)
        self.over_y = self.device(self.z, 1 - self.y, self.x, self.c)
        self.over_x = self.device(self.z, self.y, 1 - self.x, self.c)

    def device(self, z, y, x, c):
        return ((z * 2 + y) * 2 + x) * 2 + c

    def plane(self, k):
        return lax.rem(self.z + k + EXPERTS, EXPERTS)

    def above(self, k):
        return self.device(self.plane(k), self.y, self.x, self.c)

    def greet(self, meanwhile):
        barrier = pltpu.get_barrier_semaphore()
        friends = [self.above(k) for k in range(1, EXPERTS)]
        friends += [self.core, self.over_y, self.over_x]
        for friend in friends:
            pl.semaphore_signal(barrier, inc=1, device_id=(friend,), device_id_type=MESH)
        meanwhile()
        pl.semaphore_wait(barrier, len(friends))

    def first(self, route):
        return self.over_y if route == 0 else self.over_x

    def second(self, route):
        return self.over_x if route == 0 else self.over_y


class Copies:
    def __init__(self, sems, index):
        self.sems, self.index = sems, index

    def make(self, slot, source, target, device):
        send_sem, recv_sem = self.sems
        return pltpu.make_async_remote_copy(
            src_ref=source, dst_ref=target, send_sem=send_sem.at[self.index, slot],
            recv_sem=recv_sem.at[self.index, slot], device_id=(device,), device_id_type=MESH,
        )


class SumAll(Copies):
    def __init__(self, sems, index, values, landing, place):
        super().__init__(sems, index)
        self.values, self.landing, self.p = values, landing, place

    def stage(self, step):
        p = self.p
        targets = [
            [(k, p.above(k)) for k in range(1, EXPERTS)], [(4, p.over_y)], [(5, p.over_x)],
            [(6, p.core)],
        ][step]
        return [self.make(s, self.values, self.landing.at[s - 1], d) for s, d in targets]

    def begin(self, step):
        for copy in self.stage(step):
            copy.start()

    def end(self, step):
        for copy in self.stage(step):
            copy.wait()
        if step == 0:
            self.values[...] += self.landing[0] + self.landing[1] + self.landing[2]
        else:
            self.values[...] += self.landing[2 + step]


class Gather(Copies):
    def __init__(self, sems, index, shard, full, tail, route, k, place):
        super().__init__(sems, index)
        self.shard, self.full, self.tail, self.route, self.p = shard, full, tail, route, place
        self.k = k

    def at(self, lead, y, x, c):
        return self.full.at[(lead, y, x, c) + self.tail]

    def own(self):
        return self.shard.at[self.tail] if self.tail else self.shard

    def local(self, sem):
        p = self.p
        lead = p.z if self.k is None else 0
        return pltpu.make_async_copy(self.own(), self.at(lead, p.y, p.x, p.c), sem)

    def along_z(self, arriving):
        p = self.p
        if self.k is None:
            return [
                self.make(k, self.own(), self.at(p.plane(-k) if arriving else p.z, p.y, p.x, p.c),
                          p.above(k))
                for k in range(1, EXPERTS)
            ]
        if self.k == 0:
            return []
        return [self.make(1, self.own(), self.at(self.k, p.y, p.x, p.c), p.above(-self.k))]

    def lead(self):
        return FULL if self.k is None else self.k

    def across(self, step, arriving):
        p = self.p
        y, x = p.y, p.x
        if step == 0:
            if arriving:
                y, x = (1 - y, x) if self.route == 0 else (y, 1 - x)
            device = p.first(self.route)
        else:
            if arriving:
                y, x = 1 - y, 1 - x
            y, x = (FULL, x) if self.route == 0 else (y, FULL)
            device = p.second(self.route)
        block = self.at(self.lead(), y, x, p.c)
        return self.make(4 + step, block, block, device)

    def to_core(self, step, arriving):
        p = self.p
        y, x = p.y, p.x
        if step == 1:
            y, x = (1 - y, x) if self.route == 0 else (y, 1 - x)
        elif step == 2:
            y, x = (FULL, 1 - x) if self.route == 0 else (1 - y, FULL)
        block = self.at(self.lead(), y, x, 1 - p.c if arriving else p.c)
        return self.make(6 + step, block, block, p.core)

    def start_z(self):
        for copy in self.along_z(False):
            copy.start()

    def stage(self, step):
        if step == 0:
            for copy in self.along_z(True):
                copy.wait_recv()
        else:
            self.across(step - 1, True).wait_recv()
        if step < 2:
            self.across(step, False).start()
        self.to_core(step, False).start()

    def finish(self):
        for step in range(3):
            self.to_core(step, True).wait_recv()
        for copy in self.along_z(False):
            copy.wait_send()
        for step in range(2):
            self.across(step, False).wait_send()
        for step in range(3):
            self.to_core(step, False).wait_send()


class Scatter(Copies):
    def __init__(self, sems, index, full, landing, out, tail, route, k, place):
        super().__init__(sems, index)
        self.full, self.out, self.tail, self.route, self.p, self.k = (
            full, out, tail, route, place, k,
        )
        self.from_core, self.from_first, self.from_second, self.from_z = landing

    def lead(self):
        return FULL if self.k is None else self.k

    def landed(self, ref, spare):
        if self.k is None:
            return (FULL,) * (1 + spare) + self.tail
        return (self.k % ref.shape[0],) + (FULL,) * spare + self.tail

    def to_core(self):
        p = self.p
        return self.make(0, self.full.at[(self.lead(), FULL, FULL, 1 - p.c) + self.tail],
                         self.from_core.at[self.landed(self.from_core, 2)], p.core)

    def to_first(self):
        p = self.p
        y, x = (FULL, 1 - p.x) if self.route == 0 else (1 - p.y, FULL)
        return self.make(1, self.full.at[(self.lead(), y, x, p.c) + self.tail],
                         self.from_first.at[self.landed(self.from_first, 1)],
                         p.second(self.route))

    def to_second(self):
        p = self.p
        y, x = (1 - p.y, p.x) if self.route == 0 else (p.y, 1 - p.x)
        return self.make(2, self.full.at[(self.lead(), y, x, p.c) + self.tail],
                         self.from_second.at[self.landed(self.from_second, 0)],
                         p.first(self.route))

    def along_z(self):
        p = self.p
        steps = range(1, EXPERTS) if self.k is None else ([self.k] if self.k else [])
        return [
            self.make(2 + k, self.full.at[(p.plane(k) if self.k is None else k, p.y, p.x, p.c) + self.tail],
                      self.from_z.at[(k - 1,) + self.tail], p.above(k))
            for k in steps
        ]

    def add(self, mine, landed):
        def layer(k, carry):
            for at, source in zip(mine(k), landed(k)):
                self.full[at + self.tail] = self.full[at + self.tail] + source
            return carry

        if self.k is None:
            lax.fori_loop(0, EXPERTS, layer, 0)
        else:
            layer(self.k, 0)

    def slot(self, ref, k):
        return k if self.k is None else k % ref.shape[0]

    def stage(self, step):
        p, tail = self.p, self.tail
        if step == 0:
            self.to_core().start()
        elif step == 1:
            self.to_core().wait_recv()
            spots = [(y, x) for y in range(2) for x in range(2)]
            ref = self.from_core
            self.add(lambda k: [(k, y, x, p.c) for y, x in spots],
                     lambda k: [ref[(self.slot(ref, k), y, x) + tail] for y, x in spots])
            self.to_first().start()
        elif step == 2:
            self.to_first().wait_recv()
            ref = self.from_first
            self.add(lambda k: [(k, o, p.x, p.c) if self.route == 0 else (k, p.y, o, p.c) for o in range(2)],
                     lambda k: [ref[(self.slot(ref, k), o) + tail] for o in range(2)])
            self.to_second().start()
        else:
            self.to_second().wait_recv()
            ref = self.from_second
            self.add(lambda k: [(k, p.y, p.x, p.c)],
                     lambda k: [ref[(self.slot(ref, k),) + tail]])
            for copy in self.along_z():
                copy.start()

    def collect(self):
        p, tail = self.p, self.tail
        total = self.full[((p.z if self.k is None else 0), p.y, p.x, p.c) + tail].astype(F32)
        for k in range(EXPERTS - 1):
            total = total + self.from_z[(k,) + tail].astype(F32)
        rows, columns = total.shape
        height, width = self.full.shape[-2:]
        first_row, first_column = tail[0].start or 0, tail[1].start or 0
        step = width // LANES
        for j in range(columns // LANES):
            line = first_row * step + first_column // LANES + j
            self.out[pl.ds(line, rows, stride=step), :] = total[:, j * LANES : (j + 1) * LANES]

    def drain(self):
        self.to_core().wait_send()
        self.to_first().wait_send()
        self.to_second().wait_send()
        for copy in self.along_z():
            copy.wait_send()


class Refs:
    def __init__(self, names, refs):
        for name, ref in zip(names, refs, strict=True):
            setattr(self, name, ref)


SCRATCH = dict(
    image_at=((2, SEQ, D), BF16),
    other_at=((2, SEQ, D), BF16),
    grad_at=((2, SEQ, D), BF16),
    xs=((ROWS, D), F32),
    router=((LANES, D), BF16),
    qkv=((TOK, 3 * D), BF16),
    probs=((SLOTS * HEADS // 2, 2 * ROWS, ROWS), BF16),
    mix=((TOK, D), BF16),
    residual=((TOK, D), F32),
    wide=((TOK, WIDE), BF16),
    gates=((TOK, LANES), F32),
    pos_col=((TOK, LANES), F32),
    pos_row=((8, TOK), F32),
    disp=((CAPP, D), BF16),
    up=((CAPP, D), BF16),
    gexp=((CAPP, D), BF16),
    gate_slot=((CAPP, LANES), F32),
    pairs=((CAPP, LANES), BF16),
    eo=((CAPP, D), F32),
    gdisp=((CAPP, D), F32),
    total=((TOK, WIDE), F32),
    wqkv=((EXPERTS, 2, 2, 2, 16, 3 * D), BF16),
    wout=((EXPERTS, 2, 2, 2, 16, D), BF16),
    win=((EXPERTS, 2, 2, 2, BLOCK_IN, HID), BF16),
    wback=((EXPERTS, 2, 2, 2, BLOCK_BACK, D), BF16),
)
SHARDS = dict(wqkv=(16, 3 * D), wout=(16, D), win=(BLOCK_IN, HID), wback=(BLOCK_BACK, D))


def columns_of(width, h, parts=2):
    return (FULL, slice(h * width // parts, (h + 1) * width // parts))


def rows_of(height, h):
    return (slice(h * height // 2, (h + 1) * height // 2), FULL)


SMALL = dict(
    ln1_gain=16, ln1_bias=16, b_qv=32, b_out=16, ln2_gain=16, ln2_bias=16, w_router=64, b_in=256,
    b_back=64,
)
FLAT_PIECES = [("wqkv", columns_of(3 * D, h, QKV_PARTS), h % 2) for h in range(QKV_PARTS)]
FLAT_PIECES += [("wout", columns_of(D, h), h) for h in range(2)]
FLAT_PIECES += [("small", (), 0)]
EXPERT_PIECES = [("win", rows_of(BLOCK_IN, h), h) for h in range(2)]
EXPERT_PIECES += [("wback", rows_of(BLOCK_BACK, h), h) for h in range(2)]
LANDING = {}
for name in ("wqkv", "wout"):
    for part, lead in dict(core=(4, 2, 2), first=(4, 2), second=(4,), z=(3,)).items():
        LANDING[name, part] = (lead + SHARDS[name], BF16)
for name in ("win", "wback"):
    for part, lead in dict(core=(2, 2, 2), first=(4, 2), second=(4,), z=(3,)).items():
        LANDING[name, part] = (lead + SHARDS[name], BF16)
INPUTS = ["count", "images", "cotangent", "routes", "order"]


def whole_kernel(*refs):
    names = INPUTS + ["shard_small"] + ["shard_" + n for n in SHARDS]
    names += ["blocks", "gimages"] + ["out_" + n for n in SHARDS] + ["out_" + n for n in SMALL]
    names += list(SCRATCH) + ["vec", "gvec", "small", "land_gvec"]
    names += ["land_" + "_".join(key) for key in LANDING]
    names += ["local_sem", "vec_send", "vec_recv", "get_send", "get_recv", "put_send", "put_recv"]
    names += ["free_sem", "in_sem", "out_sem"]
    r = Refs(names, refs)
    p = Place()

    def landing(name):
        return [getattr(r, f"land_{name}_{part}") for part in ("core", "first", "second", "z")]

    get_sems, put_sems = (r.get_send, r.get_recv), (r.put_send, r.put_recv)
    flat_get, flat_put = [], []
    for index, (name, tail, route) in enumerate(FLAT_PIECES):
        flat_get.append(
            Gather(get_sems, index, getattr(r, "shard_" + name), getattr(r, name), tail, route, None, p)
        )
        if name != "small":
            flat_put.append(
                Scatter(put_sems, index, getattr(r, name), landing(name), getattr(r, "out_" + name),
                        tail, route, None, p)
            )
    get, put = [], []
    for k in range(EXPERTS):
        get.append([])
        put.append([])
        for index, (name, tail, route) in enumerate(EXPERT_PIECES):
            index += len(FLAT_PIECES) + k * len(EXPERT_PIECES)
            get[k].append(
                Gather(get_sems, index, getattr(r, "shard_" + name), getattr(r, name), tail, route, k, p)
            )
            put[k].append(
                Scatter(put_sems, index, getattr(r, name), landing(name), getattr(r, "out_" + name),
                        tail, route, k, p)
            )

    def part(pieces, which):
        return pieces if which is None else pieces[2 * which : 2 * which + 2]

    def gather_stage(k, step, which=None):
        for piece in part(get[k], which):
            piece.start_z() if step < 0 else piece.stage(step)

    def scatter_stage(k, step, which=None):
        if step == 0 and k >= 2 and which != 1:
            pl.semaphore_wait(r.free_sem, 1)
        for piece in part(put[k], which):
            piece.stage(step)
        if step == 1 and k < 2 and which != 0:
            pl.semaphore_signal(r.free_sem, inc=1, device_id=(p.core,), device_id_type=MESH)

    def wout_stage(step):
        for piece in flat_put[QKV_PARTS:]:
            piece.stage(step)

    events = {
        ("start",): [("get", 0, 0, 1), ("get", 0, 1, 1)],
        ("flat", 0): [("get", 3, -1, 0)],
        ("flat", 1): [("get", 3, 0, 0), ("get", 1, -1, 0)],
        ("flat", 2): [("get", 1, -1, 1), ("get", 0, 0, 0), ("get", 3, 1, 0), ("get", 0, 2, 1), ("get", 2, -1, 0)],
        ("forward", 0): [("get", 0, 1, 0)],
        ("forward", 2): [("get", 1, 0, 0)],
        ("forward", 4): [("get", 1, 0, 1)],
        ("dispatch", 0, 0): [("get", 0, 2, 0)],
        ("dispatch", 0, 2): [("get", 2, -1, 1)],
        ("dispatch", 0, 3): [("get", 1, 1, 0)],
        ("dispatch", 0, 4): [("get", 3, 2, 0)],
        ("expert", 0, 3): [("get", 1, 1, 1)],
        ("expert", 0, 7): [("get", 1, 2, 0)],
        ("combine", 0, 2): [("get", 2, 0, 0), ("get", 1, 2, 1), ("get", 3, -1, 1)],
        ("combine", 0, 3): [("get", 2, 0, 1)],
        ("dispatch", 1, 0): [("put", 0, 0, 0)],
        ("dispatch", 1, 4): [("get", 2, 1, 0)],
        ("expert", 1, 4): [("put", 0, 0, 1)],
        ("expert", 1, 5): [("get", 3, 0, 1)],
        ("expert", 1, 6): [("get", 2, 2, 0)],
        ("expert", 1, 7): [("get", 2, 1, 1)],
        ("combine", 1, 1): [("put", 1, 0, 0)],
        ("combine", 1, 3): [("get", 3, 1, 1)],
        ("dispatch", 2, 1): [("get", 2, 2, 1)],
        ("dispatch", 2, 2): [("put", 0, 1, 0)],
        ("expert", 2, 0): [("put", 1, 0, 1), ("put", 1, 1, 0)],
        ("expert", 2, 7): [("put", 0, 1, 1), ("get", 3, 2, 1)],
        ("combine", 2, 3): [("put", 2, 0, 0)],
        ("dispatch", 3, 0): [("put", 0, 2, 0)],
        ("dispatch", 3, 1): [("put", 1, 2, 0)],
        ("dispatch", 3, 4): [("put", 2, 0, 1)],
        ("expert", 3, 1): [("put", 2, 1, 0)],
        ("expert", 3, 4): [("put", 1, 3, 0)],
        ("expert", 3, 5): [("put", 2, 1, 1)],
        ("expert", 3, 7): [("put", 0, 3, 0)],
        ("combine", 3, 0): [("put", 2, 2, 0)],
        ("combine", 3, 2): [("put", 1, 1, 1)],
        ("combine", 3, 4): [("put", 3, 0, 0)],
        ("norms", 1): [("put", 2, 3, 0)],
        ("norms", 2): [("put", 2, 2, 1)],
        ("norms", 3): [("put", 3, 1, 0)],
        ("norms", 4): [("put", 0, 2, 1)],
        ("backward", 1): [("put", 2, 3, 1), ("out", 1)],
        ("backward", 2): [("put", 3, 0, 1), ("put", 1, 2, 1)],
        ("backward", 3): [("put", 3, 2, 0), ("out", 2)],
        ("tail", 0): [("put", 3, 1, 1), ("put", 1, 3, 1), ("out", 3)],
        ("tail", 3): [("put", 3, 3, 0)],
        ("tail", 4): [("put", 3, 2, 1), ("put", 0, 3, 1), ("put", 3, 3, 1)],
    }

    def beside(*key):
        def at(step):
            for (*found, when), todo in events.items():
                if tuple(found) == key:
                    pl.when(step == when)(functools.partial(act, todo))

        return at

    def act(todo):
        for kind, *what in todo:
            dict(get=gather_stage, put=scatter_stage, out=wout_stage)[kind](*what)

    def fetch(i, both):
        copies = [pltpu.make_async_copy(r.images.at[i], r.image_at.at[i % 2], r.in_sem.at[0, i % 2])]
        if both:
            copies.append(
                pltpu.make_async_copy(r.cotangent.at[i], r.other_at.at[i % 2], r.in_sem.at[1, i % 2])
            )
        return copies

    def emit_block(i):
        return [pltpu.make_async_copy(r.other_at.at[i % 2], r.blocks.at[i], r.out_sem.at[0, i % 2])]

    def emit_grad(i):
        return [pltpu.make_async_copy(r.grad_at.at[i % 2], r.gimages.at[i], r.out_sem.at[1, i % 2])]

    def start(copies):
        for copy in copies:
            copy.start()

    def wait(copies):
        for copy in copies:
            copy.wait()

    start(fetch(0, True))
    local = []
    for index, piece in enumerate(flat_get + get[0]):
        copy = piece.local(r.local_sem.at[index])
        copy.start()
        local.append(copy)

    def clear():
        r.xs[...] = jnp.zeros_like(r.xs)
        r.gvec[...] = jnp.zeros_like(r.gvec)
        r.total[...] = jnp.zeros_like(r.total)

    p.greet(clear)
    for piece in flat_get:
        piece.start_z()
    for copy in local:
        copy.wait()
    act(events.get(("start",), ()))
    for step in range(3):
        for piece in flat_get:
            piece.stage(step)
        if step == 0:
            routing(r)
        act(events.get(("flat", step), ()))
    for piece in flat_get:
        piece.finish()
    act(events.get(("flat", 3), ()))
    all_vectors(r)
    spread_router(r)

    def forward(i, carry):
        @pl.when(i + 1 < SLOTS)
        def _():
            start(fetch(i + 1, True))

        wait(fetch(i, True))
        attention_forward(i, r)
        beside("forward")(i)
        return carry

    lax.fori_loop(0, SLOTS, forward, 0)
    for k in range(EXPERTS):
        e = p.plane(k)
        dispatch(e, r, beside("dispatch", k))
        for piece in get[k]:
            piece.finish()

        def step(f, carry):
            beside("expert", k)(2 * f)
            beside("expert", k)(2 * f + 1)
            expert_step(e, f, k, r)
            return carry

        lax.fori_loop(0, HID // FT, step, 0)
        combine(e, r, beside("combine", k))
    start(fetch(0, False))

    def norms(i, carry):
        @pl.when(i >= 2)
        def _():
            wait(emit_block(i - 2))

        norm_backward(i, r)
        start(emit_block(i))
        beside("norms")(i)
        return carry

    lax.fori_loop(0, SLOTS, norms, 0)
    wout_grad(r)
    wqkv_put, wout_put = flat_put[:QKV_PARTS], flat_put[QKV_PARTS:]
    for piece in wout_put:
        piece.stage(0)

    def backward(i, carry):
        @pl.when(i + 1 < SLOTS)
        def _():
            start(fetch(i + 1, False))

        wait(fetch(i, False))

        @pl.when(i >= 2)
        def _():
            wait(emit_grad(i - 2))

        attention_backward(i, r)
        start(emit_grad(i))
        beside("backward")(i)
        return carry

    lax.fori_loop(0, SLOTS, backward, 0)
    sums = SumAll((r.vec_send, r.vec_recv), 0, r.gvec, r.land_gvec, p)
    sums.begin(0)
    for part_of in range(QKV_PARTS):
        wqkv_grad(part_of, r)
        wqkv_put[part_of].stage(0)
        if part_of % 2:
            act(events.get(("tail", part_of // 2), ()))
    for step in range(1, 4):
        sums.end(step - 1)
        sums.begin(step)
        for piece in wqkv_put:
            piece.stage(step)
        act(events.get(("tail", step + 1), ()))
    for k in range(1, EXPERTS):
        for piece in put[k]:
            for copy in piece.along_z():
                copy.wait_recv()
    for piece in put[0]:
        piece.collect()
    for piece in wout_put:
        for copy in piece.along_z():
            copy.wait_recv()
        piece.collect()
    sums.end(3)
    own_vectors(p.me, r)
    for piece in wqkv_put:
        for copy in piece.along_z():
            copy.wait_recv()
        piece.collect()
    for pieces in put + [flat_put]:
        for piece in pieces:
            piece.drain()
    for i in range(SLOTS - 2, SLOTS):
        wait(emit_block(i))
        wait(emit_grad(i))


def alone_kernel(*refs):
    names = INPUTS + ["pack"] + ["full_" + n for n in SHARDS]
    names += ["blocks", "gimages", "gvec"] + ["out_" + n for n in SHARDS]
    names += list(SCRATCH) + ["vec", "sem"]
    r = Refs(names, refs)

    def move(source, target):
        copy = pltpu.make_async_copy(source, target, r.sem)
        copy.start()
        copy.wait()

    for name in SHARDS:
        move(getattr(r, "full_" + name), getattr(r, name))
    r.vec[...] = r.pack[...]
    r.xs[...] = jnp.zeros_like(r.xs)
    r.gvec[...] = jnp.zeros_like(r.gvec)
    r.total[...] = jnp.zeros_like(r.total)
    spread_router(r)
    routing(r)

    def forward(i, carry):
        move(r.images.at[i], r.image_at.at[i % 2])
        move(r.cotangent.at[i], r.other_at.at[i % 2])
        attention_forward(i, r)
        return carry

    def expert(e, carry):
        dispatch(e, r)
        lax.fori_loop(0, HID // FT, lambda f, c: (expert_step(e, f, e, r), c)[1], 0)
        combine(e, r)
        return carry

    def norms(i, carry):
        norm_backward(i, r)
        move(r.other_at.at[i % 2], r.blocks.at[i])
        return carry

    def backward(i, carry):
        move(r.images.at[i], r.image_at.at[i % 2])
        attention_backward(i, r)
        move(r.grad_at.at[i % 2], r.gimages.at[i])
        return carry

    lax.fori_loop(0, SLOTS, forward, 0)
    lax.fori_loop(0, EXPERTS, expert, 0)
    lax.fori_loop(0, SLOTS, norms, 0)
    wout_grad(r)
    lax.fori_loop(0, SLOTS, backward, 0)
    for part in range(QKV_PARTS):
        wqkv_grad(part, r)
    for name in SHARDS:
        move(getattr(r, name), getattr(r, "out_" + name))


def alone(inputs, pack, full):
    vmem = pl.BlockSpec(memory_space=pltpu.VMEM)
    hbm = pl.BlockSpec(memory_space=pltpu.HBM)
    smem = pl.BlockSpec(memory_space=pltpu.SMEM)
    shapes = [((SLOTS, SEQ, D), BF16), ((SLOTS, SEQ, D), BF16), ((32, D), F32)]
    shapes += [SCRATCH[name] for name in SHARDS]
    return pl.pallas_call(
        alone_kernel,
        out_shape=[jax.ShapeDtypeStruct(*s) for s in shapes],
        in_specs=[smem] + [hbm] * 2 + [vmem] * 3 + [hbm] * 4,
        out_specs=[hbm] * 2 + [vmem] + [hbm] * 4,
        scratch_shapes=[pltpu.VMEM(*s) for s in SCRATCH.values()]
        + [pltpu.VMEM((32, D), F32), pltpu.SemaphoreType.DMA],
        compiler_params=pltpu.CompilerParams(vmem_limit_bytes=VMEM_LIMIT),
    )(*inputs, pack, *full)


def whole(inputs, pack, shards):
    vmem = pl.BlockSpec(memory_space=pltpu.VMEM)
    hbm = pl.BlockSpec(memory_space=pltpu.HBM)
    smem = pl.BlockSpec(memory_space=pltpu.SMEM)
    shapes = [((SLOTS, SEQ, D), BF16), ((SLOTS, SEQ, D), BF16)]
    shapes += [((rows * columns // LANES, LANES), F32) for rows, columns in SHARDS.values()]
    shapes += [((1, size), F32) for size in SMALL.values()]
    count = len(FLAT_PIECES) + EXPERTS * len(EXPERT_PIECES)
    dma = pltpu.SemaphoreType.DMA
    return pl.pallas_call(
        whole_kernel,
        out_shape=[jax.ShapeDtypeStruct(*s) for s in shapes],
        in_specs=[smem] + [hbm] * 2 + [vmem] * 2 + [hbm] * 5,
        out_specs=[hbm] * 2 + [vmem] * (len(shapes) - 2),
        scratch_shapes=[pltpu.VMEM(*s) for s in SCRATCH.values()]
        + [pltpu.VMEM((32, D), F32)] * 2
        + [pltpu.VMEM((EXPERTS, 2, 2, 2, 8, LANES), F32), pltpu.VMEM((6, 32, D), F32)]
        + [pltpu.VMEM(*s) for s in LANDING.values()]
        + [dma((len(FLAT_PIECES) + len(EXPERT_PIECES),)), dma((1, 7)), dma((1, 7))]
        + [dma((count, 9)), dma((count, 9)), dma((count, 6)), dma((count, 6))]
        + [pltpu.SemaphoreType.REGULAR, dma((2, 2)), dma((2, 2))],
        compiler_params=pltpu.CompilerParams(
            collective_id=0, has_side_effects=True, vmem_limit_bytes=VMEM_LIMIT
        ),
        cost_estimate=pl.CostEstimate(
            flops=40 * 10**9, bytes_accessed=50 * 10**6, transcendentals=10**7
        ),
    )(*inputs, pack, *shards)


def arrange_kernel(*refs):
    lines = refs[-1]
    for flat, shard in zip(refs[: len(SHARDS)], refs[len(SHARDS) : -1]):
        rows, columns = shard.shape
        step = columns // LANES
        lines[0 : rows * step, :] = flat[...].astype(F32)
        for j in range(step):
            shard[:, j * LANES : (j + 1) * LANES] = lines[
                pl.ds(j, rows, stride=step), :
            ].astype(BF16)


def arrange(flat):
    vmem = pl.BlockSpec(memory_space=pltpu.VMEM)
    longest = max(v.shape[0] for v in flat)
    return pl.pallas_call(
        arrange_kernel,
        out_shape=[jax.ShapeDtypeStruct(s, BF16) for s in SHARDS.values()],
        in_specs=[vmem] * len(flat),
        out_specs=[vmem] * len(flat),
        scratch_shapes=[pltpu.VMEM((longest, LANES), F32)],
    )(*flat)


def settle_kernel(*refs):
    count = (len(refs) - 1) // 3
    sources, targets, held, sems = refs[:count], refs[count : 2 * count], refs[2 * count : -1], refs[-1]
    coming = [pltpu.make_async_copy(sources[k], held[k], sems.at[0, k]) for k in range(count)]
    going = [pltpu.make_async_copy(held[k], targets[k], sems.at[1, k]) for k in range(count)]
    for copy in coming:
        copy.start()
    for arrived, leaving in zip(coming, going):
        arrived.wait()
        leaving.start()
    for copy in going:
        copy.wait()


def settle(arrays):
    hbm = pl.BlockSpec(memory_space=pltpu.HBM)
    return pl.pallas_call(
        settle_kernel,
        out_shape=[jax.ShapeDtypeStruct(a.shape, a.dtype) for a in arrays],
        in_specs=[hbm] * len(arrays),
        out_specs=[hbm] * len(arrays),
        scratch_shapes=[pltpu.VMEM(a.shape, a.dtype) for a in arrays]
        + [pltpu.SemaphoreType.DMA((2, len(arrays)))],
        compiler_params=pltpu.CompilerParams(vmem_limit_bytes=VMEM_LIMIT),
    )(*arrays)


def per_device(
    images, cotangent, routes, priority, image_count,
    ln1_gain, ln1_bias, w_qkv, b_qv, w_out, b_out, ln2_gain, ln2_bias,
    w_router, w_in, b_in, w_back, b_back,
):
    inputs = (image_count, images, cotangent, routes.T, priority)
    if lax.axis_size("dev") != GROUP:
        return with_collectives(
            inputs, ln1_gain, ln1_bias, w_qkv, b_qv, w_out, b_out, ln2_gain, ln2_bias,
            w_router, w_in, b_in, w_back, b_back,
        )
    small = [ln1_gain, ln1_bias, b_qv, b_out, ln2_gain, ln2_bias, None, w_router, b_back, b_in]
    pack, at = 0.0, 0
    for v in small:
        size = 16 if v is None else v.shape[0]
        if v is not None:
            pack = pack + jnp.pad(v.astype(F32), (at, 8 * LANES - at - size))
        at += size
    shards = arrange([v.reshape(-1, LANES) for v in (w_qkv, w_out, w_in, w_back)])
    blocks, gimages, *grads = settle(whole(inputs, pack.reshape(8, LANES), shards))
    grads = dict(zip(["w_qkv", "w_out", "w_in", "w_back"] + list(SMALL), grads))
    order = ["ln1_gain", "ln1_bias", "w_qkv", "b_qv", "w_out", "b_out", "ln2_gain", "ln2_bias"]
    order += ["w_router", "w_in", "b_in", "w_back", "b_back"]
    return (blocks, gimages) + tuple(grads[name].reshape(-1) for name in order)


def with_collectives(
    inputs, ln1_gain, ln1_bias, w_qkv, b_qv, w_out, b_out, ln2_gain, ln2_bias,
    w_router, w_in, b_in, w_back, b_back,
):
    gather = lambda v: lax.all_gather(v, "dev", axis=0, tiled=True)
    scatter = lambda v: lax.psum_scatter(
        v.astype(F32).reshape(-1), "dev", scatter_dimension=0, tiled=True
    )
    row = lambda v: gather(v).astype(F32).reshape(-1, D)
    zero = jnp.zeros((1, D), F32)
    pack = jnp.concatenate(
        [row(ln1_gain), row(ln1_bias), row(b_qv), row(b_out), row(ln2_gain), row(ln2_bias), zero,
         gather(w_router).astype(F32).reshape(D, EXPERTS).T, row(b_back), row(b_in)]
    )
    full = [
        gather(v).reshape(SCRATCH[name][0]) for v, name in zip((w_qkv, w_out, w_in, w_back), SHARDS)
    ]
    blocks, gimages, gvec, gwqkv, gwout, gwin, gwback = alone(inputs, pack, full)
    return (
        blocks, gimages, scatter(gvec[0]), scatter(gvec[1]), scatter(gwqkv), scatter(gvec[2:4]),
        scatter(gwout), scatter(gvec[4]), scatter(gvec[5]), scatter(gvec[6]),
        scatter(gvec[8:12].T), scatter(gwin), scatter(gvec[16:32]), scatter(gwback),
        scatter(gvec[12:16]),
    )


def solution(mesh):
    split = P("dev")
    return jax.shard_map(
        per_device, mesh=mesh, in_specs=(split,) * 18, out_specs=(split,) * 15, check_vma=False
    )
```
